32 devices in a mesh: dp: 4 (over x, core), seq: 2 (over y), mp: 4 (over z).
Axes of the slice: x: 2, y: 2, z: 4, core: 2. Of those that a mesh axis runs over, the one named last changes fastest.
Arguments:
- tokens: bfloat16 [4096, 2304], P(('dp', 'seq')), may hold values from -6 to 6
- gain_attn: bfloat16 [2304], P(('dp', 'seq')), may hold values from 0.5 to 1.5
- w_query: bfloat16 [2304, 2048], P(('dp', 'seq'), 'mp'), may hold values from -0.125 to 0.125
- w_key: bfloat16 [2304, 1024], P(('dp', 'seq'), 'mp'), may hold values from -0.125 to 0.125
- w_value: bfloat16 [2304, 1024], P(('dp', 'seq'), 'mp'), may hold values from -0.125 to 0.125
- w_out: bfloat16 [2048, 2304], P('mp', ('dp', 'seq')), may hold values from -1 to 1
- gain_ffn: bfloat16 [2304], P(('dp', 'seq')), may hold values from 0.5 to 1.5
- w_gate: bfloat16 [2304, 9216], P(('dp', 'seq'), 'mp'), may hold values from -0.125 to 0.125
- w_up: bfloat16 [2304, 9216], P(('dp', 'seq'), 'mp'), may hold values from -0.125 to 0.125
- w_down: bfloat16 [9216, 2304], P('mp', ('dp', 'seq')), may hold values from -0.125 to 0.125
- width_pick: int32 [7], replicated, may hold values from 0 to 2
- segments: int32 [4, 1024], P('dp'), may hold values from 0 to 65, as said below
- cotangent: bfloat16 [4096, 2304], P(('dp', 'seq')), may hold values from -6 to 6
Outputs:
- mixed: float32 [4096, 2304], P(('dp', 'seq'))
- grad_tokens: float32 [4096, 2304], P(('dp', 'seq'))
- grad_query: float32 [2304, 2048], P(('dp', 'seq'), 'mp')
- grad_key: float32 [2304, 1024], P(('dp', 'seq'), 'mp')
- grad_value: float32 [2304, 1024], P(('dp', 'seq'), 'mp')
- grad_out: float32 [2048, 2304], P('mp', ('dp', 'seq'))
- grad_gate: float32 [2304, 9216], P(('dp', 'seq'), 'mp')
- grad_up: float32 [2304, 9216], P(('dp', 'seq'), 'mp')
- grad_down: float32 [9216, 2304], P('mp', ('dp', 'seq'))
- grad_gain_attn: float32 [2304], P(('dp', 'seq'))
- grad_gain_ffn: float32 [2304], P(('dp', 'seq'))
- attn_scales: float32 [2, 2048], P(None, 'mp')
- kv_scales: float32 [2, 1024], P(None, 'mp')
- ffn_scales: float32 [3, 9216], P(None, 'mp')
The draws below stay inside these ranges and needn't reach their ends.
Inputs may be any that keep to these rules, and one draw needn't show every extreme that they name: `segments`: in each row the numbers start at 0 and rise by one at each new document; one document of each row covers exactly 513 consecutive slots, at the start or at the end of the row, and the other 511 slots hold exactly 65 short documents. `width_pick`: entry i picks the level of the i-th weight in the order query, key, value, out, gate, up, down.
All inputs are finite; a program needn't handle non-finite values.
Results may differ from the reference program's by a relative error of at most 0.013.
Values may be sent and summed in bfloat16 or wider, within the bound.
A program may use at most 256 MiB of HBM per device.

```python
import jax
import jax.numpy as jnp
from jax import lax

D = 2304
HQ = 8
HK = 4
HD = 256
FF = 9216
TOK_DEV = 512
GROUP = 1024
TOKENS = 4096
N_DP = 4


def draw_segments(key, part):
    key = jax.random.fold_in(key, 11)
    key_side, key_cut = jax.random.split(key, 2)
    short_count = TOK_DEV // 8
    long_len = GROUP - TOK_DEV + 1
    side = jax.random.randint(key_side, (N_DP, 1), 0, 2)
    position = jnp.arange(GROUP, dtype=jnp.int32)[None, :]
    long_start = jnp.where(side == 1, 0, TOK_DEV - 1)
    short_start = jnp.where(side == 1, long_len, 0)
    row_keys = jax.random.split(key_cut, N_DP)
    offsets = jax.vmap(lambda k: jax.random.permutation(k, TOK_DEV - 2)[:short_count])(row_keys).astype(jnp.int32) + 1
    cut_pos = short_start + offsets
    cuts = jnp.any(position[:, :, None] == cut_pos[:, None, :], axis=-1)
    starts = (position == 0) | (position == long_start) | (position == long_start + long_len) | cuts
    return (jnp.cumsum(starts.astype(jnp.int32), axis=1) - 1).astype(jnp.int32)


def with_ends(array, rng, low, top_value):
    index_at = [jax.random.randint(jax.random.fold_in(rng, axis), (), 0, length) for axis, length in enumerate(array.shape)]
    widest = array.shape.index(max(array.shape))
    neighbour = index_at[:widest] + [(index_at[widest] + 1) % array.shape[widest]] + index_at[widest + 1:]
    return array.at[tuple(index_at)].set(low).at[tuple(neighbour)].set(top_value)


def block_scale(own_key, extent, cuts, low, top_value):
    factor_of = 1.0
    for dim, shards_of in cuts:
        steps = jax.random.uniform(jax.random.fold_in(jax.random.fold_in(own_key, 6), dim), (shards_of,), jnp.float32, low / len(cuts), top_value / len(cuts))
        factor_of = factor_of * jnp.repeat(jnp.exp(steps), extent[dim] // shards_of).reshape((-1,) + (1,) * (len(extent) - 1 - dim))
    return factor_of


def normal_values(own_key, extent, scale, reach, cuts=(), kind=jnp.bfloat16):
    factor_of = block_scale(own_key, extent, cuts, -0.22, 0.18) if cuts else 1.0
    values = jax.random.normal(own_key, extent, jnp.float32) * scale * factor_of
    return jnp.minimum(jnp.maximum(values, -reach), reach).astype(kind)


def setup_inputs(seed: int = 0) -> dict:
    keys = jax.random.split(jax.random.key(seed), 14)
    tokens = normal_values(keys[0], (TOKENS, D), 1.0, 6.0, ((0, 8),))
    gain_attn = jnp.clip(1.0 + 0.1 * jax.random.normal(keys[1], (D,), jnp.float32), 0.5, 1.5).astype(jnp.bfloat16)
    w_query = normal_values(keys[2], (D, HQ * HD), D ** -0.5, 0.125, ((0, 8), (1, 4)))
    w_key = normal_values(keys[3], (D, HK * HD), D ** -0.5, 0.125, ((0, 8), (1, 4)))
    w_value = normal_values(keys[4], (D, HK * HD), D ** -0.5, 0.125, ((0, 8), (1, 4)))
    w_out = normal_values(keys[5], (HQ * HD, D), (HQ * HD // 64) ** -0.5, 1.0, ((0, 4), (1, 8)))
    gain_ffn = jnp.clip(1.0 + 0.1 * jax.random.normal(keys[6], (D,), jnp.float32), 0.5, 1.5).astype(jnp.bfloat16)
    w_gate = normal_values(keys[7], (D, FF), D ** -0.5, 0.125, ((0, 8), (1, 4)))
    w_up = normal_values(keys[8], (D, FF), D ** -0.5, 0.125, ((0, 8), (1, 4)))
    w_down = normal_values(keys[9], (FF, D), (FF // 4) ** -0.5, 0.125, ((0, 4), (1, 8)))
    width_pick = with_ends(jax.random.randint(keys[10], (7,), 0, 3), jax.random.fold_in(keys[10], 1), 0, 2).astype(jnp.int32)
    segments = draw_segments(jax.random.fold_in(keys[13], 71), 0)
    cotangent = normal_values(keys[12], (TOKENS, D), 1.0, 6.0, ((0, 8),))
    return dict(tokens=tokens, gain_attn=gain_attn, w_query=w_query, w_key=w_key, w_value=w_value, w_out=w_out, gain_ffn=gain_ffn, w_gate=w_gate, w_up=w_up, w_down=w_down, width_pick=width_pick, segments=segments, cotangent=cotangent)


EPSILON = 1e-06
SOFTCAP = 50.0
HIGHEST = lax.Precision.HIGHEST

@jax.custom_vjp
def low(v):
    return lax.optimization_barrier(v.astype(jnp.bfloat16)).astype(jnp.float32)

@jax.custom_vjp
def low_back(v):
    return v

def low_keep(v):
    return (low(v), None)

def low_pass(kept, grad):
    return (grad,)

def back_keep(v):
    return (v, None)

def back_low(kept, grad):
    return (low(grad),)
low.defvjp(low_keep, low_pass)
low_back.defvjp(back_keep, back_low)

def product(left, right):
    return jnp.dot(left, right, precision=HIGHEST, preferred_element_type=jnp.float32)

def width_levels(width_pick):
    return jnp.where(width_pick == 0, 1.0, jnp.where(width_pick == 1, 0.5, 0.25)).astype(jnp.float32)

def bounded(weight, bound):
    return bound * jnp.tanh(weight / bound)

def normalize(values):
    return values * lax.rsqrt(lax.optimization_barrier(jnp.mean(values * values, axis=-1, keepdims=True)) + EPSILON)

def attend(query, key_in, value_in, segments):
    groups, group = segments.shape
    width = min(512, group)
    blocks = group // width
    ratio = HQ // HK
    query_g = query.reshape(groups, group, HK, ratio, HD)
    key_g = key_in.reshape(groups, group, HK, HD)
    value_g = value_in.reshape(groups, group, HK, HD)
    scale = HD ** (-0.5)

    def one_block(index):
        which = index // blocks
        first = index % blocks * width
        query_all = lax.dynamic_index_in_dim(query_g, which, 0, keepdims=False)
        query_blk = lax.dynamic_slice_in_dim(query_all, first, width, 0)
        key_all = lax.dynamic_index_in_dim(key_g, which, 0, keepdims=False)
        value_all = lax.dynamic_index_in_dim(value_g, which, 0, keepdims=False)
        seg_all = lax.dynamic_index_in_dim(segments, which, 0, keepdims=False)
        seg_query = lax.dynamic_slice_in_dim(seg_all, first, width, 0)
        query_pos = first + jnp.arange(width, dtype=jnp.int32)
        key_pos = jnp.arange(group, dtype=jnp.int32)
        allowed = (seg_query[:, None] == seg_all[None, :]) & (key_pos[None, :] <= query_pos[:, None])
        raw = low_back(jnp.einsum('tjrd,kjd->jrtk', query_blk, key_all, precision=HIGHEST))
        capped = SOFTCAP * jnp.tanh(raw * scale / SOFTCAP)
        capped = jnp.where(allowed[None, None], capped, -1e+30)
        largest = lax.optimization_barrier(jnp.max(capped, axis=-1, keepdims=True))
        weights = jnp.exp(capped - largest)
        probs = low(weights / lax.optimization_barrier(jnp.sum(weights, axis=-1, keepdims=True)))
        heads = jnp.einsum('jrtk,kjd->tjrd', probs, value_all, precision=HIGHEST)
        return heads.reshape(width, HQ * HD)
    result = lax.map(jax.checkpoint(one_block), jnp.arange(groups * blocks, dtype=jnp.int32))
    return result.reshape(groups * group, HQ * HD)

def reference(tokens, gain_attn, w_query, w_key, w_value, w_out, gain_ffn, w_gate, w_up, w_down, width_pick, segments, cotangent):
    level_of = width_levels(width_pick)
    inputs = [a.astype(jnp.float32) for a in (tokens, gain_attn, w_query, w_key, w_value, w_out, gain_ffn, w_gate, w_up, w_down)]
    peak_query = lax.optimization_barrier(jnp.max(jnp.abs(inputs[2]), axis=0))
    peak_key = lax.optimization_barrier(jnp.max(jnp.abs(inputs[3]), axis=0))
    peak_value = lax.optimization_barrier(jnp.max(jnp.abs(inputs[4]), axis=0))
    peak_out = lax.optimization_barrier(jnp.max(jnp.abs(inputs[5]), axis=1))
    peak_gate = lax.optimization_barrier(jnp.max(jnp.abs(inputs[7]), axis=0))
    peak_up = lax.optimization_barrier(jnp.max(jnp.abs(inputs[8]), axis=0))
    peak_down = lax.optimization_barrier(jnp.max(jnp.abs(inputs[9]), axis=1))
    bound_query = peak_query[None, :] * level_of[0]
    bound_key = peak_key[None, :] * level_of[1]
    bound_value = peak_value[None, :] * level_of[2]
    bound_out = peak_out[:, None] * level_of[3]
    bound_gate = peak_gate[None, :] * level_of[4]
    bound_up = peak_up[None, :] * level_of[5]
    bound_down = peak_down[:, None] * level_of[6]

    def forward(values, gain_one, wq, wk, wv, wo, gain_two, wg, wu, wd):
        hidden_one = low(normalize(values) * gain_one)
        query = low_back(low(product(hidden_one, low(bounded(wq, bound_query)))))
        key_v = low_back(low(product(hidden_one, low(bounded(wk, bound_key)))))
        value_v = low_back(low(product(hidden_one, low(bounded(wv, bound_value)))))
        heads = low_back(low(attend(query, key_v, value_v, segments)))
        branch = low_back(product(heads, low(bounded(wo, bound_out))))
        resid = values + branch
        hidden_two = low(normalize(resid) * gain_two)
        gate = low_back(product(hidden_two, low(bounded(wg, bound_gate))))
        upper = low_back(product(hidden_two, low(bounded(wu, bound_up))))
        mixed_in = low(jax.nn.gelu(gate, approximate=True) * upper)
        ffn = low_back(product(mixed_in, low(bounded(wd, bound_down))))
        return resid + ffn
    mixed, back = jax.vjp(forward, *inputs)
    grads = back(cotangent.astype(jnp.float32))
    attn_scales = jnp.stack([peak_query, peak_out])
    kv_scales = jnp.stack([peak_key, peak_value])
    ffn_scales = jnp.stack([peak_gate, peak_up, peak_down])
    return (mixed, grads[0], grads[2], grads[3], grads[4], grads[5], grads[7], grads[8], grads[9], grads[1], grads[6], attn_scales, kv_scales, ffn_scales)
```

```python
import jax
import jax.numpy as jnp
from jax import lax
from jax.sharding import PartitionSpec as P

HQ = 8
HK = 4
HD = 256


EPSILON = 1e-06
SOFTCAP = 50.0


def width_levels(width_pick):
    return jnp.where(width_pick == 0, 1.0, jnp.where(width_pick == 1, 0.5, 0.25)).astype(
        jnp.float32
    )


def bounded(weight, bound):
    return (bound * jnp.tanh(weight.astype(jnp.float32) / bound)).astype(jnp.bfloat16)


def bound_slope(weight, bound):
    tangent = jnp.tanh(weight.astype(jnp.float32) / bound)
    return 1.0 - tangent * tangent


def channel_peak(weight, along):
    return jnp.max(jnp.abs(weight.astype(jnp.float32)), axis=along)


def inner_rows(left, right):
    return lax.dot_general(
        left, right, (((0,), (0,)), ((), ())), preferred_element_type=jnp.float32
    )


def against(left, weight):
    return lax.dot_general(
        left, weight, (((1,), (1,)), ((), ())), preferred_element_type=jnp.float32
    )


def forward_norm(values):
    inverse = lax.rsqrt(jnp.mean(values * values, axis=-1, keepdims=True) + EPSILON)
    return (values * inverse, inverse)


def backward_norm(grad_normed, normed, inverse):
    return inverse * (grad_normed - normed * jnp.mean(grad_normed * normed, axis=-1, keepdims=True))


def gelu_tanh(values):
    return jax.nn.gelu(values, approximate=True)


def on_device(
    tokens,
    gain_attn,
    w_query,
    w_key,
    w_value,
    w_out,
    gain_ffn,
    w_gate,
    w_up,
    w_down,
    width_pick,
    segments,
    cotangent,
):
    level_of = width_levels(width_pick)
    peaks = (
        lax.pmax(channel_peak(w_query, 0).astype(jnp.bfloat16), ("dp", "seq")).astype(jnp.float32),
        lax.pmax(channel_peak(w_key, 0).astype(jnp.bfloat16), ("dp", "seq")).astype(jnp.float32),
        lax.pmax(channel_peak(w_value, 0).astype(jnp.bfloat16), ("dp", "seq")).astype(jnp.float32),
        lax.pmax(channel_peak(w_out, 1).astype(jnp.bfloat16), ("dp", "seq")).astype(jnp.float32),
        lax.pmax(channel_peak(w_gate, 0).astype(jnp.bfloat16), ("dp", "seq")).astype(jnp.float32),
        lax.pmax(channel_peak(w_up, 0).astype(jnp.bfloat16), ("dp", "seq")).astype(jnp.float32),
        lax.pmax(channel_peak(w_down, 1).astype(jnp.bfloat16), ("dp", "seq")).astype(jnp.float32),
    )
    peak_query, peak_key, peak_value, peak_out, peak_gate, peak_up, peak_down = peaks
    bound_query = peak_query[None, :] * level_of[0]
    bound_key = peak_key[None, :] * level_of[1]
    bound_value = peak_value[None, :] * level_of[2]
    bound_out = peak_out[:, None] * level_of[3]
    bound_gate = peak_gate[None, :] * level_of[4]
    bound_up = peak_up[None, :] * level_of[5]
    bound_down = peak_down[:, None] * level_of[6]
    fetched = (
        lax.all_gather(w_query, ("dp", "seq"), axis=0, tiled=True),
        lax.all_gather(w_key, ("dp", "seq"), axis=0, tiled=True),
        lax.all_gather(w_value, ("dp", "seq"), axis=0, tiled=True),
        lax.all_gather(gain_attn, ("dp", "seq"), axis=0, tiled=True),
        lax.all_gather(w_gate, ("dp", "seq"), axis=0, tiled=True),
        lax.all_gather(w_up, ("dp", "seq"), axis=0, tiled=True),
        lax.all_gather(gain_ffn, ("dp", "seq"), axis=0, tiled=True),
    )
    full_query, full_key, full_value, full_gain_one = (
        fetched[0],
        fetched[1],
        fetched[2],
        fetched[3],
    )
    later_rows = (fetched[4], fetched[5], fetched[6])
    columns = (
        lax.all_gather(w_out, ("dp", "seq"), axis=1, tiled=True),
        lax.all_gather(w_down, ("dp", "seq"), axis=1, tiled=True),
    )
    eff_query = bounded(full_query, bound_query)
    eff_key = bounded(full_key, bound_key)
    eff_value = bounded(full_value, bound_value)
    eff_out = bounded(columns[0], bound_out)
    eff_down = bounded(columns[1], bound_down)
    gain_one = full_gain_one.astype(jnp.float32)
    mp_count = lax.axis_size("mp")
    local_kv = HK // mp_count
    ratio = HQ // HK
    rows_here = tokens.shape[0]
    seg_row = segments[0]
    group = seg_row.shape[0]
    start = lax.axis_index("seq") * rows_here
    query_pos = start + jnp.arange(rows_here, dtype=jnp.int32)
    key_pos = jnp.arange(group, dtype=jnp.int32)
    seg_query = lax.dynamic_slice_in_dim(seg_row, start, rows_here)
    allowed = (seg_query[:, None] == seg_row[None, :]) & (key_pos[None, :] <= query_pos[:, None])
    scale = HD ** (-0.5)
    tokens_full = tokens.astype(jnp.float32)
    normed_one, inverse_one = forward_norm(tokens_full)
    hidden_one = (normed_one * gain_one).astype(jnp.bfloat16)
    query_b = jnp.dot(hidden_one, eff_query, preferred_element_type=jnp.float32).astype(
        jnp.bfloat16
    )
    key_b = jnp.dot(hidden_one, eff_key, preferred_element_type=jnp.float32).astype(jnp.bfloat16)
    value_b = jnp.dot(hidden_one, eff_value, preferred_element_type=jnp.float32).astype(
        jnp.bfloat16
    )
    key_all, value_all = (
        lax.all_gather(key_b, "seq", axis=0, tiled=True),
        lax.all_gather(value_b, "seq", axis=0, tiled=True),
    )
    query_heads = query_b.reshape(rows_here, local_kv, ratio, HD)
    key_heads = key_all.reshape(group, local_kv, HD)
    value_heads = value_all.reshape(group, local_kv, HD)

    def logits():
        raw = jnp.einsum(
            "tjrd,kjd->jrtk", query_heads, key_heads, preferred_element_type=jnp.float32
        )
        bent = jnp.tanh(raw * scale / SOFTCAP)
        capped = jnp.where(allowed[None, None], SOFTCAP * bent, -1e30)
        return (capped, bent)

    capped, bent = logits()
    largest = jnp.max(capped, axis=-1, keepdims=True)
    weights = jnp.exp(capped - largest)
    totals = jnp.sum(weights, axis=-1, keepdims=True)
    log_total = largest + jnp.log(totals)
    probs_b = (weights / totals).astype(jnp.bfloat16)
    heads_b = (
        jnp.einsum("jrtk,kjd->tjrd", probs_b, value_heads, preferred_element_type=jnp.float32)
        .reshape(rows_here, -1)
        .astype(jnp.bfloat16)
    )
    attn_total = lax.psum(jnp.dot(heads_b, eff_out, preferred_element_type=jnp.float32), "mp")
    resid = tokens_full + attn_total
    eff_gate = bounded(later_rows[0], bound_gate)
    eff_up = bounded(later_rows[1], bound_up)
    gain_two = later_rows[2].astype(jnp.float32)
    normed_two, inverse_two = forward_norm(resid)
    hidden_two = (normed_two * gain_two).astype(jnp.bfloat16)
    gate_full = jnp.dot(hidden_two, eff_gate, preferred_element_type=jnp.float32)
    upper_full = jnp.dot(hidden_two, eff_up, preferred_element_type=jnp.float32)
    gelu_value, gelu_back = jax.vjp(gelu_tanh, gate_full)
    mixed_in = (gelu_value * upper_full).astype(jnp.bfloat16)
    ffn_total = lax.psum(
        jnp.dot(mixed_in, eff_down, preferred_element_type=jnp.float32).astype(jnp.bfloat16), "mp"
    ).astype(jnp.float32)
    mixed = resid + ffn_total
    grad_mixed_in = against(cotangent, eff_down)
    grad_down_eff = inner_rows(mixed_in, cotangent)
    grad_gate_b = gelu_back(grad_mixed_in * upper_full)[0].astype(jnp.bfloat16)
    grad_upper_b = (grad_mixed_in * gelu_value).astype(jnp.bfloat16)
    grad_hidden_two = lax.psum(against(grad_gate_b, eff_gate) + against(grad_upper_b, eff_up), "mp")
    gain_two_part = jnp.sum(grad_hidden_two * normed_two, axis=0)
    grad_resid = cotangent.astype(jnp.float32) + backward_norm(
        grad_hidden_two * gain_two, normed_two, inverse_two
    )
    grad_gate_eff = inner_rows(hidden_two, grad_gate_b)
    grad_up_eff = inner_rows(hidden_two, grad_upper_b)
    grad_resid_b = grad_resid.astype(jnp.bfloat16)
    grad_heads_b = against(grad_resid_b, eff_out).astype(jnp.bfloat16)
    grad_out_eff = inner_rows(heads_b, grad_resid_b)
    grad_heads = grad_heads_b.reshape(rows_here, local_kv, ratio, HD)
    capped_again, bent_again = logits()
    probs = jnp.exp(capped_again - log_total)
    probs_again = probs.astype(jnp.bfloat16)
    grad_probs = jnp.einsum(
        "tjrd,kjd->jrtk", grad_heads, value_heads, preferred_element_type=jnp.float32
    )
    row_dot = jnp.sum(probs * grad_probs, axis=-1, keepdims=True)
    grad_raw_b = (probs * (grad_probs - row_dot) * (1.0 - bent_again * bent_again) * scale).astype(
        jnp.bfloat16
    )
    grad_query_b = (
        jnp.einsum("jrtk,kjd->tjrd", grad_raw_b, key_heads, preferred_element_type=jnp.float32)
        .reshape(rows_here, -1)
        .astype(jnp.bfloat16)
    )
    grad_key_full = jnp.einsum(
        "jrtk,tjrd->kjd", grad_raw_b, query_heads, preferred_element_type=jnp.float32
    ).reshape(group, -1)
    grad_value_full = jnp.einsum(
        "jrtk,tjrd->kjd", probs_again, grad_heads, preferred_element_type=jnp.float32
    ).reshape(group, -1)
    grad_key_sum, grad_value_sum = (
        lax.psum_scatter(grad_key_full, "seq", scatter_dimension=0, tiled=True),
        lax.psum_scatter(grad_value_full, "seq", scatter_dimension=0, tiled=True),
    )
    grad_key_b = grad_key_sum.astype(jnp.bfloat16)
    grad_value_b = grad_value_sum.astype(jnp.bfloat16)
    grad_hidden_one = lax.psum(
        against(grad_query_b, eff_query)
        + against(grad_key_b, eff_key)
        + against(grad_value_b, eff_value),
        "mp",
    )
    gain_one_part = jnp.sum(grad_hidden_one * normed_one, axis=0)
    grad_tokens = grad_resid + backward_norm(grad_hidden_one * gain_one, normed_one, inverse_one)
    grad_query_eff = inner_rows(hidden_one, grad_query_b)
    grad_key_eff = inner_rows(hidden_one, grad_key_b)
    grad_value_eff = inner_rows(hidden_one, grad_value_b)
    row_sums = (
        lax.psum_scatter(grad_query_eff, ("dp", "seq"), scatter_dimension=0, tiled=True),
        lax.psum_scatter(grad_key_eff, ("dp", "seq"), scatter_dimension=0, tiled=True),
        lax.psum_scatter(grad_value_eff, ("dp", "seq"), scatter_dimension=0, tiled=True),
        lax.psum_scatter(grad_gate_eff, ("dp", "seq"), scatter_dimension=0, tiled=True),
        lax.psum_scatter(grad_up_eff, ("dp", "seq"), scatter_dimension=0, tiled=True),
        lax.psum_scatter(gain_one_part, ("dp", "seq"), scatter_dimension=0, tiled=True),
        lax.psum_scatter(gain_two_part, ("dp", "seq"), scatter_dimension=0, tiled=True),
    )
    col_sums = (
        lax.psum_scatter(grad_out_eff, ("dp", "seq"), scatter_dimension=1, tiled=True),
        lax.psum_scatter(grad_down_eff, ("dp", "seq"), scatter_dimension=1, tiled=True),
    )
    sum_query, sum_key, sum_value, sum_gate, sum_up, sum_gain_one, sum_gain_two = row_sums
    out_sum, sum_down = col_sums
    grad_query = sum_query * bound_slope(w_query, bound_query)
    grad_key = sum_key * bound_slope(w_key, bound_key)
    grad_value = sum_value * bound_slope(w_value, bound_value)
    grad_gate = sum_gate * bound_slope(w_gate, bound_gate)
    grad_up = sum_up * bound_slope(w_up, bound_up)
    grad_out = out_sum * bound_slope(w_out, bound_out)
    grad_down = sum_down * bound_slope(w_down, bound_down)
    attn_scales = jnp.stack([peak_query, peak_out])
    kv_scales = jnp.stack([peak_key, peak_value])
    ffn_scales = jnp.stack([peak_gate, peak_up, peak_down])
    return (
        mixed,
        grad_tokens,
        grad_query,
        grad_key,
        grad_value,
        grad_out,
        grad_gate,
        grad_up,
        grad_down,
        sum_gain_one,
        sum_gain_two,
        attn_scales,
        kv_scales,
        ffn_scales,
    )


F32 = jnp.float32
BF16 = jnp.bfloat16


def over_x(values):
    return lax.ppermute(values, "dp", [(i, i ^ 2) for i in range(4)])


def over_core(values):
    return lax.ppermute(values, "dp", [(i, i ^ 1) for i in range(4)])


def over_y(values):
    return lax.ppermute(values, "seq", [(0, 1), (1, 0)])


def over_z(values, step):
    return lax.ppermute(values, "mp", [(i, i ^ step) for i in range(4)])


def after(values, *others):
    return lax.optimization_barrier((values,) + others)[0]


def natural(left, right):
    return jnp.dot(left, right, preferred_element_type=F32)


def half_of(values, index, axis):
    size = values.shape[axis] // 2
    return lax.dynamic_slice_in_dim(values, index * size, size, axis)


def placed(parts, x, y):
    own, from_x, from_y, from_xy = parts
    blank = jnp.zeros((2, own.shape[0], 2) + own.shape[1:], own.dtype)

    def put(into, part, i, j):
        at = (i, 0, j) + (0,) * (own.ndim - 1)
        return lax.dynamic_update_slice(into, part[None, :, None], at)

    full = put(blank, own, x, y)
    full = put(full, from_x, 1 - x, y)
    full = put(full, from_y, x, 1 - y)
    return put(full, from_xy, 1 - x, 1 - y)


def z_chunk(values, index):
    size = values.shape[0] // 4
    return lax.dynamic_slice_in_dim(values, index * size, size, 0)


def z_scatter(partial, z):
    partial_b = partial.astype(BF16)
    arrived = [over_z(z_chunk(partial_b, z ^ step), step) for step in (2, 3, 1)]
    total = z_chunk(partial, z)
    for part in arrived:
        total = total + part.astype(F32)
    return total


def z_gather(chunk, z):
    size = chunk.shape[0]
    full = jnp.zeros((4 * size,) + chunk.shape[1:], chunk.dtype)
    full = lax.dynamic_update_slice_in_dim(full, chunk, z * size, 0)
    for step in (2, 3, 1):
        part = over_z(chunk, step)
        full = lax.dynamic_update_slice_in_dim(full, part, (z ^ step) * size, 0)
    return full


def paired_block(
    tokens,
    gain_attn,
    w_query,
    w_key,
    w_value,
    w_out,
    gain_ffn,
    w_gate,
    w_up,
    w_down,
    width_pick,
    segments,
    cotangent,
):
    dp, y, z = lax.axis_index("dp"), lax.axis_index("seq"), lax.axis_index("mp")
    x, core = dp // 2, dp % 2
    rows, width = tokens.shape
    share = w_query.shape[0]
    n_query, n_key, hidden = w_query.shape[1], w_key.shape[1], w_gate.shape[1]
    half = hidden // 2
    level_of = width_levels(width_pick)

    down_t = w_down.T
    w_ffn = (w_down.T, w_gate, w_up)
    raw = [jnp.stack([half_of(w, core, 1), over_core(half_of(w, 1 - core, 1))]) for w in w_ffn]
    cot_other = over_core(cotangent)

    sizes = [n_query, n_key, n_key, n_query, hidden, hidden, hidden]
    peaks = jnp.concatenate(
        [
            jnp.max(jnp.abs(w), axis=axis)
            for w, axis in (
                (w_query, 0),
                (w_key, 0),
                (w_value, 0),
                (w_out, 1),
                (w_gate, 0),
                (w_up, 0),
                (w_down, 1),
            )
        ]
    )
    place = ((x * 2 + core) * 2 + y) * share
    gains = jnp.zeros((2, width), BF16)
    gains = lax.dynamic_update_slice(gains, jnp.stack([gain_attn, gain_ffn]), (0, place))
    small = (peaks, gains)
    for send in (over_core, over_x, over_y):
        got = send(jnp.concatenate([small[0], small[1].reshape(-1)]))
        small = (
            jnp.maximum(small[0], got[: peaks.size]),
            small[1] + got[peaks.size :].reshape(2, width),
        )
    gain_one, gain_two = small[1][0].astype(F32), small[1][1].astype(F32)
    peak, at = [], 0
    for size in sizes:
        peak.append(small[0][at : at + size].astype(F32))
        at += size
    bounds = [p * level_of[i] for i, p in enumerate(peak)]
    b_query, b_key, b_value, b_out, b_gate, b_up, b_down = bounds

    e_attn = jnp.concatenate(
        [
            bounded(w_query, b_query[None, :]),
            bounded(w_key, b_key[None, :]),
            bounded(w_value, b_value[None, :]),
            bounded(w_out, b_out[:, None]).T,
        ],
        axis=1,
    )
    attn_x, attn_y, attn_core = over_x(e_attn), over_y(e_attn), over_core(e_attn)
    mid = e_attn.shape[1] // 2
    attn_xy = jnp.concatenate([over_y(attn_x[:, :mid]), over_x(attn_y[:, mid:])], axis=1)
    core_x, core_y, core_xy = over_core(attn_x), over_core(attn_y), over_core(attn_xy)

    def both(mine, theirs):
        pair = jnp.stack([mine, theirs])
        return jnp.where(core == 0, pair, pair[::-1])

    e_attn_full = placed(
        (
            both(e_attn, attn_core),
            both(attn_x, core_x),
            both(attn_y, core_y),
            both(attn_xy, core_xy),
        ),
        x,
        y,
    ).reshape(width, -1)
    n_in = n_query + 2 * n_key
    e_in, e_out_t = e_attn_full[:, :n_in], e_attn_full[:, n_in:]

    def gathered(raw_pair, bound, earlier):
        mine = bounded(raw_pair, half_of(bound, core, 0)[None, None, :])
        mine = jnp.where(core == 0, mine, mine[::-1])
        mine = after(mine, earlier)
        from_x, from_y = over_x(mine), over_y(mine)
        first, second = over_y(from_x[0]), over_x(from_y[1])
        diagonal = jnp.stack([first, second])
        return placed((mine, from_x, from_y, diagonal), x, y).reshape(width, half), from_x

    e_down_t, mark = gathered(raw[0], b_down, attn_x)
    e_gate, mark = gathered(raw[1], b_gate, mark)
    e_up, mark = gathered(raw[2], b_up, mark)

    tokens_full = tokens.astype(F32)
    normed_one, _ = forward_norm(tokens_full)
    hidden_one = (normed_one * gain_one).astype(BF16)
    projected = natural(hidden_one, e_in).astype(BF16)
    query_b = projected[:, :n_query]
    kv_own = projected[:, n_query:]
    kv_other = over_y(kv_own)
    kv = jnp.concatenate([kv_own, kv_other], axis=0)
    ratio = n_query // HD
    query_heads = query_b.reshape(rows, ratio, HD)
    key_all, value_all = kv[:, :HD], kv[:, HD:]
    seg_row = segments[0]
    own_at, other_at = y * rows, (1 - y) * rows
    order = jnp.arange(rows, dtype=jnp.int32)
    query_pos = own_at + order
    key_pos = jnp.concatenate([own_at + order, other_at + order])
    seg_query = lax.dynamic_slice_in_dim(seg_row, own_at, rows)
    seg_key = jnp.concatenate([seg_query, lax.dynamic_slice_in_dim(seg_row, other_at, rows)])
    allowed = (seg_query[:, None] == seg_key[None, :]) & (key_pos[None, :] <= query_pos[:, None])
    scale = HD ** (-0.5)

    def logits():
        raw = jnp.einsum("trd,kd->rtk", query_heads, key_all, preferred_element_type=F32)
        bent = jnp.tanh(raw * scale / SOFTCAP)
        capped = jnp.where(allowed[None], SOFTCAP * bent, -1e30)
        return capped, bent

    capped, bent = logits()
    largest = jnp.max(capped, axis=-1, keepdims=True)
    weights = jnp.exp(capped - largest)
    totals = jnp.sum(weights, axis=-1, keepdims=True)
    log_total = largest + jnp.log(totals)
    probs_b = (weights / totals).astype(BF16)
    heads_b = (
        jnp.einsum("rtk,kd->trd", probs_b, value_all, preferred_element_type=F32)
        .reshape(rows, -1)
        .astype(BF16)
    )
    attn_chunk = z_scatter(against(heads_b, e_out_t), z)

    resid = z_chunk(tokens, z).astype(F32) + attn_chunk
    normed_two, inverse_two = forward_norm(resid)
    hidden_two = z_gather((normed_two * gain_two).astype(BF16), z)
    hidden_two = jnp.concatenate([hidden_two, over_core(hidden_two)], axis=0)
    cot_pair = jnp.concatenate([cotangent, cot_other], axis=0)
    grad_mixed_in = natural(cot_pair, e_down_t)
    gate_full = natural(hidden_two, e_gate)
    upper_full = natural(hidden_two, e_up)
    gelu_value, gelu_back = jax.vjp(gelu_tanh, gate_full)
    mixed_in = (gelu_value * upper_full).astype(BF16)
    grad_gate_b = gelu_back(grad_mixed_in * upper_full)[0].astype(BF16)
    grad_upper_b = (grad_mixed_in * gelu_value).astype(BF16)
    back_part = against(grad_gate_b, e_gate) + against(grad_upper_b, e_up)
    back_part = back_part[:rows] + over_core(back_part[rows:].astype(BF16)).astype(F32)
    grad_hidden_two = z_scatter(back_part, z)
    gain_two_part = jnp.sum(grad_hidden_two * normed_two, axis=0)
    grad_resid = z_chunk(cotangent, z).astype(F32) + backward_norm(
        grad_hidden_two * gain_two, normed_two, inverse_two
    )
    grad_resid_b = z_gather(grad_resid.astype(BF16), z)

    def scattered(left, right):
        grad = inner_rows(left, right).astype(BF16).reshape(2, 2, 2, share, half)

        def pick(values, index, axis):
            return lax.dynamic_index_in_dim(values, index, axis, keepdims=False)

        first, second = grad[:, 0], grad[:, 1]
        first = pick(first, x, 0).astype(F32) + over_x(pick(first, 1 - x, 0)).astype(F32)
        second = pick(second, y, 1).astype(F32) + over_y(pick(second, 1 - y, 1)).astype(F32)
        first = pick(first, y, 0) + over_y(pick(first, 1 - y, 0).astype(BF16)).astype(F32)
        second = pick(second, x, 0) + over_x(pick(second, 1 - x, 0).astype(BF16)).astype(F32)
        mine = jnp.where(core == 0, first, second)
        theirs = over_core(jnp.where(core == 0, second, first).astype(BF16)).astype(F32)
        return jnp.where(
            core == 0,
            jnp.concatenate([mine, theirs], axis=1),
            jnp.concatenate([theirs, mine], axis=1),
        )

    sum_gate = scattered(hidden_two, grad_gate_b)
    sum_up = scattered(hidden_two, grad_upper_b)
    sum_down = scattered(cot_pair, mixed_in).T

    ffn_part = against(mixed_in, e_down_t)
    ffn_part = ffn_part[:rows] + over_core(ffn_part[rows:].astype(BF16)).astype(F32)
    mixed = z_gather((resid + z_scatter(ffn_part, z)).astype(BF16), z).astype(F32)

    grad_heads = natural(grad_resid_b, e_out_t).astype(BF16).reshape(rows, ratio, HD)
    capped_again, bent_again = logits()
    probs = jnp.exp(capped_again - log_total)
    probs_again = probs.astype(BF16)
    grad_probs = jnp.einsum("trd,kd->rtk", grad_heads, value_all, preferred_element_type=F32)
    row_dot = jnp.sum(probs * grad_probs, axis=-1, keepdims=True)
    grad_raw_b = (probs * (grad_probs - row_dot) * (1.0 - bent_again * bent_again) * scale).astype(
        BF16
    )
    grad_query_b = (
        jnp.einsum("rtk,kd->trd", grad_raw_b, key_all, preferred_element_type=F32)
        .reshape(rows, -1)
        .astype(BF16)
    )
    grad_kv = jnp.concatenate(
        [
            jnp.einsum("rtk,trd->kd", grad_raw_b, query_heads, preferred_element_type=F32),
            jnp.einsum("rtk,trd->kd", probs_again, grad_heads, preferred_element_type=F32),
        ],
        axis=1,
    )
    grad_kv_b = (grad_kv[:rows] + over_y(grad_kv[rows:].astype(BF16)).astype(F32)).astype(BF16)
    grad_in_b = jnp.concatenate([grad_query_b, grad_kv_b], axis=1)
    grad_hidden_one = z_scatter(against(grad_in_b, e_in), z)
    chunk_one, inverse_one = forward_norm(z_chunk(tokens, z).astype(F32))
    gain_one_part = jnp.sum(grad_hidden_one * chunk_one, axis=0)
    grad_chunk = grad_resid + backward_norm(grad_hidden_one * gain_one, chunk_one, inverse_one)
    grad_tokens = z_gather(grad_chunk.astype(BF16), z).astype(F32)

    def core_rows(values):
        return lax.dynamic_index_in_dim(
            values.reshape(values.shape[0], 2, 2, 2 * share), core, 2, keepdims=False
        ).reshape(values.shape[0], -1)

    def core_pair(values):
        pair = values.reshape(values.shape[0], 2, 2, 2 * share)
        mine = lax.dynamic_index_in_dim(pair, core, 2, keepdims=False)
        theirs = lax.dynamic_index_in_dim(pair, 1 - core, 2, keepdims=False)
        return jnp.concatenate([mine, over_core(theirs)], axis=0).reshape(2 * rows, -1)

    hidden_pair = core_pair(hidden_one)
    resid_pair = core_pair(grad_resid_b)
    heads_pair = jnp.concatenate([heads_b, over_core(heads_b)], axis=0)
    in_pair = jnp.concatenate([grad_in_b, over_core(grad_in_b)], axis=0)

    def scattered_rows(left, right):
        grad = inner_rows(left, right).astype(BF16)
        cut = grad.shape[1] // 2
        grad = grad.reshape(2, 2, share, -1)

        def pick(values, index, axis):
            return lax.dynamic_index_in_dim(values, index, axis, keepdims=False)

        first, second = grad[..., :cut], grad[..., cut:]
        first = pick(first, x, 0).astype(F32) + over_x(pick(first, 1 - x, 0)).astype(F32)
        second = pick(second, y, 1).astype(F32) + over_y(pick(second, 1 - y, 1)).astype(F32)
        first = pick(first, y, 0) + over_y(pick(first, 1 - y, 0).astype(BF16)).astype(F32)
        second = pick(second, x, 0) + over_x(pick(second, 1 - x, 0).astype(BF16)).astype(F32)
        return jnp.concatenate([first, second], axis=1)

    sum_out = scattered_rows(resid_pair, heads_pair).T
    sum_in = scattered_rows(hidden_pair, in_pair)
    sum_query = sum_in[:, :n_query]
    sum_key = sum_in[:, n_query : n_query + n_key]
    sum_value = sum_in[:, n_query + n_key :]

    gain_sum = jnp.stack([gain_one_part, gain_two_part])
    gain_sum = gain_sum + over_z(gain_sum, 1)
    gain_sum = gain_sum + over_z(gain_sum, 2)
    gain_sum = gain_sum + over_core(gain_sum)
    gain_sum = gain_sum + over_x(gain_sum)
    gain_sum = gain_sum + over_y(gain_sum)
    gain_sum = lax.dynamic_slice(gain_sum, (0, place), (2, share))

    grad_query = sum_query * bound_slope(w_query, b_query[None, :])
    grad_key = sum_key * bound_slope(w_key, b_key[None, :])
    grad_value = sum_value * bound_slope(w_value, b_value[None, :])
    grad_gate = sum_gate * bound_slope(w_gate, b_gate[None, :])
    grad_up = sum_up * bound_slope(w_up, b_up[None, :])
    grad_out = sum_out * bound_slope(w_out, b_out[:, None])
    grad_down = sum_down * bound_slope(w_down, b_down[:, None])
    return (
        mixed,
        grad_tokens,
        grad_query,
        grad_key,
        grad_value,
        grad_out,
        grad_gate,
        grad_up,
        grad_down,
        gain_sum[0],
        gain_sum[1],
        jnp.stack([peak[0], peak[3]]),
        jnp.stack([peak[1], peak[2]]),
        jnp.stack([peak[4], peak[5], peak[6]]),
    )


def solution(mesh):
    in_specs = (
        P(("dp", "seq"), None),
        P(("dp", "seq")),
        P(("dp", "seq"), "mp"),
        P(("dp", "seq"), "mp"),
        P(("dp", "seq"), "mp"),
        P("mp", ("dp", "seq")),
        P(("dp", "seq")),
        P(("dp", "seq"), "mp"),
        P(("dp", "seq"), "mp"),
        P("mp", ("dp", "seq")),
        P(),
        P("dp", None),
        P(("dp", "seq"), None),
    )
    out_specs = (
        P(("dp", "seq"), None),
        P(("dp", "seq"), None),
        P(("dp", "seq"), "mp"),
        P(("dp", "seq"), "mp"),
        P(("dp", "seq"), "mp"),
        P("mp", ("dp", "seq")),
        P(("dp", "seq"), "mp"),
        P(("dp", "seq"), "mp"),
        P("mp", ("dp", "seq")),
        P(("dp", "seq")),
        P(("dp", "seq")),
        P(None, "mp"),
        P(None, "mp"),
        P(None, "mp"),
    )
    shape = dict(mesh.shape)
    paired = shape["dp"] == 4 and shape["seq"] == 2 and shape["mp"] == 4
    block = paired_block if paired else on_device
    return jax.shard_map(
        block, mesh=mesh, in_specs=in_specs, out_specs=out_specs, check_vma=False
    )
```

```python
import itertools

import jax
import jax.numpy as jnp
from jax import lax
from jax.experimental import pallas as pl
from jax.experimental.pallas import tpu as pltpu
from jax.sharding import PartitionSpec as P

HQ = 8
HK = 4
HD = 256


EPSILON = 1e-06
SOFTCAP = 50.0


def width_levels(width_pick):
    return jnp.where(width_pick == 0, 1.0, jnp.where(width_pick == 1, 0.5, 0.25)).astype(
        jnp.float32
    )


def bounded(weight, bound):
    return (bound * jnp.tanh(weight.astype(jnp.float32) / bound)).astype(jnp.bfloat16)


def bound_slope(weight, bound):
    tangent = jnp.tanh(weight.astype(jnp.float32) / bound)
    return 1.0 - tangent * tangent


def channel_peak(weight, along):
    return jnp.max(jnp.abs(weight.astype(jnp.float32)), axis=along)


def inner_rows(left, right):
    return lax.dot_general(
        left, right, (((0,), (0,)), ((), ())), preferred_element_type=jnp.float32
    )


def against(left, weight):
    return lax.dot_general(
        left, weight, (((1,), (1,)), ((), ())), preferred_element_type=jnp.float32
    )


def forward_norm(values):
    inverse = lax.rsqrt(jnp.mean(values * values, axis=-1, keepdims=True) + EPSILON)
    return (values * inverse, inverse)


def backward_norm(grad_normed, normed, inverse):
    return inverse * (grad_normed - normed * jnp.mean(grad_normed * normed, axis=-1, keepdims=True))


def gelu_tanh(values):
    return jax.nn.gelu(values, approximate=True)


def on_device(
    tokens,
    gain_attn,
    w_query,
    w_key,
    w_value,
    w_out,
    gain_ffn,
    w_gate,
    w_up,
    w_down,
    width_pick,
    segments,
    cotangent,
):
    level_of = width_levels(width_pick)
    peaks = (
        lax.pmax(channel_peak(w_query, 0).astype(jnp.bfloat16), ("dp", "seq")).astype(jnp.float32),
        lax.pmax(channel_peak(w_key, 0).astype(jnp.bfloat16), ("dp", "seq")).astype(jnp.float32),
        lax.pmax(channel_peak(w_value, 0).astype(jnp.bfloat16), ("dp", "seq")).astype(jnp.float32),
        lax.pmax(channel_peak(w_out, 1).astype(jnp.bfloat16), ("dp", "seq")).astype(jnp.float32),
        lax.pmax(channel_peak(w_gate, 0).astype(jnp.bfloat16), ("dp", "seq")).astype(jnp.float32),
        lax.pmax(channel_peak(w_up, 0).astype(jnp.bfloat16), ("dp", "seq")).astype(jnp.float32),
        lax.pmax(channel_peak(w_down, 1).astype(jnp.bfloat16), ("dp", "seq")).astype(jnp.float32),
    )
    peak_query, peak_key, peak_value, peak_out, peak_gate, peak_up, peak_down = peaks
    bound_query = peak_query[None, :] * level_of[0]
    bound_key = peak_key[None, :] * level_of[1]
    bound_value = peak_value[None, :] * level_of[2]
    bound_out = peak_out[:, None] * level_of[3]
    bound_gate = peak_gate[None, :] * level_of[4]
    bound_up = peak_up[None, :] * level_of[5]
    bound_down = peak_down[:, None] * level_of[6]
    fetched = (
        lax.all_gather(w_query, ("dp", "seq"), axis=0, tiled=True),
        lax.all_gather(w_key, ("dp", "seq"), axis=0, tiled=True),
        lax.all_gather(w_value, ("dp", "seq"), axis=0, tiled=True),
        lax.all_gather(gain_attn, ("dp", "seq"), axis=0, tiled=True),
        lax.all_gather(w_gate, ("dp", "seq"), axis=0, tiled=True),
        lax.all_gather(w_up, ("dp", "seq"), axis=0, tiled=True),
        lax.all_gather(gain_ffn, ("dp", "seq"), axis=0, tiled=True),
    )
    full_query, full_key, full_value, full_gain_one = (
        fetched[0],
        fetched[1],
        fetched[2],
        fetched[3],
    )
    later_rows = (fetched[4], fetched[5], fetched[6])
    columns = (
        lax.all_gather(w_out, ("dp", "seq"), axis=1, tiled=True),
        lax.all_gather(w_down, ("dp", "seq"), axis=1, tiled=True),
    )
    eff_query = bounded(full_query, bound_query)
    eff_key = bounded(full_key, bound_key)
    eff_value = bounded(full_value, bound_value)
    eff_out = bounded(columns[0], bound_out)
    eff_down = bounded(columns[1], bound_down)
    gain_one = full_gain_one.astype(jnp.float32)
    mp_count = lax.axis_size("mp")
    local_kv = HK // mp_count
    ratio = HQ // HK
    rows_here = tokens.shape[0]
    seg_row = segments[0]
    group = seg_row.shape[0]
    start = lax.axis_index("seq") * rows_here
    query_pos = start + jnp.arange(rows_here, dtype=jnp.int32)
    key_pos = jnp.arange(group, dtype=jnp.int32)
    seg_query = lax.dynamic_slice_in_dim(seg_row, start, rows_here)
    allowed = (seg_query[:, None] == seg_row[None, :]) & (key_pos[None, :] <= query_pos[:, None])
    scale = HD ** (-0.5)
    tokens_full = tokens.astype(jnp.float32)
    normed_one, inverse_one = forward_norm(tokens_full)
    hidden_one = (normed_one * gain_one).astype(jnp.bfloat16)
    query_b = jnp.dot(hidden_one, eff_query, preferred_element_type=jnp.float32).astype(
        jnp.bfloat16
    )
    key_b = jnp.dot(hidden_one, eff_key, preferred_element_type=jnp.float32).astype(jnp.bfloat16)
    value_b = jnp.dot(hidden_one, eff_value, preferred_element_type=jnp.float32).astype(
        jnp.bfloat16
    )
    key_all, value_all = (
        lax.all_gather(key_b, "seq", axis=0, tiled=True),
        lax.all_gather(value_b, "seq", axis=0, tiled=True),
    )
    query_heads = query_b.reshape(rows_here, local_kv, ratio, HD)
    key_heads = key_all.reshape(group, local_kv, HD)
    value_heads = value_all.reshape(group, local_kv, HD)

    def logits():
        raw = jnp.einsum(
            "tjrd,kjd->jrtk", query_heads, key_heads, preferred_element_type=jnp.float32
        )
        bent = jnp.tanh(raw * scale / SOFTCAP)
        capped = jnp.where(allowed[None, None], SOFTCAP * bent, -1e30)
        return (capped, bent)

    capped, bent = logits()
    largest = jnp.max(capped, axis=-1, keepdims=True)
    weights = jnp.exp(capped - largest)
    totals = jnp.sum(weights, axis=-1, keepdims=True)
    log_total = largest + jnp.log(totals)
    probs_b = (weights / totals).astype(jnp.bfloat16)
    heads_b = (
        jnp.einsum("jrtk,kjd->tjrd", probs_b, value_heads, preferred_element_type=jnp.float32)
        .reshape(rows_here, -1)
        .astype(jnp.bfloat16)
    )
    attn_total = lax.psum(jnp.dot(heads_b, eff_out, preferred_element_type=jnp.float32), "mp")
    resid = tokens_full + attn_total
    eff_gate = bounded(later_rows[0], bound_gate)
    eff_up = bounded(later_rows[1], bound_up)
    gain_two = later_rows[2].astype(jnp.float32)
    normed_two, inverse_two = forward_norm(resid)
    hidden_two = (normed_two * gain_two).astype(jnp.bfloat16)
    gate_full = jnp.dot(hidden_two, eff_gate, preferred_element_type=jnp.float32)
    upper_full = jnp.dot(hidden_two, eff_up, preferred_element_type=jnp.float32)
    gelu_value, gelu_back = jax.vjp(gelu_tanh, gate_full)
    mixed_in = (gelu_value * upper_full).astype(jnp.bfloat16)
    ffn_total = lax.psum(
        jnp.dot(mixed_in, eff_down, preferred_element_type=jnp.float32).astype(jnp.bfloat16), "mp"
    ).astype(jnp.float32)
    mixed = resid + ffn_total
    grad_mixed_in = against(cotangent, eff_down)
    grad_down_eff = inner_rows(mixed_in, cotangent)
    grad_gate_b = gelu_back(grad_mixed_in * upper_full)[0].astype(jnp.bfloat16)
    grad_upper_b = (grad_mixed_in * gelu_value).astype(jnp.bfloat16)
    grad_hidden_two = lax.psum(against(grad_gate_b, eff_gate) + against(grad_upper_b, eff_up), "mp")
    gain_two_part = jnp.sum(grad_hidden_two * normed_two, axis=0)
    grad_resid = cotangent.astype(jnp.float32) + backward_norm(
        grad_hidden_two * gain_two, normed_two, inverse_two
    )
    grad_gate_eff = inner_rows(hidden_two, grad_gate_b)
    grad_up_eff = inner_rows(hidden_two, grad_upper_b)
    grad_resid_b = grad_resid.astype(jnp.bfloat16)
    grad_heads_b = against(grad_resid_b, eff_out).astype(jnp.bfloat16)
    grad_out_eff = inner_rows(heads_b, grad_resid_b)
    grad_heads = grad_heads_b.reshape(rows_here, local_kv, ratio, HD)
    capped_again, bent_again = logits()
    probs = jnp.exp(capped_again - log_total)
    probs_again = probs.astype(jnp.bfloat16)
    grad_probs = jnp.einsum(
        "tjrd,kjd->jrtk", grad_heads, value_heads, preferred_element_type=jnp.float32
    )
    row_dot = jnp.sum(probs * grad_probs, axis=-1, keepdims=True)
    grad_raw_b = (probs * (grad_probs - row_dot) * (1.0 - bent_again * bent_again) * scale).astype(
        jnp.bfloat16
    )
    grad_query_b = (
        jnp.einsum("jrtk,kjd->tjrd", grad_raw_b, key_heads, preferred_element_type=jnp.float32)
        .reshape(rows_here, -1)
        .astype(jnp.bfloat16)
    )
    grad_key_full = jnp.einsum(
        "jrtk,tjrd->kjd", grad_raw_b, query_heads, preferred_element_type=jnp.float32
    ).reshape(group, -1)
    grad_value_full = jnp.einsum(
        "jrtk,tjrd->kjd", probs_again, grad_heads, preferred_element_type=jnp.float32
    ).reshape(group, -1)
    grad_key_sum, grad_value_sum = (
        lax.psum_scatter(grad_key_full, "seq", scatter_dimension=0, tiled=True),
        lax.psum_scatter(grad_value_full, "seq", scatter_dimension=0, tiled=True),
    )
    grad_key_b = grad_key_sum.astype(jnp.bfloat16)
    grad_value_b = grad_value_sum.astype(jnp.bfloat16)
    grad_hidden_one = lax.psum(
        against(grad_query_b, eff_query)
        + against(grad_key_b, eff_key)
        + against(grad_value_b, eff_value),
        "mp",
    )
    gain_one_part = jnp.sum(grad_hidden_one * normed_one, axis=0)
    grad_tokens = grad_resid + backward_norm(grad_hidden_one * gain_one, normed_one, inverse_one)
    grad_query_eff = inner_rows(hidden_one, grad_query_b)
    grad_key_eff = inner_rows(hidden_one, grad_key_b)
    grad_value_eff = inner_rows(hidden_one, grad_value_b)
    row_sums = (
        lax.psum_scatter(grad_query_eff, ("dp", "seq"), scatter_dimension=0, tiled=True),
        lax.psum_scatter(grad_key_eff, ("dp", "seq"), scatter_dimension=0, tiled=True),
        lax.psum_scatter(grad_value_eff, ("dp", "seq"), scatter_dimension=0, tiled=True),
        lax.psum_scatter(grad_gate_eff, ("dp", "seq"), scatter_dimension=0, tiled=True),
        lax.psum_scatter(grad_up_eff, ("dp", "seq"), scatter_dimension=0, tiled=True),
        lax.psum_scatter(gain_one_part, ("dp", "seq"), scatter_dimension=0, tiled=True),
        lax.psum_scatter(gain_two_part, ("dp", "seq"), scatter_dimension=0, tiled=True),
    )
    col_sums = (
        lax.psum_scatter(grad_out_eff, ("dp", "seq"), scatter_dimension=1, tiled=True),
        lax.psum_scatter(grad_down_eff, ("dp", "seq"), scatter_dimension=1, tiled=True),
    )
    sum_query, sum_key, sum_value, sum_gate, sum_up, sum_gain_one, sum_gain_two = row_sums
    out_sum, sum_down = col_sums
    grad_query = sum_query * bound_slope(w_query, bound_query)
    grad_key = sum_key * bound_slope(w_key, bound_key)
    grad_value = sum_value * bound_slope(w_value, bound_value)
    grad_gate = sum_gate * bound_slope(w_gate, bound_gate)
    grad_up = sum_up * bound_slope(w_up, bound_up)
    grad_out = out_sum * bound_slope(w_out, bound_out)
    grad_down = sum_down * bound_slope(w_down, bound_down)
    attn_scales = jnp.stack([peak_query, peak_out])
    kv_scales = jnp.stack([peak_key, peak_value])
    ffn_scales = jnp.stack([peak_gate, peak_up, peak_down])
    return (
        mixed,
        grad_tokens,
        grad_query,
        grad_key,
        grad_value,
        grad_out,
        grad_gate,
        grad_up,
        grad_down,
        sum_gain_one,
        sum_gain_two,
        attn_scales,
        kv_scales,
        ffn_scales,
    )


F32 = jnp.float32
BF16 = jnp.bfloat16
MESH = pl.DeviceIdType.MESH
VMEM_BYTES = 63 * 1024 * 1024


def natural(left, right):
    return jnp.dot(left, right, preferred_element_type=F32)


def mul(index, size):
    return pl.multiple_of(index * size, size)


class Place:
    def __init__(self):
        dp, y, z = lax.axis_index("dp"), lax.axis_index("seq"), lax.axis_index("mp")
        x, core = dp // 2, dp % 2
        self.x, self.y, self.z, self.core = x, y, z, core
        self.to_core = (x * 2 + (1 - core), y, z)
        self.to_x = ((1 - x) * 2 + core, y, z)
        self.to_y = (dp, 1 - y, z)
        self.to_xy = ((1 - x) * 2 + core, 1 - y, z)
        self.to_up = (dp, y, jnp.minimum(z + 1, 3))
        self.to_down = (dp, y, jnp.maximum(z - 1, 0))

    def slot(self, x, core, y):
        return (x * 2 + core) * 2 + y


def greet(here, targets):
    barrier = pltpu.get_barrier_semaphore()
    for target in targets:
        pl.semaphore_signal(barrier, inc=1, device_id=target, device_id_type=MESH)

    @pl.when(here.z < 3)
    def _():
        pl.semaphore_signal(barrier, inc=1, device_id=here.to_up, device_id_type=MESH)

    @pl.when(here.z > 0)
    def _():
        pl.semaphore_signal(barrier, inc=1, device_id=here.to_down, device_id_type=MESH)

    inner = (here.z < 3) & (here.z > 0)

    @pl.when(inner)
    def _():
        pl.semaphore_wait(barrier, len(targets) + 2)

    @pl.when(jnp.logical_not(inner))
    def _():
        pl.semaphore_wait(barrier, len(targets) + 1)


def remote(src, dst, send, recv, target):
    return pltpu.make_async_remote_copy(
        src_ref=src,
        dst_ref=dst,
        send_sem=send,
        recv_sem=recv,
        device_id=target,
        device_id_type=MESH,
    )


class Line:
    def __init__(self, here, partial, gathered, land, total, sems, transform, own=None, give=None, subs=4):
        self.here, self.partial, self.gathered, self.own = here, partial, gathered, own
        self.land, self.total, self.sems, self.transform = land, total, sems, transform
        self.size, self.subs = partial.shape[0] // 4, subs
        self.give = give
        self.part = self.size // subs

    def rows(self, chunk, sub):
        return pl.ds(pl.multiple_of(chunk * self.size + sub * self.part, self.part), self.part)

    def scatter_copy(self, way, step, sub=None):
        z = self.here.z
        chunk = jnp.minimum(z + 4 - step, 3) if way == 0 else jnp.maximum(z - 4 + step, 0)
        rows, spot = self.span(chunk, sub)
        at = (0, way, step - 1)
        recv = self.sems[1].at[at + (sub or 0,)]
        target = self.here.to_up if way == 0 else self.here.to_down
        dst = self.land.at[way, step - 1, spot]
        return remote(self.partial.at[rows], dst, self.sems[0].at[at], recv, target)

    def gather_copy(self, way, step, sub=None):
        z = self.here.z
        chunk = jnp.maximum(z - (step - 1), 0) if way == 0 else jnp.minimum(z + (step - 1), 3)
        rows, spot = self.span(chunk, sub)
        at = (1, way, step - 1)
        recv = self.sems[1].at[at + (sub or 0,)]
        target = self.here.to_up if way == 0 else self.here.to_down
        ref = self.gathered.at[rows]
        src = ref
        if self.own is not None and step == 1:
            src = self.own.at[spot]
        return remote(src, ref, self.sems[0].at[at], recv, target)

    def span(self, chunk, sub):
        if sub is None:
            return pl.ds(pl.multiple_of(chunk * self.size, self.size), self.size), pl.ds(0, self.size)
        return self.rows(chunk, sub), pl.ds(sub * self.part, self.part)

    def far(self, way):
        return self.here.z if way == 0 else 3 - self.here.z

    def scatter(self, step, sub):
        for way in (0, 1):
            far = self.far(way)

            @pl.when((far <= step - 1) & (far <= 2))
            def _(way=way, far=far):
                if step > 1:

                    @pl.when(far >= 1)
                    def _():
                        self.scatter_copy(way, step - 1, sub).wait_recv()
                        z = self.here.z
                        chunk = z + 4 - step if way == 0 else z - 4 + step
                        rows = self.rows(chunk, sub)
                        came = self.land[way, step - 2, pl.ds(sub * self.part, self.part), :]
                        mine = self.partial[rows, :].astype(F32)
                        self.partial[rows, :] = (mine + came.astype(F32)).astype(BF16)

                self.scatter_copy(way, step, sub).start()

    def finish(self, sub):
        rows = self.rows(self.here.z, sub)
        spot = pl.ds(sub * self.part, self.part)
        self.total[...] = self.partial[rows, :].astype(F32)
        for way in (0, 1):

            @pl.when(self.far(way) >= 1)
            def _(way=way):
                self.scatter_copy(way, 3, sub).wait_recv()
                self.total[...] += self.land[way, 2, spot, :].astype(F32)

        result = self.transform(sub, spot, self.total[...])
        if self.own is None:
            self.gathered[rows, :] = result
        else:
            self.own[spot, :] = result

    def gather(self, step, sub):
        for way in (0, 1):
            far = self.far(way)

            @pl.when((far >= step - 1) & (far <= 2))
            def _(way=way):
                self.gather_copy(way, step, sub).start()

    def landed(self, step, sub):
        for way in (0, 1):

            @pl.when(self.far(way) >= step)
            def _(way=way):
                self.gather_copy(way, step, sub).wait_recv()

    def ticks(self):
        self.scatter(1, 0)
        for tick in range(self.subs + 6):
            for stage in range(7):
                sub = tick - stage + (stage == 0)
                if 0 <= sub < self.subs:
                    if stage < 3:
                        self.scatter(stage + 1, sub)
                    else:
                        if stage == 3:
                            self.finish(sub)
                        else:
                            self.landed(stage - 3, sub)
                        if stage < 6:
                            self.gather(stage - 2, sub)
                        elif self.give is not None:
                            self.give(sub)
            yield tick

    def close(self):
        for step in (1, 2, 3):
            for way in (0, 1):
                far = self.far(way)

                @pl.when((far <= step - 1) & (far <= 2))
                def _(way=way, step=step):
                    self.scatter_copy(way, step).wait_send()

                @pl.when((far >= step - 1) & (far <= 2))
                def _(way=way, step=step):
                    self.gather_copy(way, step).wait_send()


def line_sems(subs):
    return [pltpu.SemaphoreType.DMA((2, 2, 3)), pltpu.SemaphoreType.DMA((2, 2, 3, subs))]


def line_scratch(rows, width, subs):
    return [
        pltpu.VMEM((rows, width), BF16),
        pltpu.VMEM((2, 3, rows // 4, width), BF16),
        pltpu.VMEM((rows // 4 // subs, width), F32),
        *line_sems(subs),
    ]


class Mail:
    def __init__(self, send_sem, recv_sem):
        self.send_sem, self.recv_sem = send_sem, recv_sem
        self.sent, self.gone = [], []
        self.n_send = self.n_recv = 0

    def make(self, src, dst, target, send_at=None, recv_at=None):
        alone = send_at is None
        if alone:
            send_at, self.n_send = self.n_send, self.n_send + 1
        if recv_at is None:
            recv_at, self.n_recv = self.n_recv, self.n_recv + 1
        copy = remote(src, dst, self.send_sem.at[send_at], self.recv_sem.at[recv_at], target)
        if alone:
            self.sent.append(copy)
        return copy

    def send(self, src, dst, target, send_at=None, recv_at=None):
        copy = self.make(src, dst, target, send_at, recv_at)
        copy.start()
        return copy

    def group(self, leaving, coming, target):
        send_at, recv_at = self.n_send, self.n_recv
        self.n_send, self.n_recv = send_at + 1, recv_at + 1
        sems = self.send_sem.at[send_at], self.recv_sem.at[recv_at]
        self.sent.append(remote(leaving, leaving, *sems, target))
        return send_at, recv_at, remote(coming, coming, *sems, target)

    def finish(self, copy):
        copy.wait_send()
        self.gone.append(copy)

    def close(self):
        for copy in self.sent:
            if all(copy is not other for other in self.gone):
                copy.wait_send()


FRONT_SUBS, BACK_SUBS = 4, 8


EXTRA = 16


def edge(y, rows):
    return pl.multiple_of((1 - y) * (rows - EXTRA), EXTRA)


def number_rows(segments, y, out):
    rows = out.shape[0] - EXTRA

    def turned(start):
        row = segments[:, pl.ds(pl.multiple_of(start, 128), 128)].astype(F32)
        return jnp.transpose(jnp.broadcast_to(row, (128, 128)))

    for first in range(0, rows, 128):
        out[first : first + 128, :] = turned(y * rows + first)
    out[rows:, :] = jnp.where(y == 0, turned(rows)[:EXTRA], turned(rows - 128)[128 - EXTRA :])


def visible(keys, numbers, position, y):
    count = keys.shape[0]
    rows = count - EXTRA
    key = lax.broadcasted_iota(jnp.int32, (count, 1), 0)
    key_pos = jnp.where(key < rows, y * rows + key, key - EXTRA * y)
    return (keys[:, 0:1] == numbers) & (key_pos <= position)


def beside(value, n_heads):
    return jnp.concatenate([value] * n_heads, axis=1)


def extra_visible(keys, y, n_heads):
    rows = keys.shape[0] - EXTRA
    numbers = jnp.transpose(keys[rows:, :])[0:1, :]
    position = rows - EXTRA * y + lax.broadcasted_iota(jnp.int32, (1, EXTRA), 1)
    return visible(keys, beside(numbers, n_heads), beside(position, n_heads), y)


def soft_probs(query, kv, allowed):
    raw = against(kv[:, :HD], query)
    bent = jnp.tanh(raw * HD ** (-0.5) / SOFTCAP)
    capped = jnp.where(allowed, SOFTCAP * bent, -1e30)
    weights = jnp.exp(capped - jnp.max(capped, axis=0, keepdims=True))
    return weights / jnp.sum(weights, axis=0, keepdims=True), bent


def row_of(ref, first, count):
    return jnp.concatenate([ref[first + i : first + i + 1, :] for i in range(count)], axis=1)


def level(pick):
    return jnp.where(pick == 0, 1.0, jnp.where(pick == 1, 0.5, 0.25)).astype(F32)


GELU_C = 0.7978845608028654
GELU_A = 0.044715


def gelu_pair(value):
    square = value * value
    bent = jnp.tanh(GELU_C * value * (1.0 + GELU_A * square))
    out = 0.5 * value * (1.0 + bent)
    slope = 0.5 * (1.0 + bent)
    slope += 0.5 * value * (1.0 - bent * bent) * (GELU_C * (1.0 + 3.0 * GELU_A * square))
    return out, slope


def front_kernel(
    width_pick,
    w_query,
    w_key,
    w_value,
    w_out_t,
    w_down_t,
    w_gate,
    w_up,
    gains,
    tokens_in,
    cot_in,
    segments,
    e_attn_out,
    h2_out,
    x1_out,
    query_out,
    kv_out,
    heads_out,
    h1_out,
    cot_out,
    mixed_in_out,
    grad_gate_out,
    grad_up_out,
    back_out,
    ffn_out,
    slope_ffn_out,
    slope_attn_out,
    small_out,
    peaks_out,
    early_out,
    wf_mine,
    wf_other,
    ea,
    ed,
    eg,
    eu,
    rows_a,
    cots,
    query,
    kv,
    heads,
    h2,
    x1,
    mixed_in,
    grad_gate,
    grad_up,
    slope_attn,
    small_src,
    small_land,
    small,
    peaks_src,
    peaks_land,
    peaks,
    peaks_peer,
    keys,
    extra_heads,
    extra_land,
    early_made,
    early_sem,
    partial,
    land,
    total,
    line_send,
    line_recv,
    local_sem,
    send_sem,
    recv_sem,
):
    here = Place()
    x, y, z, core = here.x, here.y, here.z, here.core
    rows, width = tokens_in.shape
    share, n_query = w_query.shape
    n_key = w_key.shape[1]
    n_in, n_attn = n_query + 2 * n_key, 2 * n_query + 2 * n_key
    half = w_gate.shape[1] // 2
    cuts = (0, 5 * half // 9, 7 * half // 9, half)
    weights = (w_down_t, w_gate, w_up)
    effective = (ed, eg, eu)
    tokens, h1 = rows_a.at[pl.ds(0, rows)], rows_a.at[pl.ds(rows, rows)]

    local_count = [0]

    def fetch(src, dst):
        copy = pltpu.make_async_copy(src, dst, local_sem.at[local_count[0]])
        local_count[0] += 1
        copy.start()
        return copy

    def slab(ref, sx, score, sy, first=0, part=share, cols=None):
        at = pl.ds(pl.multiple_of(here.slot(sx, score, sy) * share + first, 16), part)
        return ref.at[at] if cols is None else ref.at[at, cols]

    own_at = here.slot(x, core, y) * share
    attn_cols = [(w_query, 0), (w_key, n_query), (w_value, n_query + n_key), (w_out_t, n_in)]
    get_attn = [
        fetch(w, slab(ea, x, core, y, cols=pl.ds(at, w.shape[1]))) for w, at in attn_cols
    ]
    mine_cols = pl.ds(pl.multiple_of(core * half, half), half)
    their_cols = pl.ds(pl.multiple_of((1 - core) * half, half), half)
    part_cols = [pl.ds(part * half, half) for part in range(3)]
    get_ffn = [fetch(w.at[:, mine_cols], wf_mine.at[:, part_cols[i]]) for i, w in enumerate(weights)]
    get_tokens = fetch(tokens_in, tokens)
    get_cot = fetch(cot_in, cots.at[pl.ds(0, rows)])
    greet(here, [here.to_core, here.to_x, here.to_y, here.to_xy])
    mail = Mail(send_sem, recv_sem)

    half_share = share // 2

    def peak(block):
        return jnp.max(jnp.abs(block.astype(F32)), axis=0, keepdims=True)

    def set_out(first):
        ref = slab(ea, x, core, y, first, half_share)
        return [mail.send(ref, ref, here.to_x), mail.send(ref, ref, here.to_y)]

    for copy in get_attn:
        copy.wait()
    attn_moves = set_out(0)
    own_rows = pl.ds(pl.multiple_of(own_at, 32), share)
    attn_peak = peak(ea[own_rows, :])
    piece = small_src.shape[1]
    n_pieces = n_attn // piece
    small_src[...] = gains[...].astype(F32)
    for index in range(n_pieces):
        at = slice(index * piece, (index + 1) * piece)
        small_src[index : index + 1, :] = attn_peak[:, at]
    first = mail.send(small_src, small_land.at[0], here.to_core)
    swap = [
        mail.send(w.at[:, their_cols], wf_other.at[:, part_cols[i]], here.to_core)
        for i, w in enumerate(weights)
    ]
    own = slab(ea, x, core, y)
    ac = mail.send(own, own, here.to_core)
    cot_copy = mail.send(cot_in, cots.at[pl.ds(rows, rows)], here.to_core)
    first.wait_recv()

    def merge(mine, other):
        mine[0:8, :] = jnp.maximum(mine[0:8, :], other[0:8, :])
        mine[8:, :] = mine[8:, :] + other[8:, :]

    small[...] = small_src[...]
    merge(small, small_land.at[0])
    ring = (here.to_x, here.to_y, here.to_xy)
    small_send = [mail.send(small, small_land.at[1 + i], to) for i, to in enumerate(ring)]

    for copy in get_ffn:
        copy.wait()
    for copy in swap:
        copy.wait_recv()
    peaks_src[...] = jnp.zeros_like(peaks_src)
    for part in range(3):
        cols = slice(part * half, (part + 1) * half)
        both = jnp.maximum(peak(wf_mine[:, cols]), peak(wf_other[:, cols]))
        line_at = (part + 2) % 3
        peaks_src[line_at : line_at + 1, :] = both
    peaks_send = [mail.send(peaks_src, peaks_land.at[i], to) for i, to in enumerate(ring)]
    attn_moves += set_out(half_share)

    for copy in small_send:
        copy.wait_recv()
        mail.finish(copy)
    for index in (1, 2, 3):
        merge(small, small_land.at[index])
    outs = [fetch(small, small_out)]

    get_tokens.wait()
    gain_one = row_of(small, 8, width // piece)
    gain_two = row_of(small, 8 + width // piece, width // piece)

    @pl.loop(0, rows // 32)
    def _(index):
        at = pl.ds(mul(index, 32), 32)
        h1[at, :] = (forward_norm(tokens[at, :].astype(F32))[0] * gain_one).astype(BF16)


    def tangent(block, bound):
        return jnp.tanh(block.astype(F32) / bound)

    for copy in peaks_send:
        copy.wait_recv()
    peaks[...] = peaks_src[...]
    for index in range(3):
        peaks[...] = jnp.maximum(peaks[...], peaks_land[index])
    peer_copy = mail.send(peaks, peaks_peer, here.to_core)
    outs.append(fetch(peaks, peaks_out.at[:, mine_cols]))
    picks = (6, 4, 5)
    other_at = here.slot(x, 1 - core, y) * share
    for part in range(3):
        cols = slice(part * half, (part + 1) * half)
        line_at = (part + 2) % 3
        bound = peaks[line_at : line_at + 1, :] * level(width_pick[picks[part]])

        @pl.loop(0, share // 32)
        def _(index, cols=cols, bound=bound, part=part):
            at = pl.ds(mul(index, 32), 32)
            for weight, start in ((wf_mine, own_at), (wf_other, other_at)):
                to = pl.ds(pl.multiple_of(start + index * 32, 32), 32)
                bent = tangent(weight[at, cols], bound)
                effective[part][to, :] = (bound * bent).astype(BF16)
                weight[at, cols] = (1.0 - bent * bent).astype(BF16)

    outs.append(fetch(wf_mine, slope_ffn_out.at[core]))
    outs.append(fetch(wf_other, slope_ffn_out.at[1 - core]))

    for copy in attn_moves:
        copy.wait_recv()
    from_x = slab(ea, 1 - x, core, y)
    corner = slab(ea, 1 - x, core, y, 0, half_share)
    dy = mail.send(corner, corner, here.to_y)
    cx = mail.send(from_x, from_x, here.to_core)
    from_y = slab(ea, x, core, 1 - y)
    corner = slab(ea, x, core, 1 - y, half_share, half_share)
    dx = mail.send(corner, corner, here.to_x)
    cy = mail.send(from_y, from_y, here.to_core)

    splits = [pl.ds(a, b - a) for a, b in zip(cuts, cuts[1:])]
    moving, together = {}, {}

    def block_of(part, split, count):
        return effective[part].at[pl.ds(0, count * share), splits[split]]

    def move(part, split, pair, axis, ref, target):
        if (part, split) not in together:
            leaving, coming = block_of(part, split, 6), block_of(part, split, 4)
            together[part, split] = mail.group(leaving, coming, here.to_x)
        send_at, recv_at, _ = together[part, split]
        copy = mail.send(ref, ref, target, send_at, None if pair == axis else recv_at)
        if pair == axis:
            moving[part, split, pair] = copy

    def ship(part, split, axis, pairs=(0, 1)):
        target = here.to_x if axis == 0 else here.to_y
        for pair in pairs:
            ref = slab(effective[part], x, pair, y, cols=splits[split])
            move(part, split, pair, axis, ref, target)

    def pass_on(part, split, pair):
        moving[part, split, pair].wait_recv()
        at = (1 - x, y) if pair == 0 else (x, 1 - y)
        ref = slab(effective[part], at[0], pair, at[1], cols=splits[split])
        move(part, split, pair, 2, ref, here.to_y if pair == 0 else here.to_x)

    def arrived(part, split):
        together[part, split][2].wait_recv()

    ship(0, 0, 0)
    ship(0, 0, 1, (0,))

    flat_peak = row_of(small, 0, n_pieces)
    bound_attn = jnp.concatenate(
        [
            flat_peak[:, :n_query] * level(width_pick[0]),
            flat_peak[:, n_query : n_query + n_key] * level(width_pick[1]),
            flat_peak[:, n_query + n_key : n_in] * level(width_pick[2]),
            flat_peak[:, n_in:] * level(width_pick[3]),
        ],
        axis=1,
    )

    def soften(sx, score, sy, slopes=False):
        base = here.slot(sx, score, sy) * share

        @pl.loop(0, share // 32)
        def _(index):
            at = pl.ds(mul(index, 32), 32)
            to = pl.ds(pl.multiple_of(base + index * 32, 32), 32)
            bent = tangent(ea[to, :], bound_attn)
            ea[to, :] = (bound_attn * bent).astype(BF16)
            if slopes:
                slope_attn[at, :] = (1.0 - bent * bent).astype(BF16)

    for copy in attn_moves + [ac]:
        mail.finish(copy)
    soften(x, core, y, True)
    outs.append(fetch(slope_attn, slope_attn_out))
    ac.wait_recv()
    soften(x, 1 - core, y)
    cx.wait_recv()
    soften(1 - x, 1 - core, y)
    cy.wait_recv()
    soften(x, 1 - core, 1 - y)
    dy.wait_recv()
    dx.wait_recv()
    across = slab(ea, 1 - x, core, 1 - y)
    cxy = mail.send(across, across, here.to_core)
    for copy in (dy, cx, dx, cy):
        mail.finish(copy)
    soften(1 - x, core, y)
    soften(x, core, 1 - y)
    cxy.wait_recv()
    mail.finish(cxy)
    soften(1 - x, core, 1 - y)
    soften(1 - x, 1 - core, 1 - y)
    e_attn_copy = fetch(ea, e_attn_out)

    tile = 256

    @pl.loop(0, n_query // tile)
    def _(index):
        cols = pl.ds(mul(index, tile), tile)
        query[:rows, cols] = natural(h1[...], ea[:, cols]).astype(BF16)

    @pl.loop(0, 2 * n_key // tile)
    def _(index):
        cols = pl.ds(mul(index, tile), tile)
        source = pl.ds(pl.multiple_of(n_query + index * tile, tile), tile)
        kv[:rows, cols] = natural(h1[...], ea[:, source]).astype(BF16)

    ours, theirs = pl.ds(edge(y, rows), EXTRA), pl.ds(rows, EXTRA)
    row_copies = [
        mail.send(ref.at[ours], ref.at[theirs], here.to_y) for ref in (query, kv)
    ]
    for part in (1, 2):
        ship(part, 0, 0)
    h1_copy = fetch(h1, h1_out)
    number_rows(segments, y, keys)
    for copy in row_copies:
        copy.wait_recv()

    block, n_heads = 128, n_query // HD

    def attend(at, allowed):
        stack = jnp.concatenate([query[at, i * HD : (i + 1) * HD] for i in range(n_heads)], axis=0)
        probs, _ = soft_probs(stack, kv, allowed)
        return inner_rows(probs.astype(BF16), kv[:, HD:]).astype(BF16)

    out = attend(theirs, extra_visible(keys, y, n_heads))
    for i in range(n_heads):
        extra_heads[:, i * HD : (i + 1) * HD] = out[i * EXTRA : (i + 1) * EXTRA]
    extra_copy = mail.send(extra_heads, extra_land, here.to_y)
    ship(0, 0, 1, (1,))
    for part in (1, 2):
        ship(part, 0, 1)

    @pl.loop(0, rows // block)
    def _(index):
        at = pl.ds(mul(index, block), block)
        start = pl.multiple_of(y * rows + index * block, block)
        numbers = segments[:, pl.ds(start, block)].astype(F32)
        position = start + lax.broadcasted_iota(jnp.int32, (1, block), 1)
        allowed = visible(keys, beside(numbers, n_heads), beside(position, n_heads), y)
        out = attend(at, allowed)
        for i in range(n_heads):
            heads[at, i * HD : (i + 1) * HD] = out[i * block : (i + 1) * block]

    extra_copy.wait_recv()
    middle = (lax.broadcasted_iota(jnp.int32, (EXTRA, 1), 0) == 0) & (y == 1)
    heads[:EXTRA, :] = jnp.where(middle, extra_land[...], heads[:EXTRA, :])

    @pl.loop(0, width // tile)
    def _(index):
        cols = pl.ds(mul(index, tile), tile)
        partial[:, cols] = against(heads[...], ea[cols, n_in:]).astype(BF16)

    outs += [fetch(query, query_out), fetch(kv, kv_out), fetch(heads, heads_out)]

    tall = 512

    def back_into_mixed(split):
        @pl.loop(0, 2 * rows // tall)
        def _(index):
            at = pl.ds(mul(index, tall), tall)
            grad_gate[at, splits[split]] = natural(cots[at, :], ed[:, splits[split]]).astype(BF16)

    def gated(split):
        cols, high = splits[split], 512 if split else 256

        @pl.loop(0, 2 * rows // high)
        def _(index):
            at = pl.ds(mul(index, high), high)
            gate = natural(h2[at, :], eg[:, cols])
            upper = natural(h2[at, :], eu[:, cols])
            value, slope = gelu_pair(gate)
            back = grad_gate[at, cols].astype(F32)
            mixed_in[at, cols] = (value * upper).astype(BF16)
            grad_gate[at, cols] = (back * upper * slope).astype(BF16)
            grad_up[at, cols] = (back * value).astype(BF16)

    def to_width(target, pairs, split, then=None):
        wide = width // 3

        def piece(at):
            for column in range(3):
                cols = slice(column * wide, (column + 1) * wide)
                added = against(pairs[0][0][at, splits[split]], pairs[0][1][cols, splits[split]])
                for left, right in pairs[1:]:
                    added += against(left[at, splits[split]], right[cols, splits[split]])
                if split:
                    added += target[column][at, :].astype(F32)
                target[column][at, :] = added.astype(BF16)

        if then is None:

            @pl.loop(0, 2 * rows // tall)
            def _(index):
                piece(pl.ds(mul(index, tall), tall))

        else:
            for first in range(0, 2 * rows, tall):
                piece(pl.ds(first, tall))
                then(pl.ds(first, tall))

    def transform(sub, spot, summed):
        at = pl.ds(pl.multiple_of(z * (rows // 4) + sub * line.part, line.part), line.part)
        resid = tokens[at, :].astype(F32) + summed
        x1[spot, :] = resid
        return (forward_norm(resid)[0] * gain_two).astype(BF16)

    own_half, other_half = (h2.at[pl.ds(first, rows)] for first in (0, rows))
    give_send, give_recv, all_given = mail.group(own_half, other_half, here.to_core)

    def give(sub):
        for chunk in range(4):
            first = chunk * (rows // 4) + sub * line.part
            src, dst = (h2.at[pl.ds(first + at, line.part)] for at in (0, rows))
            mail.send(src, dst, here.to_core, give_send, give_recv)

    line = Line(here, partial, h2, land, total, (line_send, line_recv), transform, give=give, subs=FRONT_SUBS)
    width_blocks = [pl.ds(i * (width // 3), width // 3) for i in range(3)]
    back_part = [rows_a.at[:, cols] for cols in width_blocks]
    spare = ((0, 0), (0, 1), (1, 0))
    ffn_part = [
        ea.at[pl.ds(i * 2 * rows, 2 * rows), pl.ds(j * (width // 3), width // 3)] for i, j in spare
    ]
    upward = ((grad_gate, eg), (grad_up, eu))
    downward = ((mixed_in, ed),)
    for tick in line.ticks():
        if tick == 1:
            pass_on(0, 0, 0)
            pass_on(0, 0, 1)
        if tick == 2:
            pass_on(1, 0, 0)
        if tick == 3:
            get_cot.wait()
            cot_copy.wait_recv()
            cot_keep = fetch(cots.at[pl.ds(rows, rows)], cot_out)
        if tick == 4:
            pass_on(1, 0, 1)
            pass_on(2, 0, 0)
        if tick == 5:
            pass_on(2, 0, 1)
            for part in range(3):
                for axis in (0, 1):
                    ship(part, 1, axis)
        if tick == 8:
            for axis in (0, 1):
                ship(0, 2, axis)
        if tick == 6:
            arrived(0, 0)
            back_into_mixed(0)
    line.close()
    outs.append(fetch(x1, x1_out))
    arrived(1, 0)
    arrived(2, 0)
    all_given.wait_recv()
    outs.append(fetch(h2, h2_out))
    gated(0)
    for part in range(3):
        for turn in (0, 1):
            pass_on(part, 1, turn)
    for part in (1, 2):
        for axis in (0, 1):
            ship(part, 2, axis)
    h1_copy.wait()
    to_width(back_part, upward, 0)
    arrived(0, 1)
    back_into_mixed(1)
    arrived(1, 1)
    arrived(2, 1)
    gated(1)
    e_attn_copy.wait()
    to_width(ffn_part, downward, 0)
    to_width(back_part, upward, 1)
    to_width(ffn_part, downward, 1)
    for part in range(3):
        for turn in (0, 1):
            pass_on(part, 2, turn)
    late = cuts[2]

    def early_copy(index):
        at = pl.ds(mul(index, tile), tile)
        return pltpu.make_async_copy(early_made, early_out.at[at], early_sem)

    @pl.loop(0, width // tile)
    def _(index):
        made = inner_rows(h2[:, pl.ds(mul(index, tile), tile)], grad_gate[:, :late]).astype(BF16)

        @pl.when(index > 0)
        def _():
            early_copy(index - 1).wait()

        early_made[...] = made
        early_copy(index).start()

    early_copy(width // tile - 1).wait()
    arrived(0, 2)
    back_into_mixed(2)
    arrived(1, 2)
    arrived(2, 2)
    gated(2)
    outs += [
        fetch(mixed_in, mixed_in_out),
        fetch(grad_gate, grad_gate_out),
        fetch(grad_up, grad_up_out),
    ]
    to_width(back_part, upward, 2, lambda at: outs.append(fetch(rows_a.at[at], back_out.at[at])))

    def ffn_leaves(at):
        for i in range(3):
            outs.append(fetch(ffn_part[i].at[at], ffn_out.at[at, width_blocks[i]]))

    to_width(ffn_part, downward, 2, ffn_leaves)
    cot_keep.wait()
    peer_copy.wait_recv()
    outs.append(fetch(peaks_peer, peaks_out.at[:, their_cols]))
    mail.close()
    for copy in outs:
        copy.wait()


def front(width_pick, weights, gains, tokens, cotangent, segments):
    rows, width = tokens.shape
    share, n_query = weights[0].shape
    n_kv = 2 * weights[1].shape[1]
    n_attn = 2 * n_query + n_kv
    hidden = weights[-1].shape[1]
    half = hidden // 2
    shapes = [
        ((width, n_attn), BF16),
        ((2 * rows, width), BF16),
        ((rows // 4, width), F32),
        ((rows + EXTRA, n_query), BF16),
        ((rows + EXTRA, n_kv), BF16),
        ((rows, n_query), BF16),
        ((rows, width), BF16),
        ((rows, width), BF16),
        ((2 * rows, half), BF16),
        ((2 * rows, half), BF16),
        ((2 * rows, half), BF16),
        ((2 * rows, width), BF16),
        ((2 * rows, width), BF16),
        ((2, share, 3 * half), BF16),
        ((share, n_attn), BF16),
        ((32, 256), F32),
        ((8, hidden), F32),
        ((width, 7 * half // 9), BF16),
    ]
    in_vmem = pl.BlockSpec(memory_space=pltpu.VMEM)
    in_smem = pl.BlockSpec(memory_space=pltpu.SMEM)
    anywhere = pl.BlockSpec(memory_space=pl.ANY)
    scratch = [
        pltpu.VMEM((share, 3 * half), BF16),
        pltpu.VMEM((share, 3 * half), BF16),
        pltpu.VMEM((width, n_attn), BF16),
        pltpu.VMEM((width, half), BF16),
        pltpu.VMEM((width, half), BF16),
        pltpu.VMEM((width, half), BF16),
        pltpu.VMEM((2 * rows, width), BF16),
        pltpu.VMEM((2 * rows, width), BF16),
        pltpu.VMEM((rows + EXTRA, n_query), BF16),
        pltpu.VMEM((rows + EXTRA, n_kv), BF16),
        pltpu.VMEM((rows, n_query), BF16),
        pltpu.VMEM((2 * rows, width), BF16),
        pltpu.VMEM((rows // 4, width), F32),
        pltpu.VMEM((2 * rows, half), BF16),
        pltpu.VMEM((2 * rows, half), BF16),
        pltpu.VMEM((2 * rows, half), BF16),
        pltpu.VMEM((share, n_attn), BF16),
        pltpu.VMEM((32, 256), F32),
        pltpu.VMEM((4, 32, 256), F32),
        pltpu.VMEM((32, 256), F32),
        pltpu.VMEM((8, half), F32),
        pltpu.VMEM((3, 8, half), F32),
        pltpu.VMEM((8, half), F32),
        pltpu.VMEM((8, half), F32),
        pltpu.VMEM((rows + EXTRA, 128), F32),
        pltpu.VMEM((EXTRA, n_query), BF16),
        pltpu.VMEM((EXTRA, n_query), BF16),
        pltpu.VMEM((256, 7 * half // 9), BF16),
        pltpu.SemaphoreType.DMA,
        *line_scratch(rows, width, FRONT_SUBS),
        pltpu.SemaphoreType.DMA((34,)),
        pltpu.SemaphoreType.DMA((35,)),
        pltpu.SemaphoreType.DMA((53,)),
    ]
    return pl.pallas_call(
        front_kernel,
        out_shape=[jax.ShapeDtypeStruct(s, d) for s, d in shapes],
        in_specs=[in_smem] + [anywhere] * 7 + [in_vmem, anywhere, anywhere, in_vmem],
        out_specs=[anywhere] * len(shapes),
        scratch_shapes=scratch,
        compiler_params=pltpu.CompilerParams(
            collective_id=0, has_side_effects=True, vmem_limit_bytes=VMEM_BYTES
        ),
        cost_estimate=pl.CostEstimate(
            flops=36 * 10**9, bytes_accessed=90 * 10**6, transcendentals=8 * 10**6
        ),
        name="front",
    )(width_pick, *weights, gains, tokens, cotangent, segments)


OUTPUT_PLAN = (7, 8, 10, 11, 12, 14, 15, 17, 18, 19, 20, 21, 22, 23)


def back_kernel(
    back_in,
    ffn_in,
    mixed_in,
    grad_gate,
    grad_up,
    h2_in,
    cot_other,
    early_in,
    x1_in,
    small,
    e_attn,
    query_in,
    kv_in,
    heads_in,
    h1_in,
    tokens_in,
    cot_in,
    segments,
    slope_ffn,
    slope_attn_in,
    out_down,
    out_gate,
    out_up,
    out_attn,
    mixed_out,
    tokens_out,
    gains_out,
    de_down,
    de_gate,
    de_up,
    stage_a,
    stage_b,
    land_a,
    land_b,
    last_a,
    last_b,
    slopes,
    partial,
    partial_ffn,
    grad_resid_b,
    own_ffn,
    own_tokens,
    land,
    land_ffn,
    total,
    ea,
    core_land,
    attn_a,
    attn_b,
    attn_last_a,
    attn_last_b,
    query,
    kv,
    heads,
    h1,
    keys,
    grad_in,
    grad_kv,
    edge_send,
    edge_land,
    row_send,
    row_land,
    x1,
    grad_resid,
    token_chunk,
    cot_chunk,
    gain_part,
    gain_sum,
    gain_land,
    line_send,
    line_recv,
    ffn_send,
    ffn_recv,
    work_sem,
    local_sem,
    send_sem,
    recv_sem,
):
    here = Place()
    x, y, z, core = here.x, here.y, here.z, here.core
    rows, width = tokens_in.shape
    share, half = last_a.shape[1], last_a.shape[2]
    n_query, n_attn = query.shape[1], ea.shape[1]
    n_in = n_attn - n_query
    de_ffn = (de_down, de_gate, de_up)
    out_ffn = (out_down, out_gate, out_up)
    chunk_rows = pl.ds(pl.multiple_of(z * (rows // 4), rows // 4), rows // 4)
    mine_cols = pl.ds(pl.multiple_of(core * half, half), half)
    tile = 256

    local_count = [0]

    def fetch(src, dst):
        copy = pltpu.make_async_copy(src, dst, local_sem.at[local_count[0]])
        local_count[0] += 1
        copy.start()
        return copy

    order = (1, 2, 0)
    slot_of = {part: i % 2 for i, part in enumerate(order)}

    late = early_in.shape[1]
    blocks = {0: [(de_down, 0, half)], 2: [(de_up, 0, half)]}
    blocks[1] = [(early_in, 0, late), (de_gate, late, half - late)]

    def lanes(ref, block):
        return ref if ref.shape[-1] == block[2] else ref.at[:, pl.ds(block[1], block[2])]

    def source(block, at):
        return lanes(block[0].at[at], block)

    def stage(part):
        a_rows = pl.ds(pl.multiple_of(here.slot(x, 0, 0) * share, share), 2 * share)
        slot = slot_of[part]
        copies = []
        for block in blocks[part]:
            copies.append(fetch(source(block, a_rows), lanes(stage_a.at[slot], block)))
            for i in (0, 1):
                b_rows = pl.ds(mul(here.slot(i, 1, y), share), share)
                copies.append(fetch(source(block, b_rows), lanes(stage_b.at[slot, i], block)))
        return copies

    sides = (mixed_in, grad_gate, grad_up)
    side_rows = [pl.ds(0, 2 * rows), pl.ds(2 * rows, 2 * rows), pl.ds(0, 2 * rows)]
    side_at = {part: ea.at[side_rows[i], pl.ds(0, half)] for i, part in enumerate(order)}
    strip_cols = pl.ds(half, tile)
    made_cols = {part: pl.ds(blocks[part][-1][1], blocks[part][-1][2]) for part in order}

    def strip_copies(part, index, slot):
        cols = pl.ds(mul(index, tile), tile)
        to = [
            ea.at[pl.ds(pl.multiple_of(slot * 2 * rows + i * rows, rows), rows), strip_cols]
            for i in (0, 1)
        ]
        if part:
            src = [h2_in.at[pl.ds(i * rows, rows), cols] for i in (0, 1)]
        else:
            src = [cot_in.at[:, cols], cot_other.at[:, cols]]
        return [
            pltpu.make_async_copy(src[i], to[i], work_sem.at[slot, i]) for i in (0, 1)
        ]

    def result_copy(part, index):
        at = pl.ds(mul(index, tile), tile)
        cols = made_cols[part]
        slot = lax.rem(index, 2)
        made = slopes.at[slot, pl.ds(0, tile), cols]
        return pltpu.make_async_copy(made, de_ffn[part].at[at, cols], work_sem.at[2, slot])

    sides_here = {order[0]: fetch(sides[order[0]], side_at[order[0]])}
    for copy in strip_copies(order[0], 0, 0):
        copy.start()
    get_x1 = fetch(x1_in, x1)
    get_cot = fetch(cot_in.at[chunk_rows], cot_chunk)
    get_tokens = fetch(tokens_in.at[chunk_rows], token_chunk)
    get_partial = fetch(back_in.at[pl.ds(0, rows)], partial)
    sides_here[order[1]] = fetch(sides[order[1]], side_at[order[1]])
    far_target = (x * 2 + core, y, lax.rem(z + 2, 4))
    near_target = (x * 2 + core, y, z + 1 - 2 * lax.rem(z, 2))
    plane = [here.to_core, here.to_x, here.to_y, here.to_xy]
    plane += [(2 * (1 - x) + 1 - core, y, z), (2 * x + 1 - core, 1 - y, z)]
    plane += [(2 * (1 - x) + 1 - core, 1 - y, z)]
    greet(here, [*plane, far_target])
    mail = Mail(send_sem, recv_sem)
    their_half = pl.ds(rows, rows)
    chunks = [jnp.where(z < 2, 3 - i, i) * (rows // 4) for i in range(4)]
    chunks = [pl.multiple_of(first, rows // 4) for first in chunks]
    back_copies = [
        mail.send(
            back_in.at[pl.ds(rows + first, rows // 4)],
            partial_ffn.at[pl.ds(first, rows // 4)],
            here.to_core,
        )
        for first in chunks
    ]
    ffn_copy = mail.send(ffn_in.at[their_half], h1, here.to_core)

    n_strips = width // tile

    def strips(part, first, last):
        if first == 0:
            sides_here[part].wait()

        @pl.loop(first, last)
        def _(index):
            slot = lax.rem(index, 2)
            for copy in strip_copies(part, index, slot):
                copy.wait()

            @pl.when(index + 1 < n_strips)
            def _():
                for copy in strip_copies(part, index + 1, 1 - slot):
                    copy.start()

            left = ea[pl.ds(pl.multiple_of(slot * 2 * rows, rows), 2 * rows), strip_cols]
            made = inner_rows(left, side_at[part][:, made_cols[part]]).astype(BF16)

            @pl.when(index > 1)
            def _():
                result_copy(part, index - 2).wait()

            slopes[slot, :tile, made_cols[part]] = made
            result_copy(part, index).start()

        if last == n_strips:
            for index in (n_strips - 2, n_strips - 1):
                result_copy(part, jnp.int32(index)).wait()
            at = order.index(part)
            if at + 1 < 3:
                for copy in strip_copies(order[at + 1], 0, 0):
                    copy.start()
            if at == 0:
                sides_here[order[2]] = fetch(sides[order[2]], side_at[order[2]])
            if at < 2:
                staged[part] = stage(part)

    staged = {}
    slope_here = {}

    def get_slopes(part):
        cols = pl.ds(part * half, half)
        slope_here[part] = fetch(slope_ffn.at[:, :, cols], slopes)

    first_hop, groups = {}, {}
    second_hop = {}
    ending = []

    def ship(part, i, block, axis):
        if axis == 0:
            at = pl.ds(mul(here.slot(1 - x, 0, i), share), share)
            to, target = land_a.at[part, pl.ds(i * share, share)], here.to_x
        else:
            at = pl.ds(mul(here.slot(i, 1, 1 - y), share), share)
            to, target = land_b.at[part, i], here.to_y
        if (part, block[1]) not in groups:
            four = lanes(de_ffn[part].at[pl.ds(0, 4 * share)], block)
            groups[part, block[1]] = mail.group(four, four, here.to_x)
            first_hop.setdefault(part, []).append(groups[part, block[1]][2])
        mail.send(source(block, at), lanes(to, block), target, *groups[part, block[1]][:2])

    def ship_all(part, i, axes=(0, 1)):
        for block in blocks[part]:
            for axis in axes:
                ship(part, i, block, axis)

    step = 32

    def relay(part):
        slot = slot_of[part]
        for copy in staged[part]:
            copy.wait()
        for copy in first_hop[part]:
            copy.wait_recv()
        base = (1 - y) * share

        @pl.loop(0, share // step)
        def _(index):
            at = pl.ds(pl.multiple_of(base + index * step, step), step)
            mine = stage_a[slot, at, :].astype(F32) + land_a[part, at, :].astype(F32)
            stage_a[slot, at, :] = mine.astype(BF16)
            at = pl.ds(mul(index, step), step)
            mine = stage_b[slot, 1 - x, at, :].astype(F32) + land_b[part, 1 - x, at, :].astype(F32)
            stage_b[slot, 1 - x, at, :] = mine.astype(BF16)

        a_src = stage_a.at[slot, pl.ds(pl.multiple_of(base, share), share)]
        second_hop[part] = (
            mail.send(a_src, last_a.at[part], here.to_y),
            mail.send(stage_b.at[slot, 1 - x], last_b.at[part], here.to_x),
        )

    def settle(part):
        slot = slot_of[part]
        slope_here[part].wait()
        for copy in second_hop[part]:
            copy.wait_recv()
        base = y * share

        @pl.loop(0, share // step)
        def _(index):
            flat = pl.ds(mul(index, step), step)
            at = pl.ds(pl.multiple_of(base + index * step, step), step)
            mine = stage_a[slot, at, :].astype(F32) + land_a[part, at, :].astype(F32)
            mine = mine + last_a[part, flat, :].astype(F32)
            stage_a[slot, at, :] = (mine * slopes[0, flat, :].astype(F32)).astype(BF16)
            mine = stage_b[slot, x, flat, :].astype(F32) + land_b[part, x, flat, :].astype(F32)
            mine = mine + last_b[part, flat, :].astype(F32)
            stage_b[slot, x, flat, :] = (mine * slopes[1, flat, :].astype(F32)).astype(BF16)

        a_ref = stage_a.at[slot, pl.ds(pl.multiple_of(base, share), share)]
        b_ref = stage_b.at[slot, x]
        out = out_ffn[part].at[:, mine_cols]
        give_b = mail.make(b_ref, out, here.to_core)
        give_a = mail.make(a_ref, out, here.to_core, mail.n_send - 1, mail.n_recv - 1)
        keep_a = pltpu.make_async_copy(a_ref, out, local_sem.at[local_count[0]])
        keep_b = pltpu.make_async_copy(b_ref, out, local_sem.at[local_count[0]])
        local_count[0] += 1

        @pl.when(core == 0)
        def _():
            keep_a.start()
            give_b.start()

        @pl.when(core == 1)
        def _():
            keep_b.start()
            give_a.start()

        ending.append((keep_a, give_b))
        finished[part] = ending[-1]

    finished = {}

    def restage(part, earlier):
        keep, give = finished[earlier]
        keep.wait()
        for copy in (give, *second_hop[earlier]):
            mail.finish(copy)
        staged[part] = stage(part)

    count = width // small.shape[1]
    gain_one = row_of(small, 8, count)
    gain_two = row_of(small, 8 + count, count)

    gain_part[...] = jnp.zeros_like(gain_part)

    def into_resid(sub, spot, summed):
        normed, inverse = forward_norm(x1[spot, :])
        gain_part[1:2, :] += jnp.sum(summed * normed, axis=0, keepdims=True)
        grad = cot_chunk[spot, :].astype(F32) + backward_norm(summed * gain_two, normed, inverse)
        grad_resid[spot, :] = grad
        return grad.astype(BF16)

    def into_mixed(sub, spot, summed):
        return (x1[spot, :] + summed).astype(BF16)

    def into_tokens(sub, spot, summed):
        normed, inverse = forward_norm(token_chunk[spot, :].astype(F32))
        gain_part[0:1, :] += jnp.sum(summed * normed, axis=0, keepdims=True)
        grad = grad_resid[spot, :] + backward_norm(summed * gain_one, normed, inverse)
        return grad.astype(BF16)

    line = Line(here, partial, grad_resid_b, land, total, (line_send, line_recv), into_resid, subs=BACK_SUBS)
    ffn_line = Line(
        here, partial_ffn, mixed_out, land_ffn, total, (ffn_send, ffn_recv), into_mixed, own_ffn, subs=BACK_SUBS
    )
    tok_line = Line(
        here, partial, tokens_out, land, total, (line_send, line_recv), into_tokens, own_tokens, subs=BACK_SUBS
    )

    for i in (0, 1):
        for axis in (0, 1):
            ship(1, i, blocks[1][0], axis)
    for copy in (get_partial, get_x1, get_cot, get_tokens):
        copy.wait()

    def join(target, came, first=0, count=rows):
        @pl.loop(0, count // step)
        def _(index):
            at = pl.ds(pl.multiple_of(first + index * step, step), step)
            target[at, :] = (target[at, :].astype(F32) + came[at, :].astype(F32)).astype(BF16)

    def join_chunk(number):
        back_copies[number].wait_recv()
        join(partial, partial_ffn, chunks[number], rows // 4)

    join_chunk(0)

    quarter, n_heads = 32, n_query // HD
    block = 4 * quarter
    number_rows(segments, y, keys)
    grad_kv[...] = jnp.zeros_like(grad_kv)

    def stacked(value):
        return jnp.concatenate([value[:, i * HD : (i + 1) * HD] for i in range(n_heads)], axis=0)

    def back_through(query_b, grad_o, allowed):
        probs, bent = soft_probs(query_b, kv, allowed)
        grad_probs = against(kv[:, HD:], grad_o)
        row_dot = jnp.sum(probs * grad_probs, axis=0, keepdims=True)
        grad_raw = probs * (grad_probs - row_dot) * (1.0 - bent * bent) * HD ** (-0.5)
        grad_raw = grad_raw.astype(BF16)
        grad_kv[:, :HD] += natural(grad_raw, query_b)
        grad_kv[:, HD:] += natural(probs.astype(BF16), grad_o)
        return inner_rows(grad_raw, kv[:, :HD]).astype(BF16)

    def attend_back(sub):
        firsts = [j * (rows // 4) + sub * quarter for j in range(4)]
        spots = [slice(at, at + quarter) for at in firsts]

        def take(ref):
            return jnp.concatenate([ref[spot, :] for spot in spots], axis=0)

        index = lax.broadcasted_iota(jnp.int32, (1, block), 1)
        chunk = sum((index >= j * quarter).astype(jnp.int32) for j in (1, 2, 3))
        position = y * rows + index + chunk * (rows // 4 - quarter) + sub * quarter
        numbers = jnp.transpose(take(keys))[0:1, :]
        allowed = visible(keys, beside(numbers, n_heads), beside(position, n_heads), y)
        grad_o = natural(take(grad_resid_b), ea[:, n_in:]).astype(BF16)
        if sub == 0:
            edge_send[...] = grad_o[:EXTRA]
            edge_copies.append(mail.send(edge_send, edge_land, here.to_y))
            theirs = (lax.broadcasted_iota(jnp.int32, (block, 1), 0) == 0) & (y == 1)
            grad_o = jnp.where(theirs, jnp.zeros_like(grad_o), grad_o)
        grad_q = back_through(stacked(take(query)), stacked(grad_o), allowed)
        for i in range(n_heads):
            for j, spot in enumerate(spots):
                at = i * block + j * quarter
                grad_in[spot, i * HD : (i + 1) * HD] = grad_q[at : at + quarter]

    edge_copies = []

    def edge_back():
        edge_copies[0].wait_recv()
        ours = (lax.broadcasted_iota(jnp.int32, (EXTRA, 1), 0) == 0) & (y == 0)
        grad_o = jnp.where(ours, edge_land[...], jnp.zeros_like(edge_land))
        allowed = extra_visible(keys, y, n_heads)
        grad_q = back_through(stacked(query[rows:, :]), stacked(grad_o), allowed)
        for i in range(n_heads):
            row_send[:, i * HD : (i + 1) * HD] = grad_q[i * EXTRA : (i + 1) * EXTRA]
        row_send[:, n_query:] = grad_kv[rows:, :].astype(BF16)

    ffn_ticks = ffn_line.ticks()
    plan, count = list(OUTPUT_PLAN), itertools.count(2)

    def output_wave(place):
        while plan and plan[0] <= place:
            plan.pop(0)
            next(ffn_ticks, None)

    later = []
    for tick in line.ticks():
        if tick == 0:
            join_chunk(1)
        if tick == 1:
            join_chunk(2)
            join_chunk(3)
            get_ffn = fetch(ffn_in.at[pl.ds(0, rows)], partial_ffn)
            strips(1, 0, n_strips // 2)
        if tick == 2:
            strips(1, n_strips // 2, n_strips)
            for i in (0, 1):
                for axis in (0, 1):
                    ship(1, i, blocks[1][1], axis)
        if tick in (3, 4, 5):
            strips(2, 3 * tick - 9, 3 * tick - 6)
        if tick == 5:
            ship_all(2, 0)
            ship_all(2, 1)
        if tick in (6, 7):
            strips(0, 5 * tick - 30, min(5 * tick - 25, n_strips))
        if tick == 5:
            get_ffn.wait()
            ffn_copy.wait_recv()
            join(partial_ffn, h1)
            get_h1 = fetch(h1_in, h1)
        if tick == 7:
            later = [
                fetch(e_attn, ea),
                fetch(query_in, query),
                fetch(kv_in, kv),
                fetch(heads_in, heads),
            ]
        output_wave(tick)
        if tick == 9:
            get_slopes(1)
            relay(1)
        if tick == 11:
            ship_all(0, 0, (0,))
        if tick == 8:
            for copy in later:
                copy.wait()
        if tick in (8, 10, 12, 13):
            attend_back((8, 10, 12, 13).index(tick))
    output_wave(14)
    line.close()
    edge_back()
    row_copy = mail.send(row_send, row_land, here.to_y)
    ship_all(0, 0, (1,))
    ship_all(0, 1)
    output_wave(15)
    settle(1)
    get_slopes(2)
    restage(0, 1)
    row_copy.wait_recv()
    at = pl.ds(edge(y, rows), EXTRA)
    grad_in[at, :n_query] = (grad_in[at, :n_query].astype(F32) + row_land[:, :n_query].astype(F32)).astype(BF16)
    grad_kv[at, :] += row_land[:, n_query:].astype(F32)
    grad_in[:, n_query:] = grad_kv[:rows, :].astype(BF16)

    @pl.loop(0, width // tile)
    def _(index):
        cols = pl.ds(mul(index, tile), tile)
        partial[:, cols] = against(grad_in[...], ea[cols, :n_in]).astype(BF16)

    tok_ticks = tok_line.ticks()
    next(tok_ticks, None)
    output_wave(17)

    @pl.loop(0, width // tile)
    def _(index):
        cols = pl.ds(mul(index, tile), tile)
        ea[cols, n_in:] = inner_rows(grad_resid_b[:, cols], heads[...]).astype(BF16)

    next(tok_ticks, None)
    output_wave(18)
    relay(2)
    get_h1.wait()

    @pl.loop(0, width // tile)
    def _(index):
        cols = pl.ds(mul(index, tile), tile)
        ea[cols, :n_in] = inner_rows(h1[:, cols], grad_in[...]).astype(BF16)

    def pair_rows(sx, score):
        return pl.ds(pl.multiple_of(here.slot(sx, score, 0) * share, 2 * share), 2 * share)

    core_copies = [
        mail.send(ea.at[pair_rows(i, 1 - core)], core_land.at[i], here.to_core) for i in (0, 1)
    ]
    for _ in range(2):
        next(tok_ticks, None)
        output_wave(17 + next(count))
    for copy in core_copies:
        copy.wait_recv()

    @pl.loop(0, 2 * share // step)
    def _(index):
        for i in (0, 1):
            at = pl.ds(
                pl.multiple_of(here.slot(i, core, 0) * share + index * step, step), step
            )
            flat = pl.ds(mul(index, step), step)
            ea[at, :] = (ea[at, :].astype(F32) + core_land[i, flat, :].astype(F32)).astype(BF16)

    slope_attn = core_land.at[0, pl.ds(0, share)]
    get_slope_attn = fetch(slope_attn_in, slope_attn)
    cut = attn_a.shape[1]
    left, right = pl.ds(0, cut), pl.ds(cut, n_attn - cut)

    def one_rows(sx, sy):
        return pl.ds(pl.multiple_of(here.slot(sx, core, sy) * share, share), share)

    attn_first = [mail.send(ea.at[pair_rows(1 - x, core), left], attn_a, here.to_x)]
    for i in (0, 1):
        attn_first.append(mail.send(ea.at[one_rows(i, 1 - y), right], attn_b.at[i], here.to_y))
    for _ in range(2):
        next(tok_ticks, None)
        output_wave(17 + next(count))
    relay(0)
    settle(2)
    get_slopes(0)
    for _ in range(3):
        next(tok_ticks, None)
        output_wave(17 + next(count))

    def gain_steps():
        rounds = (plane, [near_target], [far_target])
        mine, at = gain_part, 0
        for number, targets in enumerate(rounds):
            places = gain_land.at[pl.ds(at, len(targets))]
            send_at, recv_at, came = mail.group(places, places, here.to_core)
            for i, target in enumerate(targets):
                mail.send(mine, gain_land.at[at + i], target, send_at, recv_at)
            yield
            came.wait_recv()
            added = mine[...]
            for i in range(len(targets)):
                added = added + gain_land[at + i]
            gain_sum[number] = added
            mine, at = gain_sum.at[number], at + len(targets)

    gain_waves = gain_steps()
    for copy in attn_first:
        copy.wait_recv()

    @pl.loop(0, share // step)
    def _(index):
        flat = pl.ds(mul(index, step), step)
        at = pl.ds(pl.multiple_of(here.slot(x, core, 1 - y) * share + index * step, step), step)
        came = pl.ds(pl.multiple_of((1 - y) * share + index * step, step), step)
        ea[at, left] = (ea[at, left].astype(F32) + attn_a[came, :].astype(F32)).astype(BF16)
        at = pl.ds(pl.multiple_of(here.slot(1 - x, core, y) * share + index * step, step), step)
        ea[at, right] = (
            ea[at, right].astype(F32) + attn_b[1 - x, flat, :].astype(F32)
        ).astype(BF16)

    attn_second = [
        mail.send(ea.at[one_rows(x, 1 - y), left], attn_last_a, here.to_y),
        mail.send(ea.at[one_rows(1 - x, y), right], attn_last_b, here.to_x),
    ]
    def settle_attn():
        get_slope_attn.wait()
        for copy in attn_second:
            copy.wait_recv()

        @pl.loop(0, share // step)
        def _(index):
            flat = pl.ds(mul(index, step), step)
            at = pl.ds(pl.multiple_of(here.slot(x, core, y) * share + index * step, step), step)
            came = pl.ds(pl.multiple_of(y * share + index * step, step), step)
            mine = ea[at, left].astype(F32) + attn_a[came, :].astype(F32)
            mine = mine + attn_last_a[flat, :].astype(F32)
            ea[at, left] = (mine * slope_attn[flat, left].astype(F32)).astype(BF16)
            mine = ea[at, right].astype(F32) + attn_b[x, flat, :].astype(F32)
            mine = mine + attn_last_b[flat, :].astype(F32)
            ea[at, right] = (mine * slope_attn[flat, right].astype(F32)).astype(BF16)

        ends.append(fetch(ea.at[one_rows(x, y)], out_attn))

    ends = []
    for tick in tok_ticks:
        output_wave(17 + next(count))
        if tick > 9:
            next(gain_waves, None)
        if tick == 10:
            ends.append(fetch(own_ffn, mixed_out.at[chunk_rows]))
            ends.append(fetch(own_tokens, tokens_out.at[chunk_rows]))
        if tick == 11:
            settle(0)
        if tick == 12:
            settle_attn()
    for tick in ffn_ticks:
        pass
    for _ in gain_waves:
        pass
    ends.append(fetch(gain_sum.at[2], gains_out))
    ffn_line.close()
    tok_line.close()
    for keep, give in ending:
        give.wait_recv()
    for keep, give in ending[1:]:
        keep.wait()
    mail.close()
    for copy in ends:
        copy.wait()


def back(given, x1, small, attn, tokens, cotangent, segments, slope_ffn, slope_attn):
    rows, width = tokens.shape
    half = given[2].shape[1]
    share = width // 8
    e_attn, query, kv = attn[0], attn[1], attn[2]
    n_attn, n_query, n_kv = e_attn.shape[1], query.shape[1], kv.shape[1]
    cut = 3 * n_attn // 4
    chunk = rows // 4
    shapes = [
        *[((share, 2 * half), BF16)] * 3,
        ((share, n_attn), BF16),
        ((rows, width), BF16),
        ((rows, width), BF16),
        ((2, width), F32),
        *[((width, half), BF16)] * 3,
    ]
    in_vmem = pl.BlockSpec(memory_space=pltpu.VMEM)
    anywhere = pl.BlockSpec(memory_space=pl.ANY)
    scratch = [
        pltpu.VMEM((2, 2 * share, half), BF16),
        pltpu.VMEM((2, 2, share, half), BF16),
        pltpu.VMEM((3, 2 * share, half), BF16),
        pltpu.VMEM((3, 2, share, half), BF16),
        pltpu.VMEM((3, share, half), BF16),
        pltpu.VMEM((3, share, half), BF16),
        pltpu.VMEM((2, share, half), BF16),
        pltpu.VMEM((rows, width), BF16),
        pltpu.VMEM((rows, width), BF16),
        pltpu.VMEM((rows, width), BF16),
        pltpu.VMEM((chunk, width), BF16),
        pltpu.VMEM((chunk, width), BF16),
        pltpu.VMEM((2, 3, chunk, width), BF16),
        pltpu.VMEM((2, 3, chunk, width), BF16),
        pltpu.VMEM((chunk // BACK_SUBS, width), F32),
        pltpu.VMEM((width, n_attn), BF16),
        pltpu.VMEM((2, 2 * share, n_attn), BF16),
        pltpu.VMEM((2 * share, cut), BF16),
        pltpu.VMEM((2, share, n_attn - cut), BF16),
        pltpu.VMEM((share, cut), BF16),
        pltpu.VMEM((share, n_attn - cut), BF16),
        pltpu.VMEM((rows + EXTRA, n_query), BF16),
        pltpu.VMEM((rows + EXTRA, n_kv), BF16),
        pltpu.VMEM((rows, n_query), BF16),
        pltpu.VMEM((rows, width), BF16),
        pltpu.VMEM((rows + EXTRA, 128), F32),
        pltpu.VMEM((rows, n_query + n_kv), BF16),
        pltpu.VMEM((rows + EXTRA, n_kv), F32),
        pltpu.VMEM((EXTRA, n_query), BF16),
        pltpu.VMEM((EXTRA, n_query), BF16),
        pltpu.VMEM((EXTRA, n_query + n_kv), BF16),
        pltpu.VMEM((EXTRA, n_query + n_kv), BF16),
        pltpu.VMEM((chunk, width), F32),
        pltpu.VMEM((chunk, width), F32),
        pltpu.VMEM((chunk, width), BF16),
        pltpu.VMEM((chunk, width), BF16),
        pltpu.VMEM((2, width), F32),
        pltpu.VMEM((3, 2, width), F32),
        pltpu.VMEM((9, 2, width), F32),
        *line_sems(BACK_SUBS),
        *line_sems(BACK_SUBS),
        pltpu.SemaphoreType.DMA((3, 2)),
        pltpu.SemaphoreType.DMA((36,)),
        pltpu.SemaphoreType.DMA((31,)),
        pltpu.SemaphoreType.DMA((31,)),
    ]
    places = [anywhere] * 9 + [in_vmem] + [anywhere] * 7 + [in_vmem] + [anywhere] * 2
    return pl.pallas_call(
        back_kernel,
        out_shape=[jax.ShapeDtypeStruct(s, d) for s, d in shapes],
        in_specs=places,
        out_specs=[anywhere] * len(shapes),
        scratch_shapes=scratch,
        compiler_params=pltpu.CompilerParams(
            collective_id=1, has_side_effects=True, vmem_limit_bytes=VMEM_BYTES
        ),
        cost_estimate=pl.CostEstimate(
            flops=26 * 10**9, bytes_accessed=120 * 10**6, transcendentals=4 * 10**6
        ),
        name="back",
    )(*given, x1, small, *attn, tokens, cotangent, segments, slope_ffn, slope_attn)


def end_kernel(
    mixed_in,
    tokens_in,
    gate_in,
    up_in,
    attn_in,
    down_in,
    small,
    peaks,
    gain_sum,
    mixed,
    tokens,
    query,
    key,
    value,
    out,
    gate,
    up,
    down,
    attn_scales,
    kv_scales,
    ffn_scales,
    gain_one,
    gain_two,
    tall_in,
    tall_out,
    wide_in,
    wide_out,
    attn_b,
    attn_f,
    down_b,
    down_f,
    turned,
    in_sem,
    out_sem,
):
    n_query, n_key = query.shape[1], key.shape[1]
    n_in = n_query + 2 * n_key
    step = 32
    reads = [
        (mixed_in, tall_in.at[0]),
        (tokens_in, tall_in.at[1]),
        (down_in, down_b),
        (gate_in, wide_in.at[0]),
        (up_in, wide_in.at[1]),
        (attn_in, attn_b),
    ]
    reads = [pltpu.make_async_copy(a, b, in_sem.at[i]) for i, (a, b) in enumerate(reads)]
    for copy in reads:
        copy.start()
    writes = []

    def write(src, dst):
        copy = pltpu.make_async_copy(src, dst, out_sem.at[len(writes)])
        copy.start()
        writes.append(copy)

    def widen(src, dst):
        @pl.loop(0, src.shape[0] // step)
        def _(index):
            at = pl.ds(mul(index, step), step)
            dst[at, :] = src[at, :].astype(F32)

    for i, target in enumerate((mixed, tokens)):
        reads[i].wait()
        widen(tall_in.at[i], tall_out.at[i])
        write(tall_out.at[i], target)
    reads[2].wait()
    widen(down_b, down_f)
    write(down_f, down)
    for i, target in enumerate((gate, up)):
        reads[3 + i].wait()
        widen(wide_in.at[i], wide_out.at[i])
        write(wide_out.at[i], target)
    reads[5].wait()
    widen(attn_b, attn_f)
    write(attn_f.at[:, pl.ds(0, n_query)], query)
    write(attn_f.at[:, pl.ds(n_query, n_key)], key)
    write(attn_f.at[:, pl.ds(n_query + n_key, n_key)], value)
    write(attn_f.at[:, pl.ds(n_in, n_query)], out)
    piece = small.shape[1]
    for row, first in enumerate((0, n_in)):
        for i in range(n_query // piece):
            at = first // piece + i
            attn_scales[row : row + 1, i * piece : (i + 1) * piece] = small[at : at + 1, :]
    for row in (0, 1):
        for i in range(n_key // piece):
            at = (n_query + row * n_key) // piece + i
            kv_scales[row : row + 1, i * piece : (i + 1) * piece] = small[at : at + 1, :]
    ffn_scales[...] = peaks[0:3, :]
    share, width = gain_one.shape[0], gain_sum.shape[1]
    slot = lax.axis_index("dp") * 2 + lax.axis_index("seq")
    turned[...] = jnp.zeros_like(turned)
    turned[0:2, :] = gain_sum[...]
    turned[...] = pltpu.roll(turned[...], lax.rem(width - slot * share, width), 1)
    gain_one[...] = turned[0, :share]
    gain_two[...] = turned[1, :share]
    for copy in writes:
        copy.wait()


def end(mixed_b, tokens_b, sum_gate, sum_up, sum_attn, sum_down, small, peaks, gain_sum, n_query):
    rows, width = mixed_b.shape
    share, hidden = sum_gate.shape
    n_attn = sum_attn.shape[1]
    n_key = (n_attn - 2 * n_query) // 2
    shapes = [
        (rows, width),
        (rows, width),
        (share, n_query),
        (share, n_key),
        (share, n_key),
        (share, n_query),
        (share, hidden),
        (share, hidden),
        (share, hidden),
        (2, n_query),
        (2, n_key),
        (3, hidden),
        (share,),
        (share,),
    ]
    in_vmem = pl.BlockSpec(memory_space=pltpu.VMEM)
    anywhere = pl.BlockSpec(memory_space=pl.ANY)
    return pl.pallas_call(
        end_kernel,
        out_shape=[jax.ShapeDtypeStruct(s, F32) for s in shapes],
        in_specs=[anywhere] * 6 + [in_vmem] * 3,
        out_specs=[anywhere] * 9 + [in_vmem] * 5,
        scratch_shapes=[
            pltpu.VMEM((2, rows, width), BF16),
            pltpu.VMEM((2, rows, width), F32),
            pltpu.VMEM((2, share, hidden), BF16),
            pltpu.VMEM((2, share, hidden), F32),
            pltpu.VMEM((share, n_attn), BF16),
            pltpu.VMEM((share, n_attn), F32),
            pltpu.VMEM((share, hidden), BF16),
            pltpu.VMEM((share, hidden), F32),
            pltpu.VMEM((8, width), F32),
            pltpu.SemaphoreType.DMA((6,)),
            pltpu.SemaphoreType.DMA((9,)),
        ],
        compiler_params=pltpu.CompilerParams(vmem_limit_bytes=VMEM_BYTES),
        cost_estimate=pl.CostEstimate(flops=0, bytes_accessed=29 * 10**6, transcendentals=0),
        name="end",
    )(mixed_b, tokens_b, sum_gate, sum_up, sum_attn, sum_down, small, peaks, gain_sum)


def paired_block(
    tokens,
    gain_attn,
    w_query,
    w_key,
    w_value,
    w_out,
    gain_ffn,
    w_gate,
    w_up,
    w_down,
    width_pick,
    segments,
    cotangent,
):
    dp, y = lax.axis_index("dp"), lax.axis_index("seq")
    n_query = w_query.shape[1]
    slot = dp * 2 + y
    mine = jnp.arange(8, dtype=jnp.int32)[:, None] == slot
    gains = [jnp.where(mine, g[None, :], 0) for g in (gain_attn, gain_ffn)]
    gains = jnp.pad(jnp.stack(gains).reshape(-1, 256), ((8, 6), (0, 0)))
    weights = (w_query, w_key, w_value, w_out.T, w_down.T, w_gate, w_up)
    (
        e_attn,
        hidden_two,
        resid,
        query_b,
        kv,
        heads_b,
        hidden_one,
        cot_other,
        mixed_in,
        grad_gate_b,
        grad_up_b,
        back_part,
        ffn_part,
        slope_ffn,
        slope_attn,
        small,
        peaks,
        early,
    ) = front(width_pick, weights, gains, tokens, cotangent, segments)
    sum_down, sum_gate, sum_up, sum_attn, mixed_b, tokens_b, gain_sum, _, _, _ = back(
        (back_part, ffn_part, mixed_in, grad_gate_b, grad_up_b, hidden_two, cot_other, early),
        resid,
        small,
        (e_attn, query_b, kv, heads_b, hidden_one),
        tokens,
        cotangent,
        segments,
        slope_ffn,
        slope_attn,
    )
    mixed, grad_tokens, g_query, g_key, g_value, g_out, g_gate, g_up, g_down, *scales, gain_one, gain_two = end(
        mixed_b, tokens_b, sum_gate, sum_up, sum_attn, sum_down, small, peaks, gain_sum, n_query
    )
    return (
        mixed,
        grad_tokens,
        g_query,
        g_key,
        g_value,
        g_out.T,
        g_gate,
        g_up,
        g_down.T,
        gain_one,
        gain_two,
        *scales,
    )


def solution(mesh):
    in_specs = (
        P(("dp", "seq"), None),
        P(("dp", "seq")),
        P(("dp", "seq"), "mp"),
        P(("dp", "seq"), "mp"),
        P(("dp", "seq"), "mp"),
        P("mp", ("dp", "seq")),
        P(("dp", "seq")),
        P(("dp", "seq"), "mp"),
        P(("dp", "seq"), "mp"),
        P("mp", ("dp", "seq")),
        P(),
        P("dp", None),
        P(("dp", "seq"), None),
    )
    out_specs = (
        P(("dp", "seq"), None),
        P(("dp", "seq"), None),
        P(("dp", "seq"), "mp"),
        P(("dp", "seq"), "mp"),
        P(("dp", "seq"), "mp"),
        P("mp", ("dp", "seq")),
        P(("dp", "seq"), "mp"),
        P(("dp", "seq"), "mp"),
        P("mp", ("dp", "seq")),
        P(("dp", "seq")),
        P(("dp", "seq")),
        P(None, "mp"),
        P(None, "mp"),
        P(None, "mp"),
    )
    shape = dict(mesh.shape)
    paired = shape["dp"] == 4 and shape["seq"] == 2 and shape["mp"] == 4
    block = paired_block if paired else on_device
    return jax.shard_map(
        block, mesh=mesh, in_specs=in_specs, out_specs=out_specs, check_vma=False
    )
```

```python
import itertools

import jax
import jax.numpy as jnp
from jax import lax
from jax.experimental import pallas as pl
from jax.experimental.pallas import tpu as pltpu
from jax.sharding import PartitionSpec as P

HQ = 8
HK = 4
HD = 256


EPSILON = 1e-06
SOFTCAP = 50.0


def width_levels(width_pick):
    return jnp.where(width_pick == 0, 1.0, jnp.where(width_pick == 1, 0.5, 0.25)).astype(
        jnp.float32
    )


def bounded(weight, bound):
    return (bound * jnp.tanh(weight.astype(jnp.float32) / bound)).astype(jnp.bfloat16)


def bound_slope(weight, bound):
    tangent = jnp.tanh(weight.astype(jnp.float32) / bound)
    return 1.0 - tangent * tangent


def channel_peak(weight, along):
    return jnp.max(jnp.abs(weight.astype(jnp.float32)), axis=along)


def inner_rows(left, right):
    return lax.dot_general(
        left, right, (((0,), (0,)), ((), ())), preferred_element_type=jnp.float32
    )


def against(left, weight):
    return lax.dot_general(
        left, weight, (((1,), (1,)), ((), ())), preferred_element_type=jnp.float32
    )


def forward_norm(values):
    inverse = lax.rsqrt(jnp.mean(values * values, axis=-1, keepdims=True) + EPSILON)
    return (values * inverse, inverse)


def backward_norm(grad_normed, normed, inverse):
    return inverse * (grad_normed - normed * jnp.mean(grad_normed * normed, axis=-1, keepdims=True))


def gelu_tanh(values):
    return jax.nn.gelu(values, approximate=True)


def on_device(
    tokens,
    gain_attn,
    w_query,
    w_key,
    w_value,
    w_out,
    gain_ffn,
    w_gate,
    w_up,
    w_down,
    width_pick,
    segments,
    cotangent,
):
    level_of = width_levels(width_pick)
    peaks = (
        lax.pmax(channel_peak(w_query, 0).astype(jnp.bfloat16), ("dp", "seq")).astype(jnp.float32),
        lax.pmax(channel_peak(w_key, 0).astype(jnp.bfloat16), ("dp", "seq")).astype(jnp.float32),
        lax.pmax(channel_peak(w_value, 0).astype(jnp.bfloat16), ("dp", "seq")).astype(jnp.float32),
        lax.pmax(channel_peak(w_out, 1).astype(jnp.bfloat16), ("dp", "seq")).astype(jnp.float32),
        lax.pmax(channel_peak(w_gate, 0).astype(jnp.bfloat16), ("dp", "seq")).astype(jnp.float32),
        lax.pmax(channel_peak(w_up, 0).astype(jnp.bfloat16), ("dp", "seq")).astype(jnp.float32),
        lax.pmax(channel_peak(w_down, 1).astype(jnp.bfloat16), ("dp", "seq")).astype(jnp.float32),
    )
    peak_query, peak_key, peak_value, peak_out, peak_gate, peak_up, peak_down = peaks
    bound_query = peak_query[None, :] * level_of[0]
    bound_key = peak_key[None, :] * level_of[1]
    bound_value = peak_value[None, :] * level_of[2]
    bound_out = peak_out[:, None] * level_of[3]
    bound_gate = peak_gate[None, :] * level_of[4]
    bound_up = peak_up[None, :] * level_of[5]
    bound_down = peak_down[:, None] * level_of[6]
    fetched = (
        lax.all_gather(w_query, ("dp", "seq"), axis=0, tiled=True),
        lax.all_gather(w_key, ("dp", "seq"), axis=0, tiled=True),
        lax.all_gather(w_value, ("dp", "seq"), axis=0, tiled=True),
        lax.all_gather(gain_attn, ("dp", "seq"), axis=0, tiled=True),
        lax.all_gather(w_gate, ("dp", "seq"), axis=0, tiled=True),
        lax.all_gather(w_up, ("dp", "seq"), axis=0, tiled=True),
        lax.all_gather(gain_ffn, ("dp", "seq"), axis=0, tiled=True),
    )
    full_query, full_key, full_value, full_gain_one = (
        fetched[0],
        fetched[1],
        fetched[2],
        fetched[3],
    )
    later_rows = (fetched[4], fetched[5], fetched[6])
    columns = (
        lax.all_gather(w_out, ("dp", "seq"), axis=1, tiled=True),
        lax.all_gather(w_down, ("dp", "seq"), axis=1, tiled=True),
    )
    eff_query = bounded(full_query, bound_query)
    eff_key = bounded(full_key, bound_key)
    eff_value = bounded(full_value, bound_value)
    eff_out = bounded(columns[0], bound_out)
    eff_down = bounded(columns[1], bound_down)
    gain_one = full_gain_one.astype(jnp.float32)
    mp_count = lax.axis_size("mp")
    local_kv = HK // mp_count
    ratio = HQ // HK
    rows_here = tokens.shape[0]
    seg_row = segments[0]
    group = seg_row.shape[0]
    start = lax.axis_index("seq") * rows_here
    query_pos = start + jnp.arange(rows_here, dtype=jnp.int32)
    key_pos = jnp.arange(group, dtype=jnp.int32)
    seg_query = lax.dynamic_slice_in_dim(seg_row, start, rows_here)
    allowed = (seg_query[:, None] == seg_row[None, :]) & (key_pos[None, :] <= query_pos[:, None])
    scale = HD ** (-0.5)
    tokens_full = tokens.astype(jnp.float32)
    normed_one, inverse_one = forward_norm(tokens_full)
    hidden_one = (normed_one * gain_one).astype(jnp.bfloat16)
    query_b = jnp.dot(hidden_one, eff_query, preferred_element_type=jnp.float32).astype(
        jnp.bfloat16
    )
    key_b = jnp.dot(hidden_one, eff_key, preferred_element_type=jnp.float32).astype(jnp.bfloat16)
    value_b = jnp.dot(hidden_one, eff_value, preferred_element_type=jnp.float32).astype(
        jnp.bfloat16
    )
    key_all, value_all = (
        lax.all_gather(key_b, "seq", axis=0, tiled=True),
        lax.all_gather(value_b, "seq", axis=0, tiled=True),
    )
    query_heads = query_b.reshape(rows_here, local_kv, ratio, HD)
    key_heads = key_all.reshape(group, local_kv, HD)
    value_heads = value_all.reshape(group, local_kv, HD)

    def logits():
        raw = jnp.einsum(
            "tjrd,kjd->jrtk", query_heads, key_heads, preferred_element_type=jnp.float32
        )
        bent = jnp.tanh(raw * scale / SOFTCAP)
        capped = jnp.where(allowed[None, None], SOFTCAP * bent, -1e30)
        return (capped, bent)

    capped, bent = logits()
    largest = jnp.max(capped, axis=-1, keepdims=True)
    weights = jnp.exp(capped - largest)
    totals = jnp.sum(weights, axis=-1, keepdims=True)
    log_total = largest + jnp.log(totals)
    probs_b = (weights / totals).astype(jnp.bfloat16)
    heads_b = (
        jnp.einsum("jrtk,kjd->tjrd", probs_b, value_heads, preferred_element_type=jnp.float32)
        .reshape(rows_here, -1)
        .astype(jnp.bfloat16)
    )
    attn_total = lax.psum(jnp.dot(heads_b, eff_out, preferred_element_type=jnp.float32), "mp")
    resid = tokens_full + attn_total
    eff_gate = bounded(later_rows[0], bound_gate)
    eff_up = bounded(later_rows[1], bound_up)
    gain_two = later_rows[2].astype(jnp.float32)
    normed_two, inverse_two = forward_norm(resid)
    hidden_two = (normed_two * gain_two).astype(jnp.bfloat16)
    gate_full = jnp.dot(hidden_two, eff_gate, preferred_element_type=jnp.float32)
    upper_full = jnp.dot(hidden_two, eff_up, preferred_element_type=jnp.float32)
    gelu_value, gelu_back = jax.vjp(gelu_tanh, gate_full)
    mixed_in = (gelu_value * upper_full).astype(jnp.bfloat16)
    ffn_total = lax.psum(
        jnp.dot(mixed_in, eff_down, preferred_element_type=jnp.float32).astype(jnp.bfloat16), "mp"
    ).astype(jnp.float32)
    mixed = resid + ffn_total
    grad_mixed_in = against(cotangent, eff_down)
    grad_down_eff = inner_rows(mixed_in, cotangent)
    grad_gate_b = gelu_back(grad_mixed_in * upper_full)[0].astype(jnp.bfloat16)
    grad_upper_b = (grad_mixed_in * gelu_value).astype(jnp.bfloat16)
    grad_hidden_two = lax.psum(against(grad_gate_b, eff_gate) + against(grad_upper_b, eff_up), "mp")
    gain_two_part = jnp.sum(grad_hidden_two * normed_two, axis=0)
    grad_resid = cotangent.astype(jnp.float32) + backward_norm(
        grad_hidden_two * gain_two, normed_two, inverse_two
    )
    grad_gate_eff = inner_rows(hidden_two, grad_gate_b)
    grad_up_eff = inner_rows(hidden_two, grad_upper_b)
    grad_resid_b = grad_resid.astype(jnp.bfloat16)
    grad_heads_b = against(grad_resid_b, eff_out).astype(jnp.bfloat16)
    grad_out_eff = inner_rows(heads_b, grad_resid_b)
    grad_heads = grad_heads_b.reshape(rows_here, local_kv, ratio, HD)
    capped_again, bent_again = logits()
    probs = jnp.exp(capped_again - log_total)
    probs_again = probs.astype(jnp.bfloat16)
    grad_probs = jnp.einsum(
        "tjrd,kjd->jrtk", grad_heads, value_heads, preferred_element_type=jnp.float32
    )
    row_dot = jnp.sum(probs * grad_probs, axis=-1, keepdims=True)
    grad_raw_b = (probs * (grad_probs - row_dot) * (1.0 - bent_again * bent_again) * scale).astype(
        jnp.bfloat16
    )
    grad_query_b = (
        jnp.einsum("jrtk,kjd->tjrd", grad_raw_b, key_heads, preferred_element_type=jnp.float32)
        .reshape(rows_here, -1)
        .astype(jnp.bfloat16)
    )
    grad_key_full = jnp.einsum(
        "jrtk,tjrd->kjd", grad_raw_b, query_heads, preferred_element_type=jnp.float32
    ).reshape(group, -1)
    grad_value_full = jnp.einsum(
        "jrtk,tjrd->kjd", probs_again, grad_heads, preferred_element_type=jnp.float32
    ).reshape(group, -1)
    grad_key_sum, grad_value_sum = (
        lax.psum_scatter(grad_key_full, "seq", scatter_dimension=0, tiled=True),
        lax.psum_scatter(grad_value_full, "seq", scatter_dimension=0, tiled=True),
    )
    grad_key_b = grad_key_sum.astype(jnp.bfloat16)
    grad_value_b = grad_value_sum.astype(jnp.bfloat16)
    grad_hidden_one = lax.psum(
        against(grad_query_b, eff_query)
        + against(grad_key_b, eff_key)
        + against(grad_value_b, eff_value),
        "mp",
    )
    gain_one_part = jnp.sum(grad_hidden_one * normed_one, axis=0)
    grad_tokens = grad_resid + backward_norm(grad_hidden_one * gain_one, normed_one, inverse_one)
    grad_query_eff = inner_rows(hidden_one, grad_query_b)
    grad_key_eff = inner_rows(hidden_one, grad_key_b)
    grad_value_eff = inner_rows(hidden_one, grad_value_b)
    row_sums = (
        lax.psum_scatter(grad_query_eff, ("dp", "seq"), scatter_dimension=0, tiled=True),
        lax.psum_scatter(grad_key_eff, ("dp", "seq"), scatter_dimension=0, tiled=True),
        lax.psum_scatter(grad_value_eff, ("dp", "seq"), scatter_dimension=0, tiled=True),
        lax.psum_scatter(grad_gate_eff, ("dp", "seq"), scatter_dimension=0, tiled=True),
        lax.psum_scatter(grad_up_eff, ("dp", "seq"), scatter_dimension=0, tiled=True),
        lax.psum_scatter(gain_one_part, ("dp", "seq"), scatter_dimension=0, tiled=True),
        lax.psum_scatter(gain_two_part, ("dp", "seq"), scatter_dimension=0, tiled=True),
    )
    col_sums = (
        lax.psum_scatter(grad_out_eff, ("dp", "seq"), scatter_dimension=1, tiled=True),
        lax.psum_scatter(grad_down_eff, ("dp", "seq"), scatter_dimension=1, tiled=True),
    )
    sum_query, sum_key, sum_value, sum_gate, sum_up, sum_gain_one, sum_gain_two = row_sums
    out_sum, sum_down = col_sums
    grad_query = sum_query * bound_slope(w_query, bound_query)
    grad_key = sum_key * bound_slope(w_key, bound_key)
    grad_value = sum_value * bound_slope(w_value, bound_value)
    grad_gate = sum_gate * bound_slope(w_gate, bound_gate)
    grad_up = sum_up * bound_slope(w_up, bound_up)
    grad_out = out_sum * bound_slope(w_out, bound_out)
    grad_down = sum_down * bound_slope(w_down, bound_down)
    attn_scales = jnp.stack([peak_query, peak_out])
    kv_scales = jnp.stack([peak_key, peak_value])
    ffn_scales = jnp.stack([peak_gate, peak_up, peak_down])
    return (
        mixed,
        grad_tokens,
        grad_query,
        grad_key,
        grad_value,
        grad_out,
        grad_gate,
        grad_up,
        grad_down,
        sum_gain_one,
        sum_gain_two,
        attn_scales,
        kv_scales,
        ffn_scales,
    )


F32 = jnp.float32
BF16 = jnp.bfloat16
MESH = pl.DeviceIdType.MESH
VMEM_BYTES = 63 * 1024 * 1024


def natural(left, right):
    return jnp.dot(left, right, preferred_element_type=F32)


def mul(index, size):
    return pl.multiple_of(index * size, size)


class Place:
    def __init__(self):
        dp, y, z = lax.axis_index("dp"), lax.axis_index("seq"), lax.axis_index("mp")
        x, core = dp // 2, dp % 2
        self.x, self.y, self.z, self.core = x, y, z, core
        self.to_core = (x * 2 + (1 - core), y, z)
        self.to_x = ((1 - x) * 2 + core, y, z)
        self.to_y = (dp, 1 - y, z)
        self.to_xy = ((1 - x) * 2 + core, 1 - y, z)
        self.to_up = (dp, y, jnp.minimum(z + 1, 3))
        self.to_down = (dp, y, jnp.maximum(z - 1, 0))

    def slot(self, x, core, y):
        return (x * 2 + core) * 2 + y


def greet(here, targets):
    barrier = pltpu.get_barrier_semaphore()
    for target in targets:
        pl.semaphore_signal(barrier, inc=1, device_id=target, device_id_type=MESH)

    @pl.when(here.z < 3)
    def _():
        pl.semaphore_signal(barrier, inc=1, device_id=here.to_up, device_id_type=MESH)

    @pl.when(here.z > 0)
    def _():
        pl.semaphore_signal(barrier, inc=1, device_id=here.to_down, device_id_type=MESH)

    inner = (here.z < 3) & (here.z > 0)

    @pl.when(inner)
    def _():
        pl.semaphore_wait(barrier, len(targets) + 2)

    @pl.when(jnp.logical_not(inner))
    def _():
        pl.semaphore_wait(barrier, len(targets) + 1)


def remote(src, dst, send, recv, target):
    return pltpu.make_async_remote_copy(
        src_ref=src,
        dst_ref=dst,
        send_sem=send,
        recv_sem=recv,
        device_id=target,
        device_id_type=MESH,
    )


class Line:
    def __init__(self, here, partial, gathered, land, total, sems, transform, own=None, give=None, subs=4):
        self.here, self.partial, self.gathered, self.own = here, partial, gathered, own
        self.land, self.total, self.sems, self.transform = land, total, sems, transform
        self.size, self.subs = partial.shape[0] // 4, subs
        self.give = give
        self.part = self.size // subs

    def rows(self, chunk, sub):
        return pl.ds(pl.multiple_of(chunk * self.size + sub * self.part, self.part), self.part)

    def scatter_copy(self, way, step, sub=None):
        z = self.here.z
        chunk = jnp.minimum(z + 4 - step, 3) if way == 0 else jnp.maximum(z - 4 + step, 0)
        rows, spot = self.span(chunk, sub)
        at = (0, way, step - 1)
        recv = self.sems[1].at[at + (sub or 0,)]
        target = self.here.to_up if way == 0 else self.here.to_down
        dst = self.land.at[way, step - 1, spot]
        return remote(self.partial.at[rows], dst, self.sems[0].at[at], recv, target)

    def gather_copy(self, way, step, sub=None):
        z = self.here.z
        chunk = jnp.maximum(z - (step - 1), 0) if way == 0 else jnp.minimum(z + (step - 1), 3)
        rows, spot = self.span(chunk, sub)
        at = (1, way, step - 1)
        recv = self.sems[1].at[at + (sub or 0,)]
        target = self.here.to_up if way == 0 else self.here.to_down
        ref = self.gathered.at[rows]
        src = ref
        if self.own is not None and step == 1:
            src = self.own.at[spot]
        return remote(src, ref, self.sems[0].at[at], recv, target)

    def span(self, chunk, sub):
        if sub is None:
            return pl.ds(pl.multiple_of(chunk * self.size, self.size), self.size), pl.ds(0, self.size)
        return self.rows(chunk, sub), pl.ds(sub * self.part, self.part)

    def far(self, way):
        return self.here.z if way == 0 else 3 - self.here.z

    def scatter(self, step, sub):
        for way in (0, 1):
            far = self.far(way)

            @pl.when((far <= step - 1) & (far <= 2))
            def _(way=way, far=far):
                if step > 1:

                    @pl.when(far >= 1)
                    def _():
                        self.scatter_copy(way, step - 1, sub).wait_recv()
                        z = self.here.z
                        chunk = z + 4 - step if way == 0 else z - 4 + step
                        rows = self.rows(chunk, sub)
                        came = self.land[way, step - 2, pl.ds(sub * self.part, self.part), :]
                        mine = self.partial[rows, :].astype(F32)
                        self.partial[rows, :] = (mine + came.astype(F32)).astype(BF16)

                self.scatter_copy(way, step, sub).start()

    def finish(self, sub):
        rows = self.rows(self.here.z, sub)
        spot = pl.ds(sub * self.part, self.part)
        self.total[...] = self.partial[rows, :].astype(F32)
        for way in (0, 1):

            @pl.when(self.far(way) >= 1)
            def _(way=way):
                self.scatter_copy(way, 3, sub).wait_recv()
                self.total[...] += self.land[way, 2, spot, :].astype(F32)

        result = self.transform(sub, spot, self.total[...])
        if self.own is None:
            self.gathered[rows, :] = result
        else:
            self.own[spot, :] = result

    def gather(self, step, sub):
        for way in (0, 1):
            far = self.far(way)

            @pl.when((far >= step - 1) & (far <= 2))
            def _(way=way):
                self.gather_copy(way, step, sub).start()

    def landed(self, step, sub):
        for way in (0, 1):

            @pl.when(self.far(way) >= step)
            def _(way=way):
                self.gather_copy(way, step, sub).wait_recv()

    def ticks(self):
        self.scatter(1, 0)
        for tick in range(self.subs + 6):
            for stage in range(7):
                sub = tick - stage + (stage == 0)
                if 0 <= sub < self.subs:
                    if stage < 3:
                        self.scatter(stage + 1, sub)
                    else:
                        if stage == 3:
                            self.finish(sub)
                        else:
                            self.landed(stage - 3, sub)
                        if stage < 6:
                            self.gather(stage - 2, sub)
                        elif self.give is not None:
                            self.give(sub)
            yield tick

    def close(self):
        for step in (1, 2, 3):
            for way in (0, 1):
                far = self.far(way)

                @pl.when((far <= step - 1) & (far <= 2))
                def _(way=way, step=step):
                    self.scatter_copy(way, step).wait_send()

                @pl.when((far >= step - 1) & (far <= 2))
                def _(way=way, step=step):
                    self.gather_copy(way, step).wait_send()


def line_sems(subs):
    return [pltpu.SemaphoreType.DMA((2, 2, 3)), pltpu.SemaphoreType.DMA((2, 2, 3, subs))]


def line_scratch(rows, width, subs):
    return [
        pltpu.VMEM((rows, width), BF16),
        pltpu.VMEM((2, 3, rows // 4, width), BF16),
        pltpu.VMEM((rows // 4 // subs, width), F32),
        *line_sems(subs),
    ]


class Mail:
    def __init__(self, send_sem, recv_sem):
        self.send_sem, self.recv_sem = send_sem, recv_sem
        self.sent, self.gone = [], []
        self.n_send = self.n_recv = 0

    def make(self, src, dst, target, send_at=None, recv_at=None):
        alone = send_at is None
        if alone:
            send_at, self.n_send = self.n_send, self.n_send + 1
        if recv_at is None:
            recv_at, self.n_recv = self.n_recv, self.n_recv + 1
        copy = remote(src, dst, self.send_sem.at[send_at], self.recv_sem.at[recv_at], target)
        if alone:
            self.sent.append(copy)
        return copy

    def send(self, src, dst, target, send_at=None, recv_at=None):
        copy = self.make(src, dst, target, send_at, recv_at)
        copy.start()
        return copy

    def group(self, leaving, coming, target):
        send_at, recv_at = self.n_send, self.n_recv
        self.n_send, self.n_recv = send_at + 1, recv_at + 1
        sems = self.send_sem.at[send_at], self.recv_sem.at[recv_at]
        self.sent.append(remote(leaving, leaving, *sems, target))
        return send_at, recv_at, remote(coming, coming, *sems, target)

    def finish(self, copy):
        copy.wait_send()
        self.gone.append(copy)

    def close(self):
        for copy in self.sent:
            if all(copy is not other for other in self.gone):
                copy.wait_send()


FRONT_SUBS, BACK_SUBS = 4, 8


EXTRA = 16


def edge(y, rows):
    return pl.multiple_of((1 - y) * (rows - EXTRA), EXTRA)


def number_rows(segments, y, out):
    rows = out.shape[0] - EXTRA

    def turned(start):
        row = segments[:, pl.ds(pl.multiple_of(start, 128), 128)].astype(F32)
        return jnp.transpose(jnp.broadcast_to(row, (128, 128)))

    for first in range(0, rows, 128):
        out[first : first + 128, :] = turned(y * rows + first)
    out[rows:, :] = jnp.where(y == 0, turned(rows)[:EXTRA], turned(rows - 128)[128 - EXTRA :])


def visible(keys, numbers, position, y):
    count = keys.shape[0]
    rows = count - EXTRA
    key = lax.broadcasted_iota(jnp.int32, (count, 1), 0)
    key_pos = jnp.where(key < rows, y * rows + key, key - EXTRA * y)
    return (keys[:, 0:1] == numbers) & (key_pos <= position)


def beside(value, n_heads):
    return jnp.concatenate([value] * n_heads, axis=1)


def extra_visible(keys, y, n_heads):
    rows = keys.shape[0] - EXTRA
    numbers = jnp.transpose(keys[rows:, :])[0:1, :]
    position = rows - EXTRA * y + lax.broadcasted_iota(jnp.int32, (1, EXTRA), 1)
    return visible(keys, beside(numbers, n_heads), beside(position, n_heads), y)


def soft_probs(query, kv, allowed):
    raw = against(kv[:, :HD], query)
    bent = jnp.tanh(raw * HD ** (-0.5) / SOFTCAP)
    capped = jnp.where(allowed, SOFTCAP * bent, -1e30)
    weights = jnp.exp(capped - jnp.max(capped, axis=0, keepdims=True))
    return weights / jnp.sum(weights, axis=0, keepdims=True), bent


def row_of(ref, first, count):
    return jnp.concatenate([ref[first + i : first + i + 1, :] for i in range(count)], axis=1)


def level(pick):
    return jnp.where(pick == 0, 1.0, jnp.where(pick == 1, 0.5, 0.25)).astype(F32)


GELU_C = 0.7978845608028654
GELU_A = 0.044715


def gelu_pair(value):
    square = value * value
    bent = jnp.tanh(GELU_C * value * (1.0 + GELU_A * square))
    out = 0.5 * value * (1.0 + bent)
    slope = 0.5 * (1.0 + bent)
    slope += 0.5 * value * (1.0 - bent * bent) * (GELU_C * (1.0 + 3.0 * GELU_A * square))
    return out, slope


def front_kernel(
    width_pick,
    w_query,
    w_key,
    w_value,
    w_out_t,
    w_down_t,
    w_gate,
    w_up,
    gain_attn,
    gain_ffn,
    tokens_in,
    cot_in,
    segments,
    e_attn_out,
    h2_out,
    x1_out,
    query_out,
    kv_out,
    heads_out,
    h1_out,
    cot_out,
    mixed_in_out,
    grad_gate_out,
    grad_up_out,
    back_out,
    ffn_out,
    slope_ffn_out,
    slope_attn_out,
    small_out,
    peaks_out,
    early_out,
    wf_mine,
    wf_other,
    ea,
    ed,
    eg,
    eu,
    rows_a,
    cots,
    query,
    kv,
    heads,
    h2,
    x1,
    mixed_in,
    grad_gate,
    grad_up,
    slope_attn,
    turned,
    small_src,
    small_land,
    small,
    peaks_src,
    peaks_land,
    peaks,
    peaks_peer,
    keys,
    extra_heads,
    extra_land,
    early_made,
    early_sem,
    partial,
    land,
    total,
    line_send,
    line_recv,
    local_sem,
    send_sem,
    recv_sem,
):
    here = Place()
    x, y, z, core = here.x, here.y, here.z, here.core
    rows, width = tokens_in.shape
    share, n_query = w_query.shape
    n_key = w_key.shape[1]
    n_in, n_attn = n_query + 2 * n_key, 2 * n_query + 2 * n_key
    half = w_gate.shape[1] // 2
    cuts = (0, 5 * half // 9, 7 * half // 9, half)
    weights = (w_down_t, w_gate, w_up)
    effective = (ed, eg, eu)
    tokens, h1 = rows_a.at[pl.ds(0, rows)], rows_a.at[pl.ds(rows, rows)]

    local_count = [0]

    def fetch(src, dst):
        copy = pltpu.make_async_copy(src, dst, local_sem.at[local_count[0]])
        local_count[0] += 1
        copy.start()
        return copy

    def slab(ref, sx, score, sy, first=0, part=share, cols=None):
        at = pl.ds(pl.multiple_of(here.slot(sx, score, sy) * share + first, 16), part)
        return ref.at[at] if cols is None else ref.at[at, cols]

    own_at = here.slot(x, core, y) * share
    attn_cols = [(w_query, 0), (w_key, n_query), (w_value, n_query + n_key), (w_out_t, n_in)]
    get_attn = [
        fetch(w, slab(ea, x, core, y, cols=pl.ds(at, w.shape[1]))) for w, at in attn_cols
    ]
    mine_cols = pl.ds(pl.multiple_of(core * half, half), half)
    their_cols = pl.ds(pl.multiple_of((1 - core) * half, half), half)
    part_cols = [pl.ds(part * half, half) for part in range(3)]
    get_ffn = [fetch(w.at[:, mine_cols], wf_mine.at[:, part_cols[i]]) for i, w in enumerate(weights)]
    get_tokens = fetch(tokens_in, tokens)
    get_cot = fetch(cot_in, cots.at[pl.ds(0, rows)])
    greet(here, [here.to_core, here.to_x, here.to_y, here.to_xy])
    mail = Mail(send_sem, recv_sem)

    half_share = share // 2

    def peak(block):
        return jnp.max(jnp.abs(block.astype(F32)), axis=0, keepdims=True)

    def set_out(first):
        ref = slab(ea, x, core, y, first, half_share)
        return [mail.send(ref, ref, here.to_x), mail.send(ref, ref, here.to_y)]

    for copy in get_attn:
        copy.wait()
    attn_moves = set_out(0)
    own_rows = pl.ds(pl.multiple_of(own_at, 32), share)
    attn_peak = peak(ea[own_rows, :])
    piece = small_src.shape[1]
    n_pieces = n_attn // piece
    turned[...] = jnp.zeros_like(turned)
    turned[0, :share] = gain_attn[...].astype(F32)
    turned[1, :share] = gain_ffn[...].astype(F32)
    turned[...] = pltpu.roll(turned[...], own_at, 1)
    small_src[...] = jnp.zeros_like(small_src)
    for row in (0, 1):
        for index in range(width // piece):
            to = 8 + row * (width // piece) + index
            at = slice(index * piece, (index + 1) * piece)
            small_src[to : to + 1, :] = turned[row : row + 1, at]
    for index in range(n_pieces):
        at = slice(index * piece, (index + 1) * piece)
        small_src[index : index + 1, :] = attn_peak[:, at]
    first = mail.send(small_src, small_land.at[0], here.to_core)
    swap = [
        mail.send(w.at[:, their_cols], wf_other.at[:, part_cols[i]], here.to_core)
        for i, w in enumerate(weights)
    ]
    own = slab(ea, x, core, y)
    ac = mail.send(own, own, here.to_core)
    cot_copy = mail.send(cot_in, cots.at[pl.ds(rows, rows)], here.to_core)
    first.wait_recv()

    def merge(mine, other):
        mine[0:8, :] = jnp.maximum(mine[0:8, :], other[0:8, :])
        mine[8:, :] = mine[8:, :] + other[8:, :]

    small[...] = small_src[...]
    merge(small, small_land.at[0])
    ring = (here.to_x, here.to_y, here.to_xy)
    small_send = [mail.send(small, small_land.at[1 + i], to) for i, to in enumerate(ring)]

    for copy in get_ffn:
        copy.wait()
    for copy in swap:
        copy.wait_recv()
    peaks_src[...] = jnp.zeros_like(peaks_src)
    for part in range(3):
        cols = slice(part * half, (part + 1) * half)
        both = jnp.maximum(peak(wf_mine[:, cols]), peak(wf_other[:, cols]))
        line_at = (part + 2) % 3
        peaks_src[line_at : line_at + 1, :] = both
    peaks_send = [mail.send(peaks_src, peaks_land.at[i], to) for i, to in enumerate(ring)]
    attn_moves += set_out(half_share)

    for copy in small_send:
        copy.wait_recv()
        mail.finish(copy)
    for index in (1, 2, 3):
        merge(small, small_land.at[index])
    outs = [fetch(small, small_out)]

    get_tokens.wait()
    gain_one = row_of(small, 8, width // piece)
    gain_two = row_of(small, 8 + width // piece, width // piece)

    @pl.loop(0, rows // 32)
    def _(index):
        at = pl.ds(mul(index, 32), 32)
        h1[at, :] = (forward_norm(tokens[at, :].astype(F32))[0] * gain_one).astype(BF16)


    def tangent(block, bound):
        return jnp.tanh(block.astype(F32) / bound)

    for copy in peaks_send:
        copy.wait_recv()
    peaks[...] = peaks_src[...]
    for index in range(3):
        peaks[...] = jnp.maximum(peaks[...], peaks_land[index])
    peer_copy = mail.send(peaks, peaks_peer, here.to_core)
    outs.append(fetch(peaks, peaks_out.at[:, mine_cols]))
    picks = (6, 4, 5)
    other_at = here.slot(x, 1 - core, y) * share
    for part in range(3):
        cols = slice(part * half, (part + 1) * half)
        line_at = (part + 2) % 3
        bound = peaks[line_at : line_at + 1, :] * level(width_pick[picks[part]])

        @pl.loop(0, share // 32)
        def _(index, cols=cols, bound=bound, part=part):
            at = pl.ds(mul(index, 32), 32)
            for weight, start in ((wf_mine, own_at), (wf_other, other_at)):
                to = pl.ds(pl.multiple_of(start + index * 32, 32), 32)
                bent = tangent(weight[at, cols], bound)
                effective[part][to, :] = (bound * bent).astype(BF16)
                weight[at, cols] = (1.0 - bent * bent).astype(BF16)

    outs.append(fetch(wf_mine, slope_ffn_out.at[core]))
    outs.append(fetch(wf_other, slope_ffn_out.at[1 - core]))

    for copy in attn_moves:
        copy.wait_recv()
    from_x = slab(ea, 1 - x, core, y)
    corner = slab(ea, 1 - x, core, y, 0, half_share)
    dy = mail.send(corner, corner, here.to_y)
    cx = mail.send(from_x, from_x, here.to_core)
    from_y = slab(ea, x, core, 1 - y)
    corner = slab(ea, x, core, 1 - y, half_share, half_share)
    dx = mail.send(corner, corner, here.to_x)
    cy = mail.send(from_y, from_y, here.to_core)

    splits = [pl.ds(a, b - a) for a, b in zip(cuts, cuts[1:])]
    moving, together = {}, {}

    def block_of(part, split, count):
        return effective[part].at[pl.ds(0, count * share), splits[split]]

    def move(part, split, pair, axis, ref, target):
        if (part, split) not in together:
            leaving, coming = block_of(part, split, 6), block_of(part, split, 4)
            together[part, split] = mail.group(leaving, coming, here.to_x)
        send_at, recv_at, _ = together[part, split]
        copy = mail.send(ref, ref, target, send_at, None if pair == axis else recv_at)
        if pair == axis:
            moving[part, split, pair] = copy

    def ship(part, split, axis, pairs=(0, 1)):
        target = here.to_x if axis == 0 else here.to_y
        for pair in pairs:
            ref = slab(effective[part], x, pair, y, cols=splits[split])
            move(part, split, pair, axis, ref, target)

    def pass_on(part, split, pair):
        moving[part, split, pair].wait_recv()
        at = (1 - x, y) if pair == 0 else (x, 1 - y)
        ref = slab(effective[part], at[0], pair, at[1], cols=splits[split])
        move(part, split, pair, 2, ref, here.to_y if pair == 0 else here.to_x)

    def arrived(part, split):
        together[part, split][2].wait_recv()

    ship(0, 0, 0)
    ship(0, 0, 1, (0,))

    flat_peak = row_of(small, 0, n_pieces)
    bound_attn = jnp.concatenate(
        [
            flat_peak[:, :n_query] * level(width_pick[0]),
            flat_peak[:, n_query : n_query + n_key] * level(width_pick[1]),
            flat_peak[:, n_query + n_key : n_in] * level(width_pick[2]),
            flat_peak[:, n_in:] * level(width_pick[3]),
        ],
        axis=1,
    )

    def soften(sx, score, sy, slopes=False):
        base = here.slot(sx, score, sy) * share

        @pl.loop(0, share // 32)
        def _(index):
            at = pl.ds(mul(index, 32), 32)
            to = pl.ds(pl.multiple_of(base + index * 32, 32), 32)
            bent = tangent(ea[to, :], bound_attn)
            ea[to, :] = (bound_attn * bent).astype(BF16)
            if slopes:
                slope_attn[at, :] = (1.0 - bent * bent).astype(BF16)

    for copy in attn_moves + [ac]:
        mail.finish(copy)
    soften(x, core, y, True)
    outs.append(fetch(slope_attn, slope_attn_out))
    ac.wait_recv()
    soften(x, 1 - core, y)
    cx.wait_recv()
    soften(1 - x, 1 - core, y)
    cy.wait_recv()
    soften(x, 1 - core, 1 - y)
    dy.wait_recv()
    dx.wait_recv()
    across = slab(ea, 1 - x, core, 1 - y)
    cxy = mail.send(across, across, here.to_core)
    for copy in (dy, cx, dx, cy):
        mail.finish(copy)
    soften(1 - x, core, y)
    soften(x, core, 1 - y)
    cxy.wait_recv()
    mail.finish(cxy)
    soften(1 - x, core, 1 - y)
    soften(1 - x, 1 - core, 1 - y)
    e_attn_copy = fetch(ea, e_attn_out)

    tile = 256

    @pl.loop(0, n_query // tile)
    def _(index):
        cols = pl.ds(mul(index, tile), tile)
        query[:rows, cols] = natural(h1[...], ea[:, cols]).astype(BF16)

    @pl.loop(0, 2 * n_key // tile)
    def _(index):
        cols = pl.ds(mul(index, tile), tile)
        source = pl.ds(pl.multiple_of(n_query + index * tile, tile), tile)
        kv[:rows, cols] = natural(h1[...], ea[:, source]).astype(BF16)

    ours, theirs = pl.ds(edge(y, rows), EXTRA), pl.ds(rows, EXTRA)
    row_copies = [
        mail.send(ref.at[ours], ref.at[theirs], here.to_y) for ref in (query, kv)
    ]
    for part in (1, 2):
        ship(part, 0, 0)
    h1_copy = fetch(h1, h1_out)
    number_rows(segments, y, keys)
    for copy in row_copies:
        copy.wait_recv()

    block, n_heads = 128, n_query // HD

    def attend(at, allowed):
        stack = jnp.concatenate([query[at, i * HD : (i + 1) * HD] for i in range(n_heads)], axis=0)
        probs, _ = soft_probs(stack, kv, allowed)
        return inner_rows(probs.astype(BF16), kv[:, HD:]).astype(BF16)

    out = attend(theirs, extra_visible(keys, y, n_heads))
    for i in range(n_heads):
        extra_heads[:, i * HD : (i + 1) * HD] = out[i * EXTRA : (i + 1) * EXTRA]
    extra_copy = mail.send(extra_heads, extra_land, here.to_y)
    ship(0, 0, 1, (1,))
    for part in (1, 2):
        ship(part, 0, 1)

    @pl.loop(0, rows // block)
    def _(index):
        at = pl.ds(mul(index, block), block)
        start = pl.multiple_of(y * rows + index * block, block)
        numbers = segments[:, pl.ds(start, block)].astype(F32)
        position = start + lax.broadcasted_iota(jnp.int32, (1, block), 1)
        allowed = visible(keys, beside(numbers, n_heads), beside(position, n_heads), y)
        out = attend(at, allowed)
        for i in range(n_heads):
            heads[at, i * HD : (i + 1) * HD] = out[i * block : (i + 1) * block]

    extra_copy.wait_recv()
    middle = (lax.broadcasted_iota(jnp.int32, (EXTRA, 1), 0) == 0) & (y == 1)
    heads[:EXTRA, :] = jnp.where(middle, extra_land[...], heads[:EXTRA, :])

    @pl.loop(0, width // tile)
    def _(index):
        cols = pl.ds(mul(index, tile), tile)
        partial[:, cols] = against(heads[...], ea[cols, n_in:]).astype(BF16)

    outs += [fetch(query, query_out), fetch(kv, kv_out), fetch(heads, heads_out)]

    tall = 512

    def back_into_mixed(split):
        @pl.loop(0, 2 * rows // tall)
        def _(index):
            at = pl.ds(mul(index, tall), tall)
            grad_gate[at, splits[split]] = natural(cots[at, :], ed[:, splits[split]]).astype(BF16)

    def gated(split):
        cols, high = splits[split], 512 if split else 256

        @pl.loop(0, 2 * rows // high)
        def _(index):
            at = pl.ds(mul(index, high), high)
            gate = natural(h2[at, :], eg[:, cols])
            upper = natural(h2[at, :], eu[:, cols])
            value, slope = gelu_pair(gate)
            back = grad_gate[at, cols].astype(F32)
            mixed_in[at, cols] = (value * upper).astype(BF16)
            grad_gate[at, cols] = (back * upper * slope).astype(BF16)
            grad_up[at, cols] = (back * value).astype(BF16)

    def to_width(target, pairs, split, then=None):
        wide = width // 3

        def piece(at):
            for column in range(3):
                cols = slice(column * wide, (column + 1) * wide)
                added = against(pairs[0][0][at, splits[split]], pairs[0][1][cols, splits[split]])
                for left, right in pairs[1:]:
                    added += against(left[at, splits[split]], right[cols, splits[split]])
                if split:
                    added += target[column][at, :].astype(F32)
                target[column][at, :] = added.astype(BF16)

        if then is None:

            @pl.loop(0, 2 * rows // tall)
            def _(index):
                piece(pl.ds(mul(index, tall), tall))

        else:
            for first in range(0, 2 * rows, tall):
                piece(pl.ds(first, tall))
                then(pl.ds(first, tall))

    def transform(sub, spot, summed):
        at = pl.ds(pl.multiple_of(z * (rows // 4) + sub * line.part, line.part), line.part)
        resid = tokens[at, :].astype(F32) + summed
        x1[spot, :] = resid
        return (forward_norm(resid)[0] * gain_two).astype(BF16)

    own_half, other_half = (h2.at[pl.ds(first, rows)] for first in (0, rows))
    give_send, give_recv, all_given = mail.group(own_half, other_half, here.to_core)

    def give(sub):
        for chunk in range(4):
            first = chunk * (rows // 4) + sub * line.part
            src, dst = (h2.at[pl.ds(first + at, line.part)] for at in (0, rows))
            mail.send(src, dst, here.to_core, give_send, give_recv)

    line = Line(here, partial, h2, land, total, (line_send, line_recv), transform, give=give, subs=FRONT_SUBS)
    width_blocks = [pl.ds(i * (width // 3), width // 3) for i in range(3)]
    back_part = [rows_a.at[:, cols] for cols in width_blocks]
    spare = ((0, 0), (0, 1), (1, 0))
    ffn_part = [
        ea.at[pl.ds(i * 2 * rows, 2 * rows), pl.ds(j * (width // 3), width // 3)] for i, j in spare
    ]
    upward = ((grad_gate, eg), (grad_up, eu))
    downward = ((mixed_in, ed),)
    for tick in line.ticks():
        if tick == 1:
            pass_on(0, 0, 0)
            pass_on(0, 0, 1)
        if tick == 2:
            pass_on(1, 0, 0)
        if tick == 3:
            get_cot.wait()
            cot_copy.wait_recv()
            cot_keep = fetch(cots.at[pl.ds(rows, rows)], cot_out)
        if tick == 4:
            pass_on(1, 0, 1)
            pass_on(2, 0, 0)
        if tick == 5:
            pass_on(2, 0, 1)
            for part in range(3):
                for axis in (0, 1):
                    ship(part, 1, axis)
        if tick == 8:
            for axis in (0, 1):
                ship(0, 2, axis)
        if tick == 6:
            arrived(0, 0)
            back_into_mixed(0)
    line.close()
    outs.append(fetch(x1, x1_out))
    arrived(1, 0)
    arrived(2, 0)
    all_given.wait_recv()
    outs.append(fetch(h2, h2_out))
    gated(0)
    for part in range(3):
        for turn in (0, 1):
            pass_on(part, 1, turn)
    for part in (1, 2):
        for axis in (0, 1):
            ship(part, 2, axis)
    h1_copy.wait()
    to_width(back_part, upward, 0)
    arrived(0, 1)
    back_into_mixed(1)
    arrived(1, 1)
    arrived(2, 1)
    gated(1)
    e_attn_copy.wait()
    to_width(ffn_part, downward, 0)
    to_width(back_part, upward, 1)
    to_width(ffn_part, downward, 1)
    for part in range(3):
        for turn in (0, 1):
            pass_on(part, 2, turn)
    late = cuts[2]

    def early_copy(index):
        at = pl.ds(mul(index, tile), tile)
        return pltpu.make_async_copy(early_made, early_out.at[at], early_sem)

    @pl.loop(0, width // tile)
    def _(index):
        made = inner_rows(h2[:, pl.ds(mul(index, tile), tile)], grad_gate[:, :late]).astype(BF16)

        @pl.when(index > 0)
        def _():
            early_copy(index - 1).wait()

        early_made[...] = made
        early_copy(index).start()

    early_copy(width // tile - 1).wait()
    arrived(0, 2)
    back_into_mixed(2)
    arrived(1, 2)
    arrived(2, 2)
    gated(2)
    outs += [
        fetch(mixed_in, mixed_in_out),
        fetch(grad_gate, grad_gate_out),
        fetch(grad_up, grad_up_out),
    ]
    to_width(back_part, upward, 2, lambda at: outs.append(fetch(rows_a.at[at], back_out.at[at])))

    def ffn_leaves(at):
        for i in range(3):
            outs.append(fetch(ffn_part[i].at[at], ffn_out.at[at, width_blocks[i]]))

    to_width(ffn_part, downward, 2, ffn_leaves)
    cot_keep.wait()
    peer_copy.wait_recv()
    outs.append(fetch(peaks_peer, peaks_out.at[:, their_cols]))
    mail.close()
    for copy in outs:
        copy.wait()


def front(width_pick, weights, gain_attn, gain_ffn, tokens, cotangent, segments):
    rows, width = tokens.shape
    share, n_query = weights[0].shape
    n_kv = 2 * weights[1].shape[1]
    n_attn = 2 * n_query + n_kv
    hidden = weights[-1].shape[1]
    half = hidden // 2
    shapes = [
        ((width, n_attn), BF16),
        ((2 * rows, width), BF16),
        ((rows // 4, width), F32),
        ((rows + EXTRA, n_query), BF16),
        ((rows + EXTRA, n_kv), BF16),
        ((rows, n_query), BF16),
        ((rows, width), BF16),
        ((rows, width), BF16),
        ((2 * rows, half), BF16),
        ((2 * rows, half), BF16),
        ((2 * rows, half), BF16),
        ((2 * rows, width), BF16),
        ((2 * rows, width), BF16),
        ((2, share, 3 * half), BF16),
        ((share, n_attn), BF16),
        ((32, 256), F32),
        ((8, hidden), F32),
        ((width, 7 * half // 9), BF16),
    ]
    in_vmem = pl.BlockSpec(memory_space=pltpu.VMEM)
    in_smem = pl.BlockSpec(memory_space=pltpu.SMEM)
    anywhere = pl.BlockSpec(memory_space=pl.ANY)
    scratch = [
        pltpu.VMEM((share, 3 * half), BF16),
        pltpu.VMEM((share, 3 * half), BF16),
        pltpu.VMEM((width, n_attn), BF16),
        pltpu.VMEM((width, half), BF16),
        pltpu.VMEM((width, half), BF16),
        pltpu.VMEM((width, half), BF16),
        pltpu.VMEM((2 * rows, width), BF16),
        pltpu.VMEM((2 * rows, width), BF16),
        pltpu.VMEM((rows + EXTRA, n_query), BF16),
        pltpu.VMEM((rows + EXTRA, n_kv), BF16),
        pltpu.VMEM((rows, n_query), BF16),
        pltpu.VMEM((2 * rows, width), BF16),
        pltpu.VMEM((rows // 4, width), F32),
        pltpu.VMEM((2 * rows, half), BF16),
        pltpu.VMEM((2 * rows, half), BF16),
        pltpu.VMEM((2 * rows, half), BF16),
        pltpu.VMEM((share, n_attn), BF16),
        pltpu.VMEM((8, width), F32),
        pltpu.VMEM((32, 256), F32),
        pltpu.VMEM((4, 32, 256), F32),
        pltpu.VMEM((32, 256), F32),
        pltpu.VMEM((8, half), F32),
        pltpu.VMEM((3, 8, half), F32),
        pltpu.VMEM((8, half), F32),
        pltpu.VMEM((8, half), F32),
        pltpu.VMEM((rows + EXTRA, 128), F32),
        pltpu.VMEM((EXTRA, n_query), BF16),
        pltpu.VMEM((EXTRA, n_query), BF16),
        pltpu.VMEM((256, 7 * half // 9), BF16),
        pltpu.SemaphoreType.DMA,
        *line_scratch(rows, width, FRONT_SUBS),
        pltpu.SemaphoreType.DMA((34,)),
        pltpu.SemaphoreType.DMA((35,)),
        pltpu.SemaphoreType.DMA((53,)),
    ]
    return pl.pallas_call(
        front_kernel,
        out_shape=[jax.ShapeDtypeStruct(s, d) for s, d in shapes],
        in_specs=[in_smem] + [anywhere] * 7 + [in_vmem] * 2 + [anywhere] * 2 + [in_vmem],
        out_specs=[anywhere] * len(shapes),
        scratch_shapes=scratch,
        compiler_params=pltpu.CompilerParams(
            collective_id=0, has_side_effects=True, vmem_limit_bytes=VMEM_BYTES
        ),
        cost_estimate=pl.CostEstimate(
            flops=36 * 10**9, bytes_accessed=90 * 10**6, transcendentals=8 * 10**6
        ),
        name="front",
    )(width_pick, *weights, gain_attn, gain_ffn, tokens, cotangent, segments)


OUTPUT_PLAN = (7, 8, 10, 11, 12, 14, 15, 17, 18, 19, 20, 21, 22, 23)


def back_kernel(
    back_in,
    ffn_in,
    mixed_in,
    grad_gate,
    grad_up,
    h2_in,
    cot_other,
    early_in,
    x1_in,
    small,
    e_attn,
    query_in,
    kv_in,
    heads_in,
    h1_in,
    tokens_in,
    cot_in,
    segments,
    slope_ffn,
    slope_attn_in,
    out_down,
    out_gate,
    out_up,
    out_attn,
    mixed_out,
    tokens_out,
    gains_out,
    de_down,
    de_gate,
    de_up,
    stage_a,
    stage_b,
    land_a,
    land_b,
    last_a,
    last_b,
    slopes,
    partial,
    partial_ffn,
    grad_resid_b,
    own_ffn,
    own_tokens,
    land,
    land_ffn,
    total,
    ea,
    core_land,
    attn_a,
    attn_b,
    attn_last_a,
    attn_last_b,
    query,
    kv,
    heads,
    h1,
    keys,
    grad_in,
    grad_kv,
    edge_send,
    edge_land,
    row_send,
    row_land,
    x1,
    grad_resid,
    token_chunk,
    cot_chunk,
    gain_part,
    gain_sum,
    gain_land,
    line_send,
    line_recv,
    ffn_send,
    ffn_recv,
    work_sem,
    local_sem,
    send_sem,
    recv_sem,
):
    here = Place()
    x, y, z, core = here.x, here.y, here.z, here.core
    rows, width = tokens_in.shape
    share, half = last_a.shape[1], last_a.shape[2]
    n_query, n_attn = query.shape[1], ea.shape[1]
    n_in = n_attn - n_query
    de_ffn = (de_down, de_gate, de_up)
    out_ffn = (out_down, out_gate, out_up)
    chunk_rows = pl.ds(pl.multiple_of(z * (rows // 4), rows // 4), rows // 4)
    mine_cols = pl.ds(pl.multiple_of(core * half, half), half)
    tile = 256

    local_count = [0]

    def fetch(src, dst):
        copy = pltpu.make_async_copy(src, dst, local_sem.at[local_count[0]])
        local_count[0] += 1
        copy.start()
        return copy

    order = (1, 2, 0)
    slot_of = {part: i % 2 for i, part in enumerate(order)}

    late = early_in.shape[1]
    blocks = {0: [(de_down, 0, half)], 2: [(de_up, 0, half)]}
    blocks[1] = [(early_in, 0, late), (de_gate, late, half - late)]

    def lanes(ref, block):
        return ref if ref.shape[-1] == block[2] else ref.at[:, pl.ds(block[1], block[2])]

    def source(block, at):
        return lanes(block[0].at[at], block)

    def stage(part):
        a_rows = pl.ds(pl.multiple_of(here.slot(x, 0, 0) * share, share), 2 * share)
        slot = slot_of[part]
        copies = []
        for block in blocks[part]:
            copies.append(fetch(source(block, a_rows), lanes(stage_a.at[slot], block)))
            for i in (0, 1):
                b_rows = pl.ds(mul(here.slot(i, 1, y), share), share)
                copies.append(fetch(source(block, b_rows), lanes(stage_b.at[slot, i], block)))
        return copies

    sides = (mixed_in, grad_gate, grad_up)
    side_rows = [pl.ds(0, 2 * rows), pl.ds(2 * rows, 2 * rows), pl.ds(0, 2 * rows)]
    side_at = {part: ea.at[side_rows[i], pl.ds(0, half)] for i, part in enumerate(order)}
    strip_cols = pl.ds(half, tile)
    made_cols = {part: pl.ds(blocks[part][-1][1], blocks[part][-1][2]) for part in order}

    def strip_copies(part, index, slot):
        cols = pl.ds(mul(index, tile), tile)
        to = [
            ea.at[pl.ds(pl.multiple_of(slot * 2 * rows + i * rows, rows), rows), strip_cols]
            for i in (0, 1)
        ]
        if part:
            src = [h2_in.at[pl.ds(i * rows, rows), cols] for i in (0, 1)]
        else:
            src = [cot_in.at[:, cols], cot_other.at[:, cols]]
        return [
            pltpu.make_async_copy(src[i], to[i], work_sem.at[slot, i]) for i in (0, 1)
        ]

    def result_copy(part, index):
        at = pl.ds(mul(index, tile), tile)
        cols = made_cols[part]
        slot = lax.rem(index, 2)
        made = slopes.at[slot, pl.ds(0, tile), cols]
        return pltpu.make_async_copy(made, de_ffn[part].at[at, cols], work_sem.at[2, slot])

    sides_here = {order[0]: fetch(sides[order[0]], side_at[order[0]])}
    for copy in strip_copies(order[0], 0, 0):
        copy.start()
    get_x1 = fetch(x1_in, x1)
    get_cot = fetch(cot_in.at[chunk_rows], cot_chunk)
    get_tokens = fetch(tokens_in.at[chunk_rows], token_chunk)
    get_partial = fetch(back_in.at[pl.ds(0, rows)], partial)
    sides_here[order[1]] = fetch(sides[order[1]], side_at[order[1]])
    far_target = (x * 2 + core, y, lax.rem(z + 2, 4))
    near_target = (x * 2 + core, y, z + 1 - 2 * lax.rem(z, 2))
    plane = [here.to_core, here.to_x, here.to_y, here.to_xy]
    plane += [(2 * (1 - x) + 1 - core, y, z), (2 * x + 1 - core, 1 - y, z)]
    plane += [(2 * (1 - x) + 1 - core, 1 - y, z)]
    greet(here, [*plane, far_target])
    mail = Mail(send_sem, recv_sem)
    their_half = pl.ds(rows, rows)
    chunks = [jnp.where(z < 2, 3 - i, i) * (rows // 4) for i in range(4)]
    chunks = [pl.multiple_of(first, rows // 4) for first in chunks]
    back_copies = [
        mail.send(
            back_in.at[pl.ds(rows + first, rows // 4)],
            partial_ffn.at[pl.ds(first, rows // 4)],
            here.to_core,
        )
        for first in chunks
    ]
    ffn_copy = mail.send(ffn_in.at[their_half], h1, here.to_core)

    n_strips = width // tile

    def strips(part, first, last):
        if first == 0:
            sides_here[part].wait()

        @pl.loop(first, last)
        def _(index):
            slot = lax.rem(index, 2)
            for copy in strip_copies(part, index, slot):
                copy.wait()

            @pl.when(index + 1 < n_strips)
            def _():
                for copy in strip_copies(part, index + 1, 1 - slot):
                    copy.start()

            left = ea[pl.ds(pl.multiple_of(slot * 2 * rows, rows), 2 * rows), strip_cols]
            made = inner_rows(left, side_at[part][:, made_cols[part]]).astype(BF16)

            @pl.when(index > 1)
            def _():
                result_copy(part, index - 2).wait()

            slopes[slot, :tile, made_cols[part]] = made
            result_copy(part, index).start()

        if last == n_strips:
            for index in (n_strips - 2, n_strips - 1):
                result_copy(part, jnp.int32(index)).wait()
            at = order.index(part)
            if at + 1 < 3:
                for copy in strip_copies(order[at + 1], 0, 0):
                    copy.start()
            if at == 0:
                sides_here[order[2]] = fetch(sides[order[2]], side_at[order[2]])
            if at < 2:
                staged[part] = stage(part)

    staged = {}
    slope_here = {}

    def get_slopes(part):
        cols = pl.ds(part * half, half)
        slope_here[part] = fetch(slope_ffn.at[:, :, cols], slopes)

    first_hop, groups = {}, {}
    second_hop = {}
    ending = []

    def ship(part, i, block, axis):
        if axis == 0:
            at = pl.ds(mul(here.slot(1 - x, 0, i), share), share)
            to, target = land_a.at[part, pl.ds(i * share, share)], here.to_x
        else:
            at = pl.ds(mul(here.slot(i, 1, 1 - y), share), share)
            to, target = land_b.at[part, i], here.to_y
        if (part, block[1]) not in groups:
            four = lanes(de_ffn[part].at[pl.ds(0, 4 * share)], block)
            groups[part, block[1]] = mail.group(four, four, here.to_x)
            first_hop.setdefault(part, []).append(groups[part, block[1]][2])
        mail.send(source(block, at), lanes(to, block), target, *groups[part, block[1]][:2])

    def ship_all(part, i, axes=(0, 1)):
        for block in blocks[part]:
            for axis in axes:
                ship(part, i, block, axis)

    step = 32

    def relay(part):
        slot = slot_of[part]
        for copy in staged[part]:
            copy.wait()
        for copy in first_hop[part]:
            copy.wait_recv()
        base = (1 - y) * share

        @pl.loop(0, share // step)
        def _(index):
            at = pl.ds(pl.multiple_of(base + index * step, step), step)
            mine = stage_a[slot, at, :].astype(F32) + land_a[part, at, :].astype(F32)
            stage_a[slot, at, :] = mine.astype(BF16)
            at = pl.ds(mul(index, step), step)
            mine = stage_b[slot, 1 - x, at, :].astype(F32) + land_b[part, 1 - x, at, :].astype(F32)
            stage_b[slot, 1 - x, at, :] = mine.astype(BF16)

        a_src = stage_a.at[slot, pl.ds(pl.multiple_of(base, share), share)]
        second_hop[part] = (
            mail.send(a_src, last_a.at[part], here.to_y),
            mail.send(stage_b.at[slot, 1 - x], last_b.at[part], here.to_x),
        )

    def settle(part):
        slot = slot_of[part]
        slope_here[part].wait()
        for copy in second_hop[part]:
            copy.wait_recv()
        base = y * share

        @pl.loop(0, share // step)
        def _(index):
            flat = pl.ds(mul(index, step), step)
            at = pl.ds(pl.multiple_of(base + index * step, step), step)
            mine = stage_a[slot, at, :].astype(F32) + land_a[part, at, :].astype(F32)
            mine = mine + last_a[part, flat, :].astype(F32)
            stage_a[slot, at, :] = (mine * slopes[0, flat, :].astype(F32)).astype(BF16)
            mine = stage_b[slot, x, flat, :].astype(F32) + land_b[part, x, flat, :].astype(F32)
            mine = mine + last_b[part, flat, :].astype(F32)
            stage_b[slot, x, flat, :] = (mine * slopes[1, flat, :].astype(F32)).astype(BF16)

        a_ref = stage_a.at[slot, pl.ds(pl.multiple_of(base, share), share)]
        b_ref = stage_b.at[slot, x]
        out = out_ffn[part].at[:, mine_cols]
        give_b = mail.make(b_ref, out, here.to_core)
        give_a = mail.make(a_ref, out, here.to_core, mail.n_send - 1, mail.n_recv - 1)
        keep_a = pltpu.make_async_copy(a_ref, out, local_sem.at[local_count[0]])
        keep_b = pltpu.make_async_copy(b_ref, out, local_sem.at[local_count[0]])
        local_count[0] += 1

        @pl.when(core == 0)
        def _():
            keep_a.start()
            give_b.start()

        @pl.when(core == 1)
        def _():
            keep_b.start()
            give_a.start()

        ending.append((keep_a, give_b))
        finished[part] = ending[-1]

    finished = {}

    def restage(part, earlier):
        keep, give = finished[earlier]
        keep.wait()
        for copy in (give, *second_hop[earlier]):
            mail.finish(copy)
        staged[part] = stage(part)

    count = width // small.shape[1]
    gain_one = row_of(small, 8, count)
    gain_two = row_of(small, 8 + count, count)

    gain_part[...] = jnp.zeros_like(gain_part)

    def into_resid(sub, spot, summed):
        normed, inverse = forward_norm(x1[spot, :])
        gain_part[1:2, :] += jnp.sum(summed * normed, axis=0, keepdims=True)
        grad = cot_chunk[spot, :].astype(F32) + backward_norm(summed * gain_two, normed, inverse)
        grad_resid[spot, :] = grad
        return grad.astype(BF16)

    def into_mixed(sub, spot, summed):
        return (x1[spot, :] + summed).astype(BF16)

    def into_tokens(sub, spot, summed):
        normed, inverse = forward_norm(token_chunk[spot, :].astype(F32))
        gain_part[0:1, :] += jnp.sum(summed * normed, axis=0, keepdims=True)
        grad = grad_resid[spot, :] + backward_norm(summed * gain_one, normed, inverse)
        return grad.astype(BF16)

    line = Line(here, partial, grad_resid_b, land, total, (line_send, line_recv), into_resid, subs=BACK_SUBS)
    ffn_line = Line(
        here, partial_ffn, mixed_out, land_ffn, total, (ffn_send, ffn_recv), into_mixed, own_ffn, subs=BACK_SUBS
    )
    tok_line = Line(
        here, partial, tokens_out, land, total, (line_send, line_recv), into_tokens, own_tokens, subs=BACK_SUBS
    )

    for i in (0, 1):
        for axis in (0, 1):
            ship(1, i, blocks[1][0], axis)
    for copy in (get_partial, get_x1, get_cot, get_tokens):
        copy.wait()

    def join(target, came, first=0, count=rows):
        @pl.loop(0, count // step)
        def _(index):
            at = pl.ds(pl.multiple_of(first + index * step, step), step)
            target[at, :] = (target[at, :].astype(F32) + came[at, :].astype(F32)).astype(BF16)

    def join_chunk(number):
        back_copies[number].wait_recv()
        join(partial, partial_ffn, chunks[number], rows // 4)

    join_chunk(0)

    quarter, n_heads = 32, n_query // HD
    block = 4 * quarter
    number_rows(segments, y, keys)
    grad_kv[...] = jnp.zeros_like(grad_kv)

    def stacked(value):
        return jnp.concatenate([value[:, i * HD : (i + 1) * HD] for i in range(n_heads)], axis=0)

    def back_through(query_b, grad_o, allowed):
        probs, bent = soft_probs(query_b, kv, allowed)
        grad_probs = against(kv[:, HD:], grad_o)
        row_dot = jnp.sum(probs * grad_probs, axis=0, keepdims=True)
        grad_raw = probs * (grad_probs - row_dot) * (1.0 - bent * bent) * HD ** (-0.5)
        grad_raw = grad_raw.astype(BF16)
        grad_kv[:, :HD] += natural(grad_raw, query_b)
        grad_kv[:, HD:] += natural(probs.astype(BF16), grad_o)
        return inner_rows(grad_raw, kv[:, :HD]).astype(BF16)

    def attend_back(sub):
        firsts = [j * (rows // 4) + sub * quarter for j in range(4)]
        spots = [slice(at, at + quarter) for at in firsts]

        def take(ref):
            return jnp.concatenate([ref[spot, :] for spot in spots], axis=0)

        index = lax.broadcasted_iota(jnp.int32, (1, block), 1)
        chunk = sum((index >= j * quarter).astype(jnp.int32) for j in (1, 2, 3))
        position = y * rows + index + chunk * (rows // 4 - quarter) + sub * quarter
        numbers = jnp.transpose(take(keys))[0:1, :]
        allowed = visible(keys, beside(numbers, n_heads), beside(position, n_heads), y)
        grad_o = natural(take(grad_resid_b), ea[:, n_in:]).astype(BF16)
        if sub == 0:
            edge_send[...] = grad_o[:EXTRA]
            edge_copies.append(mail.send(edge_send, edge_land, here.to_y))
            theirs = (lax.broadcasted_iota(jnp.int32, (block, 1), 0) == 0) & (y == 1)
            grad_o = jnp.where(theirs, jnp.zeros_like(grad_o), grad_o)
        grad_q = back_through(stacked(take(query)), stacked(grad_o), allowed)
        for i in range(n_heads):
            for j, spot in enumerate(spots):
                at = i * block + j * quarter
                grad_in[spot, i * HD : (i + 1) * HD] = grad_q[at : at + quarter]

    edge_copies = []

    def edge_back():
        edge_copies[0].wait_recv()
        ours = (lax.broadcasted_iota(jnp.int32, (EXTRA, 1), 0) == 0) & (y == 0)
        grad_o = jnp.where(ours, edge_land[...], jnp.zeros_like(edge_land))
        allowed = extra_visible(keys, y, n_heads)
        grad_q = back_through(stacked(query[rows:, :]), stacked(grad_o), allowed)
        for i in range(n_heads):
            row_send[:, i * HD : (i + 1) * HD] = grad_q[i * EXTRA : (i + 1) * EXTRA]
        row_send[:, n_query:] = grad_kv[rows:, :].astype(BF16)

    ffn_ticks = ffn_line.ticks()
    plan, count = list(OUTPUT_PLAN), itertools.count(2)

    def output_wave(place):
        while plan and plan[0] <= place:
            plan.pop(0)
            next(ffn_ticks, None)

    later = []
    for tick in line.ticks():
        if tick == 0:
            join_chunk(1)
        if tick == 1:
            join_chunk(2)
            join_chunk(3)
            get_ffn = fetch(ffn_in.at[pl.ds(0, rows)], partial_ffn)
            strips(1, 0, n_strips // 2)
        if tick == 2:
            strips(1, n_strips // 2, n_strips)
            for i in (0, 1):
                for axis in (0, 1):
                    ship(1, i, blocks[1][1], axis)
        if tick in (3, 4, 5):
            strips(2, 3 * tick - 9, 3 * tick - 6)
        if tick == 5:
            ship_all(2, 0)
            ship_all(2, 1)
        if tick in (6, 7):
            strips(0, 5 * tick - 30, min(5 * tick - 25, n_strips))
        if tick == 5:
            get_ffn.wait()
            ffn_copy.wait_recv()
            join(partial_ffn, h1)
            get_h1 = fetch(h1_in, h1)
        if tick == 7:
            later = [
                fetch(e_attn, ea),
                fetch(query_in, query),
                fetch(kv_in, kv),
                fetch(heads_in, heads),
            ]
        output_wave(tick)
        if tick == 9:
            get_slopes(1)
            relay(1)
        if tick == 11:
            ship_all(0, 0, (0,))
        if tick == 8:
            for copy in later:
                copy.wait()
        if tick in (8, 10, 12, 13):
            attend_back((8, 10, 12, 13).index(tick))
    output_wave(14)
    line.close()
    edge_back()
    row_copy = mail.send(row_send, row_land, here.to_y)
    ship_all(0, 0, (1,))
    ship_all(0, 1)
    output_wave(15)
    row_copy.wait_recv()
    at = pl.ds(edge(y, rows), EXTRA)
    grad_in[at, :n_query] = (grad_in[at, :n_query].astype(F32) + row_land[:, :n_query].astype(F32)).astype(BF16)
    grad_kv[at, :] += row_land[:, n_query:].astype(F32)
    grad_in[:, n_query:] = grad_kv[:rows, :].astype(BF16)

    @pl.loop(0, width // tile)
    def _(index):
        cols = pl.ds(mul(index, tile), tile)
        partial[:, cols] = against(grad_in[...], ea[cols, :n_in]).astype(BF16)

    tok_ticks = tok_line.ticks()
    next(tok_ticks, None)
    output_wave(17)

    @pl.loop(0, width // tile)
    def _(index):
        cols = pl.ds(mul(index, tile), tile)
        ea[cols, n_in:] = inner_rows(grad_resid_b[:, cols], heads[...]).astype(BF16)

    next(tok_ticks, None)
    output_wave(18)
    relay(2)
    settle(1)
    get_slopes(2)
    restage(0, 1)
    get_h1.wait()

    @pl.loop(0, width // tile)
    def _(index):
        cols = pl.ds(mul(index, tile), tile)
        ea[cols, :n_in] = inner_rows(h1[:, cols], grad_in[...]).astype(BF16)

    def pair_rows(sx, score):
        return pl.ds(pl.multiple_of(here.slot(sx, score, 0) * share, 2 * share), 2 * share)

    core_copies = [
        mail.send(ea.at[pair_rows(i, 1 - core)], core_land.at[i], here.to_core) for i in (0, 1)
    ]
    for _ in range(2):
        next(tok_ticks, None)
        output_wave(17 + next(count))
    for copy in core_copies:
        copy.wait_recv()

    @pl.loop(0, 2 * share // step)
    def _(index):
        for i in (0, 1):
            at = pl.ds(
                pl.multiple_of(here.slot(i, core, 0) * share + index * step, step), step
            )
            flat = pl.ds(mul(index, step), step)
            ea[at, :] = (ea[at, :].astype(F32) + core_land[i, flat, :].astype(F32)).astype(BF16)

    slope_attn = core_land.at[0, pl.ds(0, share)]
    get_slope_attn = fetch(slope_attn_in, slope_attn)
    cut = attn_a.shape[1]
    left, right = pl.ds(0, cut), pl.ds(cut, n_attn - cut)

    def one_rows(sx, sy):
        return pl.ds(pl.multiple_of(here.slot(sx, core, sy) * share, share), share)

    attn_first = [mail.send(ea.at[pair_rows(1 - x, core), left], attn_a, here.to_x)]
    for i in (0, 1):
        attn_first.append(mail.send(ea.at[one_rows(i, 1 - y), right], attn_b.at[i], here.to_y))
    for _ in range(2):
        next(tok_ticks, None)
        output_wave(17 + next(count))
    relay(0)
    settle(2)
    get_slopes(0)
    for _ in range(3):
        next(tok_ticks, None)
        output_wave(17 + next(count))

    def gain_steps():
        rounds = (plane, [near_target], [far_target])
        mine, at = gain_part, 0
        for number, targets in enumerate(rounds):
            places = gain_land.at[pl.ds(at, len(targets))]
            send_at, recv_at, came = mail.group(places, places, here.to_core)
            for i, target in enumerate(targets):
                mail.send(mine, gain_land.at[at + i], target, send_at, recv_at)
            yield
            came.wait_recv()
            added = mine[...]
            for i in range(len(targets)):
                added = added + gain_land[at + i]
            gain_sum[number] = added
            mine, at = gain_sum.at[number], at + len(targets)

    gain_waves = gain_steps()
    for copy in attn_first:
        copy.wait_recv()

    @pl.loop(0, share // step)
    def _(index):
        flat = pl.ds(mul(index, step), step)
        at = pl.ds(pl.multiple_of(here.slot(x, core, 1 - y) * share + index * step, step), step)
        came = pl.ds(pl.multiple_of((1 - y) * share + index * step, step), step)
        ea[at, left] = (ea[at, left].astype(F32) + attn_a[came, :].astype(F32)).astype(BF16)
        at = pl.ds(pl.multiple_of(here.slot(1 - x, core, y) * share + index * step, step), step)
        ea[at, right] = (
            ea[at, right].astype(F32) + attn_b[1 - x, flat, :].astype(F32)
        ).astype(BF16)

    attn_second = [
        mail.send(ea.at[one_rows(x, 1 - y), left], attn_last_a, here.to_y),
        mail.send(ea.at[one_rows(1 - x, y), right], attn_last_b, here.to_x),
    ]
    def settle_attn():
        get_slope_attn.wait()
        for copy in attn_second:
            copy.wait_recv()

        @pl.loop(0, share // step)
        def _(index):
            flat = pl.ds(mul(index, step), step)
            at = pl.ds(pl.multiple_of(here.slot(x, core, y) * share + index * step, step), step)
            came = pl.ds(pl.multiple_of(y * share + index * step, step), step)
            mine = ea[at, left].astype(F32) + attn_a[came, :].astype(F32)
            mine = mine + attn_last_a[flat, :].astype(F32)
            ea[at, left] = (mine * slope_attn[flat, left].astype(F32)).astype(BF16)
            mine = ea[at, right].astype(F32) + attn_b[x, flat, :].astype(F32)
            mine = mine + attn_last_b[flat, :].astype(F32)
            ea[at, right] = (mine * slope_attn[flat, right].astype(F32)).astype(BF16)

        ends.append(fetch(ea.at[one_rows(x, y)], out_attn))

    ends = []
    for tick in tok_ticks:
        output_wave(17 + next(count))
        if tick > 9:
            next(gain_waves, None)
        if tick == 10:
            ends.append(fetch(own_ffn, mixed_out.at[chunk_rows]))
            ends.append(fetch(own_tokens, tokens_out.at[chunk_rows]))
        if tick == 11:
            settle(0)
        if tick == 12:
            settle_attn()
    for tick in ffn_ticks:
        pass
    for _ in gain_waves:
        pass
    ends.append(fetch(gain_sum.at[2], gains_out))
    ffn_line.close()
    tok_line.close()
    for keep, give in ending:
        give.wait_recv()
    for keep, give in ending[1:]:
        keep.wait()
    mail.close()
    for copy in ends:
        copy.wait()


def back(given, x1, small, attn, tokens, cotangent, segments, slope_ffn, slope_attn):
    rows, width = tokens.shape
    half = given[2].shape[1]
    share = width // 8
    e_attn, query, kv = attn[0], attn[1], attn[2]
    n_attn, n_query, n_kv = e_attn.shape[1], query.shape[1], kv.shape[1]
    cut = 3 * n_attn // 4
    chunk = rows // 4
    shapes = [
        *[((share, 2 * half), BF16)] * 3,
        ((share, n_attn), BF16),
        ((rows, width), BF16),
        ((rows, width), BF16),
        ((2, width), F32),
        *[((width, half), BF16)] * 3,
    ]
    in_vmem = pl.BlockSpec(memory_space=pltpu.VMEM)
    anywhere = pl.BlockSpec(memory_space=pl.ANY)
    scratch = [
        pltpu.VMEM((2, 2 * share, half), BF16),
        pltpu.VMEM((2, 2, share, half), BF16),
        pltpu.VMEM((3, 2 * share, half), BF16),
        pltpu.VMEM((3, 2, share, half), BF16),
        pltpu.VMEM((3, share, half), BF16),
        pltpu.VMEM((3, share, half), BF16),
        pltpu.VMEM((2, share, half), BF16),
        pltpu.VMEM((rows, width), BF16),
        pltpu.VMEM((rows, width), BF16),
        pltpu.VMEM((rows, width), BF16),
        pltpu.VMEM((chunk, width), BF16),
        pltpu.VMEM((chunk, width), BF16),
        pltpu.VMEM((2, 3, chunk, width), BF16),
        pltpu.VMEM((2, 3, chunk, width), BF16),
        pltpu.VMEM((chunk // BACK_SUBS, width), F32),
        pltpu.VMEM((width, n_attn), BF16),
        pltpu.VMEM((2, 2 * share, n_attn), BF16),
        pltpu.VMEM((2 * share, cut), BF16),
        pltpu.VMEM((2, share, n_attn - cut), BF16),
        pltpu.VMEM((share, cut), BF16),
        pltpu.VMEM((share, n_attn - cut), BF16),
        pltpu.VMEM((rows + EXTRA, n_query), BF16),
        pltpu.VMEM((rows + EXTRA, n_kv), BF16),
        pltpu.VMEM((rows, n_query), BF16),
        pltpu.VMEM((rows, width), BF16),
        pltpu.VMEM((rows + EXTRA, 128), F32),
        pltpu.VMEM((rows, n_query + n_kv), BF16),
        pltpu.VMEM((rows + EXTRA, n_kv), F32),
        pltpu.VMEM((EXTRA, n_query), BF16),
        pltpu.VMEM((EXTRA, n_query), BF16),
        pltpu.VMEM((EXTRA, n_query + n_kv), BF16),
        pltpu.VMEM((EXTRA, n_query + n_kv), BF16),
        pltpu.VMEM((chunk, width), F32),
        pltpu.VMEM((chunk, width), F32),
        pltpu.VMEM((chunk, width), BF16),
        pltpu.VMEM((chunk, width), BF16),
        pltpu.VMEM((2, width), F32),
        pltpu.VMEM((3, 2, width), F32),
        pltpu.VMEM((9, 2, width), F32),
        *line_sems(BACK_SUBS),
        *line_sems(BACK_SUBS),
        pltpu.SemaphoreType.DMA((3, 2)),
        pltpu.SemaphoreType.DMA((36,)),
        pltpu.SemaphoreType.DMA((31,)),
        pltpu.SemaphoreType.DMA((31,)),
    ]
    places = [anywhere] * 9 + [in_vmem] + [anywhere] * 7 + [in_vmem] + [anywhere] * 2
    return pl.pallas_call(
        back_kernel,
        out_shape=[jax.ShapeDtypeStruct(s, d) for s, d in shapes],
        in_specs=places,
        out_specs=[anywhere] * len(shapes),
        scratch_shapes=scratch,
        compiler_params=pltpu.CompilerParams(
            collective_id=1, has_side_effects=True, vmem_limit_bytes=VMEM_BYTES
        ),
        cost_estimate=pl.CostEstimate(
            flops=26 * 10**9, bytes_accessed=120 * 10**6, transcendentals=4 * 10**6
        ),
        name="back",
    )(*given, x1, small, *attn, tokens, cotangent, segments, slope_ffn, slope_attn)


def end_kernel(
    mixed_in,
    tokens_in,
    gate_in,
    up_in,
    attn_in,
    down_in,
    small_in,
    peaks_in,
    gains_in,
    mixed,
    tokens,
    query,
    key,
    value,
    out,
    gate,
    up,
    down,
    attn_out,
    kv_out,
    ffn_out,
    one_out,
    two_out,
    small,
    peaks,
    gain_sum,
    attn_scales,
    kv_scales,
    ffn_scales,
    gain_one,
    gain_two,
    tall_in,
    tall_out,
    wide_in,
    wide_out,
    attn_b,
    attn_f,
    down_b,
    down_f,
    turned,
    in_sem,
    out_sem,
):
    n_query, n_key = query.shape[1], key.shape[1]
    n_in = n_query + 2 * n_key
    step = 32
    reads = [
        (mixed_in, tall_in.at[0]),
        (tokens_in, tall_in.at[1]),
        (down_in, down_b),
        (gate_in, wide_in.at[0]),
        (up_in, wide_in.at[1]),
        (attn_in, attn_b),
        (small_in, small),
        (peaks_in, peaks),
        (gains_in, gain_sum),
    ]
    reads = [pltpu.make_async_copy(a, b, in_sem.at[i]) for i, (a, b) in enumerate(reads)]
    for copy in reads:
        copy.start()
    writes = []

    def write(src, dst):
        copy = pltpu.make_async_copy(src, dst, out_sem.at[len(writes)])
        copy.start()
        writes.append(copy)

    def widen(src, dst):
        @pl.loop(0, src.shape[0] // step)
        def _(index):
            at = pl.ds(mul(index, step), step)
            dst[at, :] = src[at, :].astype(F32)

    for i, target in enumerate((mixed, tokens)):
        reads[i].wait()
        widen(tall_in.at[i], tall_out.at[i])
        write(tall_out.at[i], target)
    for copy in reads[6:]:
        copy.wait()
    piece = small.shape[1]
    for row, first in enumerate((0, n_in)):
        for i in range(n_query // piece):
            at = first // piece + i
            attn_scales[row : row + 1, i * piece : (i + 1) * piece] = small[at : at + 1, :]
    for row in (0, 1):
        for i in range(n_key // piece):
            at = (n_query + row * n_key) // piece + i
            kv_scales[row : row + 1, i * piece : (i + 1) * piece] = small[at : at + 1, :]
    ffn_scales[...] = peaks[0:3, :]
    share, width = gain_one.shape[0], gain_sum.shape[1]
    slot = lax.axis_index("dp") * 2 + lax.axis_index("seq")
    turned[...] = jnp.zeros_like(turned)
    turned[0:2, :] = gain_sum[...]
    turned[...] = pltpu.roll(turned[...], lax.rem(width - slot * share, width), 1)
    gain_one[...] = turned[0, :share]
    gain_two[...] = turned[1, :share]
    for src, dst in (
        (attn_scales, attn_out),
        (kv_scales, kv_out),
        (ffn_scales, ffn_out),
        (gain_one, one_out),
        (gain_two, two_out),
    ):
        write(src, dst)
    reads[2].wait()
    widen(down_b, down_f)
    write(down_f, down)
    for i, target in enumerate((gate, up)):
        reads[3 + i].wait()
        widen(wide_in.at[i], wide_out.at[i])
        write(wide_out.at[i], target)
    reads[5].wait()
    widen(attn_b, attn_f)
    write(attn_f.at[:, pl.ds(0, n_query)], query)
    write(attn_f.at[:, pl.ds(n_query, n_key)], key)
    write(attn_f.at[:, pl.ds(n_query + n_key, n_key)], value)
    write(attn_f.at[:, pl.ds(n_in, n_query)], out)
    for copy in writes:
        copy.wait()


def end(mixed_b, tokens_b, sum_gate, sum_up, sum_attn, sum_down, small, peaks, gain_sum, n_query):
    rows, width = mixed_b.shape
    share, hidden = sum_gate.shape
    n_attn = sum_attn.shape[1]
    n_key = (n_attn - 2 * n_query) // 2
    shapes = [
        (rows, width),
        (rows, width),
        (share, n_query),
        (share, n_key),
        (share, n_key),
        (share, n_query),
        (share, hidden),
        (share, hidden),
        (share, hidden),
        (2, n_query),
        (2, n_key),
        (3, hidden),
        (share,),
        (share,),
    ]
    anywhere = pl.BlockSpec(memory_space=pl.ANY)
    return pl.pallas_call(
        end_kernel,
        out_shape=[jax.ShapeDtypeStruct(s, F32) for s in shapes],
        in_specs=[anywhere] * 9,
        out_specs=[anywhere] * 14,
        scratch_shapes=[
            *(pltpu.VMEM(a.shape, F32) for a in (small, peaks, gain_sum)),
            *(pltpu.VMEM(shape, F32) for shape in shapes[9:]),
            pltpu.VMEM((2, rows, width), BF16),
            pltpu.VMEM((2, rows, width), F32),
            pltpu.VMEM((2, share, hidden), BF16),
            pltpu.VMEM((2, share, hidden), F32),
            pltpu.VMEM((share, n_attn), BF16),
            pltpu.VMEM((share, n_attn), F32),
            pltpu.VMEM((share, hidden), BF16),
            pltpu.VMEM((share, hidden), F32),
            pltpu.VMEM((8, width), F32),
            pltpu.SemaphoreType.DMA((9,)),
            pltpu.SemaphoreType.DMA((14,)),
        ],
        compiler_params=pltpu.CompilerParams(vmem_limit_bytes=VMEM_BYTES),
        cost_estimate=pl.CostEstimate(flops=0, bytes_accessed=29 * 10**6, transcendentals=0),
        name="end",
    )(mixed_b, tokens_b, sum_gate, sum_up, sum_attn, sum_down, small, peaks, gain_sum)


def paired_block(
    tokens,
    gain_attn,
    w_query,
    w_key,
    w_value,
    w_out,
    gain_ffn,
    w_gate,
    w_up,
    w_down,
    width_pick,
    segments,
    cotangent,
):
    n_query = w_query.shape[1]
    weights = (w_query, w_key, w_value, w_out.T, w_down.T, w_gate, w_up)
    (
        e_attn,
        hidden_two,
        resid,
        query_b,
        kv,
        heads_b,
        hidden_one,
        cot_other,
        mixed_in,
        grad_gate_b,
        grad_up_b,
        back_part,
        ffn_part,
        slope_ffn,
        slope_attn,
        small,
        peaks,
        early,
    ) = front(width_pick, weights, gain_attn, gain_ffn, tokens, cotangent, segments)
    sum_down, sum_gate, sum_up, sum_attn, mixed_b, tokens_b, gain_sum, _, _, _ = back(
        (back_part, ffn_part, mixed_in, grad_gate_b, grad_up_b, hidden_two, cot_other, early),
        resid,
        small,
        (e_attn, query_b, kv, heads_b, hidden_one),
        tokens,
        cotangent,
        segments,
        slope_ffn,
        slope_attn,
    )
    mixed, grad_tokens, g_query, g_key, g_value, g_out, g_gate, g_up, g_down, *scales, gain_one, gain_two = end(
        mixed_b, tokens_b, sum_gate, sum_up, sum_attn, sum_down, small, peaks, gain_sum, n_query
    )
    return (
        mixed,
        grad_tokens,
        g_query,
        g_key,
        g_value,
        g_out.T,
        g_gate,
        g_up,
        g_down.T,
        gain_one,
        gain_two,
        *scales,
    )


def solution(mesh):
    in_specs = (
        P(("dp", "seq"), None),
        P(("dp", "seq")),
        P(("dp", "seq"), "mp"),
        P(("dp", "seq"), "mp"),
        P(("dp", "seq"), "mp"),
        P("mp", ("dp", "seq")),
        P(("dp", "seq")),
        P(("dp", "seq"), "mp"),
        P(("dp", "seq"), "mp"),
        P("mp", ("dp", "seq")),
        P(),
        P("dp", None),
        P(("dp", "seq"), None),
    )
    out_specs = (
        P(("dp", "seq"), None),
        P(("dp", "seq"), None),
        P(("dp", "seq"), "mp"),
        P(("dp", "seq"), "mp"),
        P(("dp", "seq"), "mp"),
        P("mp", ("dp", "seq")),
        P(("dp", "seq"), "mp"),
        P(("dp", "seq"), "mp"),
        P("mp", ("dp", "seq")),
        P(("dp", "seq")),
        P(("dp", "seq")),
        P(None, "mp"),
        P(None, "mp"),
        P(None, "mp"),
    )
    shape = dict(mesh.shape)
    paired = shape["dp"] == 4 and shape["seq"] == 2 and shape["mp"] == 4
    block = paired_block if paired else on_device
    return jax.shard_map(
        block, mesh=mesh, in_specs=in_specs, out_specs=out_specs, check_vma=False
    )
```

```python
import itertools

import jax
import jax.numpy as jnp
from jax import lax
from jax.experimental import pallas as pl
from jax.experimental.pallas import tpu as pltpu
from jax.sharding import PartitionSpec as P

HQ = 8
HK = 4
HD = 256


EPSILON = 1e-06
SOFTCAP = 50.0


def width_levels(width_pick):
    return jnp.where(width_pick == 0, 1.0, jnp.where(width_pick == 1, 0.5, 0.25)).astype(
        jnp.float32
    )


def bounded(weight, bound):
    return (bound * jnp.tanh(weight.astype(jnp.float32) / bound)).astype(jnp.bfloat16)


def bound_slope(weight, bound):
    tangent = jnp.tanh(weight.astype(jnp.float32) / bound)
    return 1.0 - tangent * tangent


def channel_peak(weight, along):
    return jnp.max(jnp.abs(weight.astype(jnp.float32)), axis=along)


def inner_rows(left, right):
    return lax.dot_general(
        left, right, (((0,), (0,)), ((), ())), preferred_element_type=jnp.float32
    )


def against(left, weight):
    return lax.dot_general(
        left, weight, (((1,), (1,)), ((), ())), preferred_element_type=jnp.float32
    )


def forward_norm(values):
    inverse = lax.rsqrt(jnp.mean(values * values, axis=-1, keepdims=True) + EPSILON)
    return (values * inverse, inverse)


def backward_norm(grad_normed, normed, inverse):
    return inverse * (grad_normed - normed * jnp.mean(grad_normed * normed, axis=-1, keepdims=True))


def gelu_tanh(values):
    return jax.nn.gelu(values, approximate=True)


def on_device(
    tokens,
    gain_attn,
    w_query,
    w_key,
    w_value,
    w_out,
    gain_ffn,
    w_gate,
    w_up,
    w_down,
    width_pick,
    segments,
    cotangent,
):
    level_of = width_levels(width_pick)
    peaks = (
        lax.pmax(channel_peak(w_query, 0).astype(jnp.bfloat16), ("dp", "seq")).astype(jnp.float32),
        lax.pmax(channel_peak(w_key, 0).astype(jnp.bfloat16), ("dp", "seq")).astype(jnp.float32),
        lax.pmax(channel_peak(w_value, 0).astype(jnp.bfloat16), ("dp", "seq")).astype(jnp.float32),
        lax.pmax(channel_peak(w_out, 1).astype(jnp.bfloat16), ("dp", "seq")).astype(jnp.float32),
        lax.pmax(channel_peak(w_gate, 0).astype(jnp.bfloat16), ("dp", "seq")).astype(jnp.float32),
        lax.pmax(channel_peak(w_up, 0).astype(jnp.bfloat16), ("dp", "seq")).astype(jnp.float32),
        lax.pmax(channel_peak(w_down, 1).astype(jnp.bfloat16), ("dp", "seq")).astype(jnp.float32),
    )
    peak_query, peak_key, peak_value, peak_out, peak_gate, peak_up, peak_down = peaks
    bound_query = peak_query[None, :] * level_of[0]
    bound_key = peak_key[None, :] * level_of[1]
    bound_value = peak_value[None, :] * level_of[2]
    bound_out = peak_out[:, None] * level_of[3]
    bound_gate = peak_gate[None, :] * level_of[4]
    bound_up = peak_up[None, :] * level_of[5]
    bound_down = peak_down[:, None] * level_of[6]
    fetched = (
        lax.all_gather(w_query, ("dp", "seq"), axis=0, tiled=True),
        lax.all_gather(w_key, ("dp", "seq"), axis=0, tiled=True),
        lax.all_gather(w_value, ("dp", "seq"), axis=0, tiled=True),
        lax.all_gather(gain_attn, ("dp", "seq"), axis=0, tiled=True),
        lax.all_gather(w_gate, ("dp", "seq"), axis=0, tiled=True),
        lax.all_gather(w_up, ("dp", "seq"), axis=0, tiled=True),
        lax.all_gather(gain_ffn, ("dp", "seq"), axis=0, tiled=True),
    )
    full_query, full_key, full_value, full_gain_one = (
        fetched[0],
        fetched[1],
        fetched[2],
        fetched[3],
    )
    later_rows = (fetched[4], fetched[5], fetched[6])
    columns = (
        lax.all_gather(w_out, ("dp", "seq"), axis=1, tiled=True),
        lax.all_gather(w_down, ("dp", "seq"), axis=1, tiled=True),
    )
    eff_query = bounded(full_query, bound_query)
    eff_key = bounded(full_key, bound_key)
    eff_value = bounded(full_value, bound_value)
    eff_out = bounded(columns[0], bound_out)
    eff_down = bounded(columns[1], bound_down)
    gain_one = full_gain_one.astype(jnp.float32)
    mp_count = lax.axis_size("mp")
    local_kv = HK // mp_count
    ratio = HQ // HK
    rows_here = tokens.shape[0]
    seg_row = segments[0]
    group = seg_row.shape[0]
    start = lax.axis_index("seq") * rows_here
    query_pos = start + jnp.arange(rows_here, dtype=jnp.int32)
    key_pos = jnp.arange(group, dtype=jnp.int32)
    seg_query = lax.dynamic_slice_in_dim(seg_row, start, rows_here)
    allowed = (seg_query[:, None] == seg_row[None, :]) & (key_pos[None, :] <= query_pos[:, None])
    scale = HD ** (-0.5)
    tokens_full = tokens.astype(jnp.float32)
    normed_one, inverse_one = forward_norm(tokens_full)
    hidden_one = (normed_one * gain_one).astype(jnp.bfloat16)
    query_b = jnp.dot(hidden_one, eff_query, preferred_element_type=jnp.float32).astype(
        jnp.bfloat16
    )
    key_b = jnp.dot(hidden_one, eff_key, preferred_element_type=jnp.float32).astype(jnp.bfloat16)
    value_b = jnp.dot(hidden_one, eff_value, preferred_element_type=jnp.float32).astype(
        jnp.bfloat16
    )
    key_all, value_all = (
        lax.all_gather(key_b, "seq", axis=0, tiled=True),
        lax.all_gather(value_b, "seq", axis=0, tiled=True),
    )
    query_heads = query_b.reshape(rows_here, local_kv, ratio, HD)
    key_heads = key_all.reshape(group, local_kv, HD)
    value_heads = value_all.reshape(group, local_kv, HD)

    def logits():
        raw = jnp.einsum(
            "tjrd,kjd->jrtk", query_heads, key_heads, preferred_element_type=jnp.float32
        )
        bent = jnp.tanh(raw * scale / SOFTCAP)
        capped = jnp.where(allowed[None, None], SOFTCAP * bent, -1e30)
        return (capped, bent)

    capped, bent = logits()
    largest = jnp.max(capped, axis=-1, keepdims=True)
    weights = jnp.exp(capped - largest)
    totals = jnp.sum(weights, axis=-1, keepdims=True)
    log_total = largest + jnp.log(totals)
    probs_b = (weights / totals).astype(jnp.bfloat16)
    heads_b = (
        jnp.einsum("jrtk,kjd->tjrd", probs_b, value_heads, preferred_element_type=jnp.float32)
        .reshape(rows_here, -1)
        .astype(jnp.bfloat16)
    )
    attn_total = lax.psum(jnp.dot(heads_b, eff_out, preferred_element_type=jnp.float32), "mp")
    resid = tokens_full + attn_total
    eff_gate = bounded(later_rows[0], bound_gate)
    eff_up = bounded(later_rows[1], bound_up)
    gain_two = later_rows[2].astype(jnp.float32)
    normed_two, inverse_two = forward_norm(resid)
    hidden_two = (normed_two * gain_two).astype(jnp.bfloat16)
    gate_full = jnp.dot(hidden_two, eff_gate, preferred_element_type=jnp.float32)
    upper_full = jnp.dot(hidden_two, eff_up, preferred_element_type=jnp.float32)
    gelu_value, gelu_back = jax.vjp(gelu_tanh, gate_full)
    mixed_in = (gelu_value * upper_full).astype(jnp.bfloat16)
    ffn_total = lax.psum(
        jnp.dot(mixed_in, eff_down, preferred_element_type=jnp.float32).astype(jnp.bfloat16), "mp"
    ).astype(jnp.float32)
    mixed = resid + ffn_total
    grad_mixed_in = against(cotangent, eff_down)
    grad_down_eff = inner_rows(mixed_in, cotangent)
    grad_gate_b = gelu_back(grad_mixed_in * upper_full)[0].astype(jnp.bfloat16)
    grad_upper_b = (grad_mixed_in * gelu_value).astype(jnp.bfloat16)
    grad_hidden_two = lax.psum(against(grad_gate_b, eff_gate) + against(grad_upper_b, eff_up), "mp")
    gain_two_part = jnp.sum(grad_hidden_two * normed_two, axis=0)
    grad_resid = cotangent.astype(jnp.float32) + backward_norm(
        grad_hidden_two * gain_two, normed_two, inverse_two
    )
    grad_gate_eff = inner_rows(hidden_two, grad_gate_b)
    grad_up_eff = inner_rows(hidden_two, grad_upper_b)
    grad_resid_b = grad_resid.astype(jnp.bfloat16)
    grad_heads_b = against(grad_resid_b, eff_out).astype(jnp.bfloat16)
    grad_out_eff = inner_rows(heads_b, grad_resid_b)
    grad_heads = grad_heads_b.reshape(rows_here, local_kv, ratio, HD)
    capped_again, bent_again = logits()
    probs = jnp.exp(capped_again - log_total)
    probs_again = probs.astype(jnp.bfloat16)
    grad_probs = jnp.einsum(
        "tjrd,kjd->jrtk", grad_heads, value_heads, preferred_element_type=jnp.float32
    )
    row_dot = jnp.sum(probs * grad_probs, axis=-1, keepdims=True)
    grad_raw_b = (probs * (grad_probs - row_dot) * (1.0 - bent_again * bent_again) * scale).astype(
        jnp.bfloat16
    )
    grad_query_b = (
        jnp.einsum("jrtk,kjd->tjrd", grad_raw_b, key_heads, preferred_element_type=jnp.float32)
        .reshape(rows_here, -1)
        .astype(jnp.bfloat16)
    )
    grad_key_full = jnp.einsum(
        "jrtk,tjrd->kjd", grad_raw_b, query_heads, preferred_element_type=jnp.float32
    ).reshape(group, -1)
    grad_value_full = jnp.einsum(
        "jrtk,tjrd->kjd", probs_again, grad_heads, preferred_element_type=jnp.float32
    ).reshape(group, -1)
    grad_key_sum, grad_value_sum = (
        lax.psum_scatter(grad_key_full, "seq", scatter_dimension=0, tiled=True),
        lax.psum_scatter(grad_value_full, "seq", scatter_dimension=0, tiled=True),
    )
    grad_key_b = grad_key_sum.astype(jnp.bfloat16)
    grad_value_b = grad_value_sum.astype(jnp.bfloat16)
    grad_hidden_one = lax.psum(
        against(grad_query_b, eff_query)
        + against(grad_key_b, eff_key)
        + against(grad_value_b, eff_value),
        "mp",
    )
    gain_one_part = jnp.sum(grad_hidden_one * normed_one, axis=0)
    grad_tokens = grad_resid + backward_norm(grad_hidden_one * gain_one, normed_one, inverse_one)
    grad_query_eff = inner_rows(hidden_one, grad_query_b)
    grad_key_eff = inner_rows(hidden_one, grad_key_b)
    grad_value_eff = inner_rows(hidden_one, grad_value_b)
    row_sums = (
        lax.psum_scatter(grad_query_eff, ("dp", "seq"), scatter_dimension=0, tiled=True),
        lax.psum_scatter(grad_key_eff, ("dp", "seq"), scatter_dimension=0, tiled=True),
        lax.psum_scatter(grad_value_eff, ("dp", "seq"), scatter_dimension=0, tiled=True),
        lax.psum_scatter(grad_gate_eff, ("dp", "seq"), scatter_dimension=0, tiled=True),
        lax.psum_scatter(grad_up_eff, ("dp", "seq"), scatter_dimension=0, tiled=True),
        lax.psum_scatter(gain_one_part, ("dp", "seq"), scatter_dimension=0, tiled=True),
        lax.psum_scatter(gain_two_part, ("dp", "seq"), scatter_dimension=0, tiled=True),
    )
    col_sums = (
        lax.psum_scatter(grad_out_eff, ("dp", "seq"), scatter_dimension=1, tiled=True),
        lax.psum_scatter(grad_down_eff, ("dp", "seq"), scatter_dimension=1, tiled=True),
    )
    sum_query, sum_key, sum_value, sum_gate, sum_up, sum_gain_one, sum_gain_two = row_sums
    out_sum, sum_down = col_sums
    grad_query = sum_query * bound_slope(w_query, bound_query)
    grad_key = sum_key * bound_slope(w_key, bound_key)
    grad_value = sum_value * bound_slope(w_value, bound_value)
    grad_gate = sum_gate * bound_slope(w_gate, bound_gate)
    grad_up = sum_up * bound_slope(w_up, bound_up)
    grad_out = out_sum * bound_slope(w_out, bound_out)
    grad_down = sum_down * bound_slope(w_down, bound_down)
    attn_scales = jnp.stack([peak_query, peak_out])
    kv_scales = jnp.stack([peak_key, peak_value])
    ffn_scales = jnp.stack([peak_gate, peak_up, peak_down])
    return (
        mixed,
        grad_tokens,
        grad_query,
        grad_key,
        grad_value,
        grad_out,
        grad_gate,
        grad_up,
        grad_down,
        sum_gain_one,
        sum_gain_two,
        attn_scales,
        kv_scales,
        ffn_scales,
    )


F32 = jnp.float32
BF16 = jnp.bfloat16
MESH = pl.DeviceIdType.MESH
VMEM_BYTES = 63 * 1024 * 1024


def natural(left, right):
    return jnp.dot(left, right, preferred_element_type=F32)


def mul(index, size):
    return pl.multiple_of(index * size, size)


class Place:
    def __init__(self):
        dp, y, z = lax.axis_index("dp"), lax.axis_index("seq"), lax.axis_index("mp")
        x, core = dp // 2, dp % 2
        self.x, self.y, self.z, self.core = x, y, z, core
        self.to_core = (x * 2 + (1 - core), y, z)
        self.to_x = ((1 - x) * 2 + core, y, z)
        self.to_y = (dp, 1 - y, z)
        self.to_xy = ((1 - x) * 2 + core, 1 - y, z)
        self.to_up = (dp, y, jnp.minimum(z + 1, 3))
        self.to_down = (dp, y, jnp.maximum(z - 1, 0))

    def slot(self, x, core, y):
        return (x * 2 + core) * 2 + y


def greet(here, targets):
    barrier = pltpu.get_barrier_semaphore()
    for target in targets:
        pl.semaphore_signal(barrier, inc=1, device_id=target, device_id_type=MESH)

    @pl.when(here.z < 3)
    def _():
        pl.semaphore_signal(barrier, inc=1, device_id=here.to_up, device_id_type=MESH)

    @pl.when(here.z > 0)
    def _():
        pl.semaphore_signal(barrier, inc=1, device_id=here.to_down, device_id_type=MESH)

    inner = (here.z < 3) & (here.z > 0)

    @pl.when(inner)
    def _():
        pl.semaphore_wait(barrier, len(targets) + 2)

    @pl.when(jnp.logical_not(inner))
    def _():
        pl.semaphore_wait(barrier, len(targets) + 1)


def remote(src, dst, send, recv, target):
    return pltpu.make_async_remote_copy(
        src_ref=src,
        dst_ref=dst,
        send_sem=send,
        recv_sem=recv,
        device_id=target,
        device_id_type=MESH,
    )


class Line:
    def __init__(self, here, partial, gathered, land, total, sems, transform, own=None, give=None, subs=4):
        self.here, self.partial, self.gathered, self.own = here, partial, gathered, own
        self.land, self.total, self.sems, self.transform = land, total, sems, transform
        self.size, self.subs = partial.shape[0] // 4, subs
        self.give = give
        self.part = self.size // subs

    def rows(self, chunk, sub):
        return pl.ds(pl.multiple_of(chunk * self.size + sub * self.part, self.part), self.part)

    def scatter_copy(self, way, step, sub=None):
        z = self.here.z
        chunk = jnp.minimum(z + 4 - step, 3) if way == 0 else jnp.maximum(z - 4 + step, 0)
        rows, spot = self.span(chunk, sub)
        at = (0, way, step - 1)
        recv = self.sems[1].at[at + (sub or 0,)]
        target = self.here.to_up if way == 0 else self.here.to_down
        dst = self.land.at[way, step - 1, spot]
        return remote(self.partial.at[rows], dst, self.sems[0].at[at], recv, target)

    def gather_copy(self, way, step, sub=None):
        z = self.here.z
        chunk = jnp.maximum(z - (step - 1), 0) if way == 0 else jnp.minimum(z + (step - 1), 3)
        rows, spot = self.span(chunk, sub)
        at = (1, way, step - 1)
        recv = self.sems[1].at[at + (sub or 0,)]
        target = self.here.to_up if way == 0 else self.here.to_down
        ref = self.gathered.at[rows]
        src = ref
        if self.own is not None and step == 1:
            src = self.own.at[spot]
        return remote(src, ref, self.sems[0].at[at], recv, target)

    def span(self, chunk, sub):
        if sub is None:
            return pl.ds(pl.multiple_of(chunk * self.size, self.size), self.size), pl.ds(0, self.size)
        return self.rows(chunk, sub), pl.ds(sub * self.part, self.part)

    def far(self, way):
        return self.here.z if way == 0 else 3 - self.here.z

    def scatter(self, step, sub):
        for way in (0, 1):
            far = self.far(way)

            @pl.when((far <= step - 1) & (far <= 2))
            def _(way=way, far=far):
                if step > 1:

                    @pl.when(far >= 1)
                    def _():
                        self.scatter_copy(way, step - 1, sub).wait_recv()
                        z = self.here.z
                        chunk = z + 4 - step if way == 0 else z - 4 + step
                        rows = self.rows(chunk, sub)
                        came = self.land[way, step - 2, pl.ds(sub * self.part, self.part), :]
                        mine = self.partial[rows, :].astype(F32)
                        self.partial[rows, :] = (mine + came.astype(F32)).astype(BF16)

                self.scatter_copy(way, step, sub).start()

    def finish(self, sub):
        rows = self.rows(self.here.z, sub)
        spot = pl.ds(sub * self.part, self.part)
        self.total[...] = self.partial[rows, :].astype(F32)
        for way in (0, 1):

            @pl.when(self.far(way) >= 1)
            def _(way=way):
                self.scatter_copy(way, 3, sub).wait_recv()
                self.total[...] += self.land[way, 2, spot, :].astype(F32)

        result = self.transform(sub, spot, self.total[...])
        if self.own is None:
            self.gathered[rows, :] = result
        else:
            self.own[spot, :] = result

    def gather(self, step, sub):
        for way in (0, 1):
            far = self.far(way)

            @pl.when((far >= step - 1) & (far <= 2))
            def _(way=way):
                self.gather_copy(way, step, sub).start()

    def landed(self, step, sub):
        for way in (0, 1):

            @pl.when(self.far(way) >= step)
            def _(way=way):
                self.gather_copy(way, step, sub).wait_recv()

    def ticks(self):
        self.scatter(1, 0)
        for tick in range(self.subs + 6):
            for stage in range(7):
                sub = tick - stage + (stage == 0)
                if 0 <= sub < self.subs:
                    if stage < 3:
                        self.scatter(stage + 1, sub)
                    else:
                        if stage == 3:
                            self.finish(sub)
                        else:
                            self.landed(stage - 3, sub)
                        if stage < 6:
                            self.gather(stage - 2, sub)
                        elif self.give is not None:
                            self.give(sub)
            yield tick

    def close(self):
        for step in (1, 2, 3):
            for way in (0, 1):
                far = self.far(way)

                @pl.when((far <= step - 1) & (far <= 2))
                def _(way=way, step=step):
                    self.scatter_copy(way, step).wait_send()

                @pl.when((far >= step - 1) & (far <= 2))
                def _(way=way, step=step):
                    self.gather_copy(way, step).wait_send()


def line_sems(subs):
    return [pltpu.SemaphoreType.DMA((2, 2, 3)), pltpu.SemaphoreType.DMA((2, 2, 3, subs))]


def line_scratch(rows, width, subs):
    return [
        pltpu.VMEM((rows, width), BF16),
        pltpu.VMEM((2, 3, rows // 4, width), BF16),
        pltpu.VMEM((rows // 4 // subs, width), F32),
        *line_sems(subs),
    ]


class Mail:
    def __init__(self, send_sem, recv_sem):
        self.send_sem, self.recv_sem = send_sem, recv_sem
        self.sent, self.gone = [], []
        self.n_send = self.n_recv = 0

    def make(self, src, dst, target, send_at=None, recv_at=None):
        alone = send_at is None
        if alone:
            send_at, self.n_send = self.n_send, self.n_send + 1
        if recv_at is None:
            recv_at, self.n_recv = self.n_recv, self.n_recv + 1
        copy = remote(src, dst, self.send_sem.at[send_at], self.recv_sem.at[recv_at], target)
        if alone:
            self.sent.append(copy)
        return copy

    def send(self, src, dst, target, send_at=None, recv_at=None):
        copy = self.make(src, dst, target, send_at, recv_at)
        copy.start()
        return copy

    def group(self, leaving, coming, target):
        send_at, recv_at = self.n_send, self.n_recv
        self.n_send, self.n_recv = send_at + 1, recv_at + 1
        sems = self.send_sem.at[send_at], self.recv_sem.at[recv_at]
        self.sent.append(remote(leaving, leaving, *sems, target))
        return send_at, recv_at, remote(coming, coming, *sems, target)

    def finish(self, copy):
        copy.wait_send()
        self.gone.append(copy)

    def close(self):
        for copy in self.sent:
            if all(copy is not other for other in self.gone):
                copy.wait_send()


FRONT_SUBS, BACK_SUBS = 4, 8


EXTRA = 16


def edge(y, rows):
    return pl.multiple_of((1 - y) * (rows - EXTRA), EXTRA)


def number_rows(segments, y, out):
    rows = out.shape[0] - EXTRA

    def turned(start):
        row = segments[:, pl.ds(pl.multiple_of(start, 128), 128)].astype(F32)
        return jnp.transpose(jnp.broadcast_to(row, (128, 128)))

    for first in range(0, rows, 128):
        out[first : first + 128, :] = turned(y * rows + first)
    out[rows:, :] = jnp.where(y == 0, turned(rows)[:EXTRA], turned(rows - 128)[128 - EXTRA :])


def visible(keys, numbers, position, y):
    count = keys.shape[0]
    rows = count - EXTRA
    key = lax.broadcasted_iota(jnp.int32, (count, 1), 0)
    key_pos = jnp.where(key < rows, y * rows + key, key - EXTRA * y)
    return (keys[:, 0:1] == numbers) & (key_pos <= position)


def beside(value, n_heads):
    return jnp.concatenate([value] * n_heads, axis=1)


def extra_visible(keys, y, n_heads):
    rows = keys.shape[0] - EXTRA
    numbers = jnp.transpose(keys[rows:, :])[0:1, :]
    position = rows - EXTRA * y + lax.broadcasted_iota(jnp.int32, (1, EXTRA), 1)
    return visible(keys, beside(numbers, n_heads), beside(position, n_heads), y)


def soft_probs(query, kv, allowed):
    raw = against(kv[:, :HD], query)
    bent = jnp.tanh(raw * HD ** (-0.5) / SOFTCAP)
    capped = jnp.where(allowed, SOFTCAP * bent, -1e30)
    weights = jnp.exp(capped - jnp.max(capped, axis=0, keepdims=True))
    return weights / jnp.sum(weights, axis=0, keepdims=True), bent


def row_of(ref, first, count):
    return jnp.concatenate([ref[first + i : first + i + 1, :] for i in range(count)], axis=1)


def level(pick):
    return jnp.where(pick == 0, 1.0, jnp.where(pick == 1, 0.5, 0.25)).astype(F32)


GELU_C = 0.7978845608028654
GELU_A = 0.044715


def gelu_pair(value):
    square = value * value
    bent = jnp.tanh(GELU_C * value * (1.0 + GELU_A * square))
    out = 0.5 * value * (1.0 + bent)
    slope = 0.5 * (1.0 + bent)
    slope += 0.5 * value * (1.0 - bent * bent) * (GELU_C * (1.0 + 3.0 * GELU_A * square))
    return out, slope


def front_kernel(
    width_pick,
    w_query,
    w_key,
    w_value,
    w_out_t,
    w_down_t,
    w_gate,
    w_up,
    gain_attn,
    gain_ffn,
    tokens_in,
    cot_in,
    segments,
    e_attn_out,
    h2_out,
    x1_out,
    query_out,
    kv_out,
    heads_out,
    h1_out,
    cot_out,
    mixed_in_out,
    grad_gate_out,
    grad_up_out,
    back_out,
    ffn_out,
    slope_ffn_out,
    slope_attn_out,
    small_out,
    peaks_out,
    early_out,
    wf_mine,
    wf_other,
    ea,
    ed,
    eg,
    eu,
    rows_a,
    cots,
    query,
    kv,
    heads,
    h2,
    x1,
    mixed_in,
    grad_gate,
    grad_up,
    slope_attn,
    turned,
    small_src,
    small_land,
    small,
    peaks_src,
    peaks_land,
    peaks,
    peaks_peer,
    keys,
    extra_heads,
    extra_land,
    early_made,
    early_sem,
    partial,
    land,
    total,
    line_send,
    line_recv,
    local_sem,
    send_sem,
    recv_sem,
):
    here = Place()
    x, y, z, core = here.x, here.y, here.z, here.core
    rows, width = tokens_in.shape
    share, n_query = w_query.shape
    n_key = w_key.shape[1]
    n_in, n_attn = n_query + 2 * n_key, 2 * n_query + 2 * n_key
    half = w_gate.shape[1] // 2
    cuts = (0, 5 * half // 9, 7 * half // 9, half)
    weights = (w_down_t, w_gate, w_up)
    effective = (ed, eg, eu)
    tokens, h1 = rows_a.at[pl.ds(0, rows)], rows_a.at[pl.ds(rows, rows)]

    local_count = [0]

    def fetch(src, dst):
        copy = pltpu.make_async_copy(src, dst, local_sem.at[local_count[0]])
        local_count[0] += 1
        copy.start()
        return copy

    def slab(ref, sx, score, sy, first=0, part=share, cols=None):
        at = pl.ds(pl.multiple_of(here.slot(sx, score, sy) * share + first, 16), part)
        return ref.at[at] if cols is None else ref.at[at, cols]

    own_at = here.slot(x, core, y) * share
    attn_cols = [(w_query, 0), (w_key, n_query), (w_value, n_query + n_key), (w_out_t, n_in)]
    get_attn = [
        fetch(w, slab(ea, x, core, y, cols=pl.ds(at, w.shape[1]))) for w, at in attn_cols
    ]
    mine_cols = pl.ds(pl.multiple_of(core * half, half), half)
    their_cols = pl.ds(pl.multiple_of((1 - core) * half, half), half)
    part_cols = [pl.ds(part * half, half) for part in range(3)]
    get_ffn = [fetch(w.at[:, mine_cols], wf_mine.at[:, part_cols[i]]) for i, w in enumerate(weights)]
    get_tokens = fetch(tokens_in, tokens)
    get_cot = fetch(cot_in, cots.at[pl.ds(0, rows)])
    greet(here, [here.to_core, here.to_x, here.to_y, here.to_xy])
    mail = Mail(send_sem, recv_sem)

    half_share = share // 2

    def peak(block):
        return jnp.max(jnp.abs(block.astype(F32)), axis=0, keepdims=True)

    def set_out(first):
        ref = slab(ea, x, core, y, first, half_share)
        return [mail.send(ref, ref, here.to_x), mail.send(ref, ref, here.to_y)]

    for copy in get_attn:
        copy.wait()
    attn_moves = set_out(0)
    own_rows = pl.ds(pl.multiple_of(own_at, 32), share)
    attn_peak = peak(ea[own_rows, :])
    piece = small_src.shape[1]
    n_pieces = n_attn // piece
    turned[...] = jnp.zeros_like(turned)
    turned[0, :share] = gain_attn[...].astype(F32)
    turned[1, :share] = gain_ffn[...].astype(F32)
    turned[...] = pltpu.roll(turned[...], own_at, 1)
    small_src[...] = jnp.zeros_like(small_src)
    for row in (0, 1):
        for index in range(width // piece):
            to = 8 + row * (width // piece) + index
            at = slice(index * piece, (index + 1) * piece)
            small_src[to : to + 1, :] = turned[row : row + 1, at]
    for index in range(n_pieces):
        at = slice(index * piece, (index + 1) * piece)
        small_src[index : index + 1, :] = attn_peak[:, at]
    first = mail.send(small_src, small_land.at[0], here.to_core)
    swap = [
        mail.send(w.at[:, their_cols], wf_other.at[:, part_cols[i]], here.to_core)
        for i, w in enumerate(weights)
    ]
    own = slab(ea, x, core, y)
    ac = mail.send(own, own, here.to_core)
    cot_copy = mail.send(cot_in, cots.at[pl.ds(rows, rows)], here.to_core)
    first.wait_recv()

    def merge(mine, other):
        mine[0:8, :] = jnp.maximum(mine[0:8, :], other[0:8, :])
        mine[8:, :] = mine[8:, :] + other[8:, :]

    small[...] = small_src[...]
    merge(small, small_land.at[0])
    ring = (here.to_x, here.to_y, here.to_xy)
    small_send = [mail.send(small, small_land.at[1 + i], to) for i, to in enumerate(ring)]

    for copy in get_ffn:
        copy.wait()
    for copy in swap:
        copy.wait_recv()
    peaks_src[...] = jnp.zeros_like(peaks_src)
    for part in range(3):
        cols = slice(part * half, (part + 1) * half)
        both = jnp.maximum(peak(wf_mine[:, cols]), peak(wf_other[:, cols]))
        line_at = (part + 2) % 3
        peaks_src[line_at : line_at + 1, :] = both
    peaks_send = [mail.send(peaks_src, peaks_land.at[i], to) for i, to in enumerate(ring)]
    attn_moves += set_out(half_share)

    for copy in small_send:
        copy.wait_recv()
        mail.finish(copy)
    for index in (1, 2, 3):
        merge(small, small_land.at[index])
    outs = [fetch(small, small_out)]

    get_tokens.wait()
    gain_one = row_of(small, 8, width // piece)
    gain_two = row_of(small, 8 + width // piece, width // piece)

    @pl.loop(0, rows // 32)
    def _(index):
        at = pl.ds(mul(index, 32), 32)
        h1[at, :] = (forward_norm(tokens[at, :].astype(F32))[0] * gain_one).astype(BF16)


    def tangent(block, bound):
        return jnp.tanh(block.astype(F32) / bound)

    for copy in peaks_send:
        copy.wait_recv()
    peaks[...] = peaks_src[...]
    for index in range(3):
        peaks[...] = jnp.maximum(peaks[...], peaks_land[index])
    peer_copy = mail.send(peaks, peaks_peer, here.to_core)
    outs.append(fetch(peaks, peaks_out.at[:, mine_cols]))
    picks = (6, 4, 5)
    other_at = here.slot(x, 1 - core, y) * share
    for part in range(3):
        cols = slice(part * half, (part + 1) * half)
        line_at = (part + 2) % 3
        bound = peaks[line_at : line_at + 1, :] * level(width_pick[picks[part]])

        @pl.loop(0, share // 32)
        def _(index, cols=cols, bound=bound, part=part):
            at = pl.ds(mul(index, 32), 32)
            for weight, start in ((wf_mine, own_at), (wf_other, other_at)):
                to = pl.ds(pl.multiple_of(start + index * 32, 32), 32)
                bent = tangent(weight[at, cols], bound)
                effective[part][to, :] = (bound * bent).astype(BF16)
                weight[at, cols] = (1.0 - bent * bent).astype(BF16)

    outs.append(fetch(wf_mine, slope_ffn_out.at[core]))
    outs.append(fetch(wf_other, slope_ffn_out.at[1 - core]))

    for copy in attn_moves:
        copy.wait_recv()
    from_x = slab(ea, 1 - x, core, y)
    corner = slab(ea, 1 - x, core, y, 0, half_share)
    dy = mail.send(corner, corner, here.to_y)
    cx = mail.send(from_x, from_x, here.to_core)
    from_y = slab(ea, x, core, 1 - y)
    corner = slab(ea, x, core, 1 - y, half_share, half_share)
    dx = mail.send(corner, corner, here.to_x)
    cy = mail.send(from_y, from_y, here.to_core)

    splits = [pl.ds(a, b - a) for a, b in zip(cuts, cuts[1:])]
    moving, together = {}, {}

    def block_of(part, split, count):
        return effective[part].at[pl.ds(0, count * share), splits[split]]

    def move(part, split, pair, axis, ref, target):
        if (part, split) not in together:
            leaving, coming = block_of(part, split, 6), block_of(part, split, 4)
            together[part, split] = mail.group(leaving, coming, here.to_x)
        send_at, recv_at, _ = together[part, split]
        copy = mail.send(ref, ref, target, send_at, None if pair == axis else recv_at)
        if pair == axis:
            moving[part, split, pair] = copy

    def ship(part, split, axis, pairs=(0, 1)):
        target = here.to_x if axis == 0 else here.to_y
        for pair in pairs:
            ref = slab(effective[part], x, pair, y, cols=splits[split])
            move(part, split, pair, axis, ref, target)

    def pass_on(part, split, pair):
        moving[part, split, pair].wait_recv()
        at = (1 - x, y) if pair == 0 else (x, 1 - y)
        ref = slab(effective[part], at[0], pair, at[1], cols=splits[split])
        move(part, split, pair, 2, ref, here.to_y if pair == 0 else here.to_x)

    def arrived(part, split):
        together[part, split][2].wait_recv()

    ship(0, 0, 0)
    ship(0, 0, 1, (0,))

    flat_peak = row_of(small, 0, n_pieces)
    bound_attn = jnp.concatenate(
        [
            flat_peak[:, :n_query] * level(width_pick[0]),
            flat_peak[:, n_query : n_query + n_key] * level(width_pick[1]),
            flat_peak[:, n_query + n_key : n_in] * level(width_pick[2]),
            flat_peak[:, n_in:] * level(width_pick[3]),
        ],
        axis=1,
    )

    def soften(sx, score, sy, slopes=False):
        base = here.slot(sx, score, sy) * share

        @pl.loop(0, share // 32)
        def _(index):
            at = pl.ds(mul(index, 32), 32)
            to = pl.ds(pl.multiple_of(base + index * 32, 32), 32)
            bent = tangent(ea[to, :], bound_attn)
            ea[to, :] = (bound_attn * bent).astype(BF16)
            if slopes:
                slope_attn[at, :] = (1.0 - bent * bent).astype(BF16)

    for copy in attn_moves + [ac]:
        mail.finish(copy)
    soften(x, core, y, True)
    outs.append(fetch(slope_attn, slope_attn_out))
    ac.wait_recv()
    soften(x, 1 - core, y)
    cx.wait_recv()
    soften(1 - x, 1 - core, y)
    cy.wait_recv()
    soften(x, 1 - core, 1 - y)
    dy.wait_recv()
    dx.wait_recv()
    across = slab(ea, 1 - x, core, 1 - y)
    cxy = mail.send(across, across, here.to_core)
    for copy in (dy, cx, dx, cy):
        mail.finish(copy)
    soften(1 - x, core, y)
    soften(x, core, 1 - y)
    cxy.wait_recv()
    mail.finish(cxy)
    soften(1 - x, core, 1 - y)
    soften(1 - x, 1 - core, 1 - y)
    e_attn_copy = fetch(ea, e_attn_out)

    tile = 256

    @pl.loop(0, n_query // tile)
    def _(index):
        cols = pl.ds(mul(index, tile), tile)
        query[:rows, cols] = natural(h1[...], ea[:, cols]).astype(BF16)

    @pl.loop(0, 2 * n_key // tile)
    def _(index):
        cols = pl.ds(mul(index, tile), tile)
        source = pl.ds(pl.multiple_of(n_query + index * tile, tile), tile)
        kv[:rows, cols] = natural(h1[...], ea[:, source]).astype(BF16)

    ours, theirs = pl.ds(edge(y, rows), EXTRA), pl.ds(rows, EXTRA)
    row_copies = [
        mail.send(ref.at[ours], ref.at[theirs], here.to_y) for ref in (query, kv)
    ]
    for part in (1, 2):
        ship(part, 0, 0)
    h1_copy = fetch(h1, h1_out)
    number_rows(segments, y, keys)
    for copy in row_copies:
        copy.wait_recv()

    block, n_heads = 128, n_query // HD

    def attend(at, allowed):
        stack = jnp.concatenate([query[at, i * HD : (i + 1) * HD] for i in range(n_heads)], axis=0)
        probs, _ = soft_probs(stack, kv, allowed)
        return inner_rows(probs.astype(BF16), kv[:, HD:]).astype(BF16)

    out = attend(theirs, extra_visible(keys, y, n_heads))
    for i in range(n_heads):
        extra_heads[:, i * HD : (i + 1) * HD] = out[i * EXTRA : (i + 1) * EXTRA]
    extra_copy = mail.send(extra_heads, extra_land, here.to_y)
    ship(0, 0, 1, (1,))
    for part in (1, 2):
        ship(part, 0, 1)

    @pl.loop(0, rows // block)
    def _(index):
        at = pl.ds(mul(index, block), block)
        start = pl.multiple_of(y * rows + index * block, block)
        numbers = segments[:, pl.ds(start, block)].astype(F32)
        position = start + lax.broadcasted_iota(jnp.int32, (1, block), 1)
        allowed = visible(keys, beside(numbers, n_heads), beside(position, n_heads), y)
        out = attend(at, allowed)
        for i in range(n_heads):
            heads[at, i * HD : (i + 1) * HD] = out[i * block : (i + 1) * block]

    extra_copy.wait_recv()
    middle = (lax.broadcasted_iota(jnp.int32, (EXTRA, 1), 0) == 0) & (y == 1)
    heads[:EXTRA, :] = jnp.where(middle, extra_land[...], heads[:EXTRA, :])

    @pl.loop(0, width // tile)
    def _(index):
        cols = pl.ds(mul(index, tile), tile)
        partial[:, cols] = against(heads[...], ea[cols, n_in:]).astype(BF16)

    outs += [fetch(query, query_out), fetch(kv, kv_out), fetch(heads, heads_out)]

    tall = 512

    def back_into_mixed(split):
        @pl.loop(0, 2 * rows // tall)
        def _(index):
            at = pl.ds(mul(index, tall), tall)
            grad_gate[at, splits[split]] = natural(cots[at, :], ed[:, splits[split]]).astype(BF16)

    def gated(split):
        cols, high = splits[split], 512 if split else 256

        @pl.loop(0, 2 * rows // high)
        def _(index):
            at = pl.ds(mul(index, high), high)
            gate = natural(h2[at, :], eg[:, cols])
            upper = natural(h2[at, :], eu[:, cols])
            value, slope = gelu_pair(gate)
            back = grad_gate[at, cols].astype(F32)
            mixed_in[at, cols] = (value * upper).astype(BF16)
            grad_gate[at, cols] = (back * upper * slope).astype(BF16)
            grad_up[at, cols] = (back * value).astype(BF16)

    def to_width(target, pairs, split, then=None):
        wide = width // 3

        def piece(at):
            for column in range(3):
                cols = slice(column * wide, (column + 1) * wide)
                added = against(pairs[0][0][at, splits[split]], pairs[0][1][cols, splits[split]])
                for left, right in pairs[1:]:
                    added += against(left[at, splits[split]], right[cols, splits[split]])
                if split:
                    added += target[column][at, :].astype(F32)
                target[column][at, :] = added.astype(BF16)

        if then is None:

            @pl.loop(0, 2 * rows // tall)
            def _(index):
                piece(pl.ds(mul(index, tall), tall))

        else:
            for first in range(0, 2 * rows, tall):
                piece(pl.ds(first, tall))
                then(pl.ds(first, tall))

    def transform(sub, spot, summed):
        at = pl.ds(pl.multiple_of(z * (rows // 4) + sub * line.part, line.part), line.part)
        resid = tokens[at, :].astype(F32) + summed
        x1[spot, :] = resid
        return (forward_norm(resid)[0] * gain_two).astype(BF16)

    own_half, other_half = (h2.at[pl.ds(first, rows)] for first in (0, rows))
    give_send, give_recv, all_given = mail.group(own_half, other_half, here.to_core)

    def give(sub):
        for chunk in range(4):
            first = chunk * (rows // 4) + sub * line.part
            src, dst = (h2.at[pl.ds(first + at, line.part)] for at in (0, rows))
            mail.send(src, dst, here.to_core, give_send, give_recv)

    line = Line(here, partial, h2, land, total, (line_send, line_recv), transform, give=give, subs=FRONT_SUBS)
    width_blocks = [pl.ds(i * (width // 3), width // 3) for i in range(3)]
    back_part = [rows_a.at[:, cols] for cols in width_blocks]
    spare = ((0, 0), (0, 1), (1, 0))
    ffn_part = [
        ea.at[pl.ds(i * 2 * rows, 2 * rows), pl.ds(j * (width // 3), width // 3)] for i, j in spare
    ]
    upward = ((grad_gate, eg), (grad_up, eu))
    downward = ((mixed_in, ed),)
    for tick in line.ticks():
        if tick == 1:
            pass_on(0, 0, 0)
            pass_on(0, 0, 1)
        if tick == 2:
            pass_on(1, 0, 0)
        if tick == 3:
            get_cot.wait()
            cot_copy.wait_recv()
            cot_keep = fetch(cots.at[pl.ds(rows, rows)], cot_out)
        if tick == 4:
            pass_on(1, 0, 1)
            pass_on(2, 0, 0)
        if tick == 5:
            pass_on(2, 0, 1)
            for part in range(3):
                for axis in (0, 1):
                    ship(part, 1, axis)
        if tick == 8:
            for axis in (0, 1):
                ship(0, 2, axis)
        if tick == 6:
            arrived(0, 0)
            back_into_mixed(0)
    line.close()
    outs.append(fetch(x1, x1_out))
    peer_copy.wait_recv()
    outs.append(fetch(peaks_peer, peaks_out.at[:, their_cols]))
    arrived(1, 0)
    arrived(2, 0)
    all_given.wait_recv()
    outs.append(fetch(h2, h2_out))
    gated(0)
    for part in range(3):
        for turn in (0, 1):
            pass_on(part, 1, turn)
    for part in (1, 2):
        for axis in (0, 1):
            ship(part, 2, axis)
    h1_copy.wait()
    to_width(back_part, upward, 0)
    arrived(0, 1)
    back_into_mixed(1)
    arrived(1, 1)
    arrived(2, 1)
    gated(1)
    e_attn_copy.wait()
    to_width(ffn_part, downward, 0)
    to_width(back_part, upward, 1)
    to_width(ffn_part, downward, 1)
    for part in range(3):
        for turn in (0, 1):
            pass_on(part, 2, turn)
    late = cuts[2]

    def early_copy(index):
        at = pl.ds(mul(index, tile), tile)
        return pltpu.make_async_copy(early_made, early_out.at[at], early_sem)

    @pl.loop(0, width // tile)
    def _(index):
        made = inner_rows(h2[:, pl.ds(mul(index, tile), tile)], grad_gate[:, :late]).astype(BF16)

        @pl.when(index > 0)
        def _():
            early_copy(index - 1).wait()

        early_made[...] = made
        early_copy(index).start()

    early_copy(width // tile - 1).wait()
    arrived(0, 2)
    back_into_mixed(2)
    arrived(1, 2)
    arrived(2, 2)
    gated(2)
    outs += [
        fetch(mixed_in, mixed_in_out),
        fetch(grad_gate, grad_gate_out),
        fetch(grad_up, grad_up_out),
    ]
    to_width(back_part, upward, 2, lambda at: outs.append(fetch(rows_a.at[at], back_out.at[at])))

    def ffn_leaves(at):
        for i in range(3):
            outs.append(fetch(ffn_part[i].at[at], ffn_out.at[at, width_blocks[i]]))

    to_width(ffn_part, downward, 2, ffn_leaves)
    cot_keep.wait()
    mail.close()
    for copy in outs:
        copy.wait()


def front(width_pick, weights, gain_attn, gain_ffn, tokens, cotangent, segments):
    rows, width = tokens.shape
    share, n_query = weights[0].shape
    n_kv = 2 * weights[1].shape[1]
    n_attn = 2 * n_query + n_kv
    hidden = weights[-1].shape[1]
    half = hidden // 2
    shapes = [
        ((width, n_attn), BF16),
        ((2 * rows, width), BF16),
        ((rows // 4, width), F32),
        ((rows + EXTRA, n_query), BF16),
        ((rows + EXTRA, n_kv), BF16),
        ((rows, n_query), BF16),
        ((rows, width), BF16),
        ((rows, width), BF16),
        ((2 * rows, half), BF16),
        ((2 * rows, half), BF16),
        ((2 * rows, half), BF16),
        ((2 * rows, width), BF16),
        ((2 * rows, width), BF16),
        ((2, share, 3 * half), BF16),
        ((share, n_attn), BF16),
        ((32, 256), F32),
        ((8, hidden), F32),
        ((width, 7 * half // 9), BF16),
    ]
    in_vmem = pl.BlockSpec(memory_space=pltpu.VMEM)
    in_smem = pl.BlockSpec(memory_space=pltpu.SMEM)
    anywhere = pl.BlockSpec(memory_space=pl.ANY)
    scratch = [
        pltpu.VMEM((share, 3 * half), BF16),
        pltpu.VMEM((share, 3 * half), BF16),
        pltpu.VMEM((width, n_attn), BF16),
        pltpu.VMEM((width, half), BF16),
        pltpu.VMEM((width, half), BF16),
        pltpu.VMEM((width, half), BF16),
        pltpu.VMEM((2 * rows, width), BF16),
        pltpu.VMEM((2 * rows, width), BF16),
        pltpu.VMEM((rows + EXTRA, n_query), BF16),
        pltpu.VMEM((rows + EXTRA, n_kv), BF16),
        pltpu.VMEM((rows, n_query), BF16),
        pltpu.VMEM((2 * rows, width), BF16),
        pltpu.VMEM((rows // 4, width), F32),
        pltpu.VMEM((2 * rows, half), BF16),
        pltpu.VMEM((2 * rows, half), BF16),
        pltpu.VMEM((2 * rows, half), BF16),
        pltpu.VMEM((share, n_attn), BF16),
        pltpu.VMEM((8, width), F32),
        pltpu.VMEM((32, 256), F32),
        pltpu.VMEM((4, 32, 256), F32),
        pltpu.VMEM((32, 256), F32),
        pltpu.VMEM((8, half), F32),
        pltpu.VMEM((3, 8, half), F32),
        pltpu.VMEM((8, half), F32),
        pltpu.VMEM((8, half), F32),
        pltpu.VMEM((rows + EXTRA, 128), F32),
        pltpu.VMEM((EXTRA, n_query), BF16),
        pltpu.VMEM((EXTRA, n_query), BF16),
        pltpu.VMEM((256, 7 * half // 9), BF16),
        pltpu.SemaphoreType.DMA,
        *line_scratch(rows, width, FRONT_SUBS),
        pltpu.SemaphoreType.DMA((34,)),
        pltpu.SemaphoreType.DMA((35,)),
        pltpu.SemaphoreType.DMA((53,)),
    ]
    return pl.pallas_call(
        front_kernel,
        out_shape=[jax.ShapeDtypeStruct(s, d) for s, d in shapes],
        in_specs=[in_smem] + [anywhere] * 7 + [in_vmem] * 2 + [anywhere] * 2 + [in_vmem],
        out_specs=[anywhere] * len(shapes),
        scratch_shapes=scratch,
        compiler_params=pltpu.CompilerParams(
            collective_id=0, has_side_effects=True, vmem_limit_bytes=VMEM_BYTES
        ),
        cost_estimate=pl.CostEstimate(
            flops=36 * 10**9, bytes_accessed=90 * 10**6, transcendentals=8 * 10**6
        ),
        name="front",
    )(width_pick, *weights, gain_attn, gain_ffn, tokens, cotangent, segments)


OUTPUT_PLAN = (7, 8, 10, 11, 12, 14, 15, 17, 18, 19, 20, 21, 22, 23)


def back_kernel(
    back_in,
    ffn_in,
    mixed_in,
    grad_gate,
    grad_up,
    h2_in,
    cot_other,
    early_in,
    x1_in,
    small,
    e_attn,
    query_in,
    kv_in,
    heads_in,
    h1_in,
    tokens_in,
    cot_in,
    segments,
    slope_ffn,
    slope_attn_in,
    out_down,
    out_gate,
    out_up,
    out_attn,
    mixed_out,
    tokens_out,
    gains_out,
    de_down,
    de_gate,
    de_up,
    stage_a,
    stage_b,
    land_a,
    land_b,
    last_a,
    last_b,
    slopes,
    partial,
    partial_ffn,
    grad_resid_b,
    own_ffn,
    own_tokens,
    land,
    land_ffn,
    total,
    ea,
    core_land,
    attn_a,
    attn_b,
    attn_last_a,
    attn_last_b,
    query,
    kv,
    heads,
    h1,
    keys,
    grad_in,
    grad_kv,
    edge_send,
    edge_land,
    row_send,
    row_land,
    x1,
    grad_resid,
    token_chunk,
    cot_chunk,
    gain_part,
    gain_sum,
    gain_land,
    line_send,
    line_recv,
    ffn_send,
    ffn_recv,
    work_sem,
    local_sem,
    send_sem,
    recv_sem,
):
    here = Place()
    x, y, z, core = here.x, here.y, here.z, here.core
    rows, width = tokens_in.shape
    share, half = last_a.shape[1], last_a.shape[2]
    n_query, n_attn = query.shape[1], ea.shape[1]
    n_in = n_attn - n_query
    de_ffn = (de_down, de_gate, de_up)
    out_ffn = (out_down, out_gate, out_up)
    chunk_rows = pl.ds(pl.multiple_of(z * (rows // 4), rows // 4), rows // 4)
    mine_cols = pl.ds(pl.multiple_of(core * half, half), half)
    tile = 256

    local_count = [0]

    def fetch(src, dst):
        copy = pltpu.make_async_copy(src, dst, local_sem.at[local_count[0]])
        local_count[0] += 1
        copy.start()
        return copy

    order = (1, 2, 0)
    slot_of = {part: i % 2 for i, part in enumerate(order)}

    late = early_in.shape[1]
    blocks = {0: [(de_down, 0, half)], 2: [(de_up, 0, half)]}
    blocks[1] = [(early_in, 0, late), (de_gate, late, half - late)]

    def lanes(ref, block):
        return ref if ref.shape[-1] == block[2] else ref.at[:, pl.ds(block[1], block[2])]

    def source(block, at):
        return lanes(block[0].at[at], block)

    def stage(part):
        a_rows = pl.ds(pl.multiple_of(here.slot(x, 0, 0) * share, share), 2 * share)
        slot = slot_of[part]
        copies = []
        for block in blocks[part]:
            copies.append(fetch(source(block, a_rows), lanes(stage_a.at[slot], block)))
            for i in (0, 1):
                b_rows = pl.ds(mul(here.slot(i, 1, y), share), share)
                copies.append(fetch(source(block, b_rows), lanes(stage_b.at[slot, i], block)))
        return copies

    sides = (mixed_in, grad_gate, grad_up)
    side_rows = [pl.ds(0, 2 * rows), pl.ds(2 * rows, 2 * rows), pl.ds(0, 2 * rows)]
    side_at = {part: ea.at[side_rows[i], pl.ds(0, half)] for i, part in enumerate(order)}
    strip_cols = pl.ds(half, tile)
    made_cols = {part: pl.ds(blocks[part][-1][1], blocks[part][-1][2]) for part in order}

    def strip_copies(part, index, slot):
        cols = pl.ds(mul(index, tile), tile)
        to = [
            ea.at[pl.ds(pl.multiple_of(slot * 2 * rows + i * rows, rows), rows), strip_cols]
            for i in (0, 1)
        ]
        if part:
            src = [h2_in.at[pl.ds(i * rows, rows), cols] for i in (0, 1)]
        else:
            src = [cot_in.at[:, cols], cot_other.at[:, cols]]
        return [
            pltpu.make_async_copy(src[i], to[i], work_sem.at[slot, i]) for i in (0, 1)
        ]

    def result_copy(part, index):
        at = pl.ds(mul(index, tile), tile)
        cols = made_cols[part]
        slot = lax.rem(index, 2)
        made = slopes.at[slot, pl.ds(0, tile), cols]
        return pltpu.make_async_copy(made, de_ffn[part].at[at, cols], work_sem.at[2, slot])

    sides_here = {order[0]: fetch(sides[order[0]], side_at[order[0]])}
    for copy in strip_copies(order[0], 0, 0):
        copy.start()
    get_x1 = fetch(x1_in, x1)
    get_cot = fetch(cot_in.at[chunk_rows], cot_chunk)
    get_tokens = fetch(tokens_in.at[chunk_rows], token_chunk)
    get_partial = fetch(back_in.at[pl.ds(0, rows)], partial)
    sides_here[order[1]] = fetch(sides[order[1]], side_at[order[1]])
    far_target = (x * 2 + core, y, lax.rem(z + 2, 4))
    near_target = (x * 2 + core, y, z + 1 - 2 * lax.rem(z, 2))
    plane = [here.to_core, here.to_x, here.to_y, here.to_xy]
    plane += [(2 * (1 - x) + 1 - core, y, z), (2 * x + 1 - core, 1 - y, z)]
    plane += [(2 * (1 - x) + 1 - core, 1 - y, z)]
    greet(here, [*plane, far_target])
    mail = Mail(send_sem, recv_sem)
    their_half = pl.ds(rows, rows)
    chunks = [jnp.where(z < 2, 3 - i, i) * (rows // 4) for i in range(4)]
    chunks = [pl.multiple_of(first, rows // 4) for first in chunks]
    back_copies = [
        mail.send(
            back_in.at[pl.ds(rows + first, rows // 4)],
            partial_ffn.at[pl.ds(first, rows // 4)],
            here.to_core,
        )
        for first in chunks
    ]
    ffn_copy = mail.send(ffn_in.at[their_half], h1, here.to_core)

    n_strips = width // tile

    def strips(part, first, last):
        if first == 0:
            sides_here[part].wait()

        @pl.loop(first, last)
        def _(index):
            slot = lax.rem(index, 2)
            for copy in strip_copies(part, index, slot):
                copy.wait()

            @pl.when(index + 1 < n_strips)
            def _():
                for copy in strip_copies(part, index + 1, 1 - slot):
                    copy.start()

            left = ea[pl.ds(pl.multiple_of(slot * 2 * rows, rows), 2 * rows), strip_cols]
            made = inner_rows(left, side_at[part][:, made_cols[part]]).astype(BF16)

            @pl.when(index > 1)
            def _():
                result_copy(part, index - 2).wait()

            slopes[slot, :tile, made_cols[part]] = made
            result_copy(part, index).start()

        if last == n_strips:
            for index in (n_strips - 2, n_strips - 1):
                result_copy(part, jnp.int32(index)).wait()
            at = order.index(part)
            if at + 1 < 3:
                for copy in strip_copies(order[at + 1], 0, 0):
                    copy.start()
            if at == 0:
                sides_here[order[2]] = fetch(sides[order[2]], side_at[order[2]])
            if at < 2:
                staged[part] = stage(part)

    staged = {}
    slope_here = {}

    def get_slopes(part):
        cols = pl.ds(part * half, half)
        slope_here[part] = fetch(slope_ffn.at[:, :, cols], slopes)

    first_hop, groups = {}, {}
    second_hop = {}
    ending = []

    def ship(part, i, block, axis):
        if axis == 0:
            at = pl.ds(mul(here.slot(1 - x, 0, i), share), share)
            to, target = land_a.at[part, pl.ds(i * share, share)], here.to_x
        else:
            at = pl.ds(mul(here.slot(i, 1, 1 - y), share), share)
            to, target = land_b.at[part, i], here.to_y
        if (part, block[1]) not in groups:
            four = lanes(de_ffn[part].at[pl.ds(0, 4 * share)], block)
            groups[part, block[1]] = mail.group(four, four, here.to_x)
            first_hop.setdefault(part, []).append(groups[part, block[1]][2])
        mail.send(source(block, at), lanes(to, block), target, *groups[part, block[1]][:2])

    def ship_all(part, i, axes=(0, 1)):
        for block in blocks[part]:
            for axis in axes:
                ship(part, i, block, axis)

    step = 32

    def relay(part):
        slot = slot_of[part]
        for copy in staged[part]:
            copy.wait()
        for copy in first_hop[part]:
            copy.wait_recv()
        base = (1 - y) * share

        @pl.loop(0, share // step)
        def _(index):
            at = pl.ds(pl.multiple_of(base + index * step, step), step)
            mine = stage_a[slot, at, :].astype(F32) + land_a[part, at, :].astype(F32)
            stage_a[slot, at, :] = mine.astype(BF16)
            at = pl.ds(mul(index, step), step)
            mine = stage_b[slot, 1 - x, at, :].astype(F32) + land_b[part, 1 - x, at, :].astype(F32)
            stage_b[slot, 1 - x, at, :] = mine.astype(BF16)

        a_src = stage_a.at[slot, pl.ds(pl.multiple_of(base, share), share)]
        second_hop[part] = (
            mail.send(a_src, last_a.at[part], here.to_y),
            mail.send(stage_b.at[slot, 1 - x], last_b.at[part], here.to_x),
        )

    def settle(part):
        slot = slot_of[part]
        slope_here[part].wait()
        for copy in second_hop[part]:
            copy.wait_recv()
        base = y * share

        @pl.loop(0, share // step)
        def _(index):
            flat = pl.ds(mul(index, step), step)
            at = pl.ds(pl.multiple_of(base + index * step, step), step)
            mine = stage_a[slot, at, :].astype(F32) + land_a[part, at, :].astype(F32)
            mine = mine + last_a[part, flat, :].astype(F32)
            stage_a[slot, at, :] = (mine * slopes[0, flat, :].astype(F32)).astype(BF16)
            mine = stage_b[slot, x, flat, :].astype(F32) + land_b[part, x, flat, :].astype(F32)
            mine = mine + last_b[part, flat, :].astype(F32)
            stage_b[slot, x, flat, :] = (mine * slopes[1, flat, :].astype(F32)).astype(BF16)

        a_ref = stage_a.at[slot, pl.ds(pl.multiple_of(base, share), share)]
        b_ref = stage_b.at[slot, x]
        out = out_ffn[part].at[:, mine_cols]
        give_b = mail.make(b_ref, out, here.to_core)
        give_a = mail.make(a_ref, out, here.to_core, mail.n_send - 1, mail.n_recv - 1)
        keep_a = pltpu.make_async_copy(a_ref, out, local_sem.at[local_count[0]])
        keep_b = pltpu.make_async_copy(b_ref, out, local_sem.at[local_count[0]])
        local_count[0] += 1

        @pl.when(core == 0)
        def _():
            keep_a.start()
            give_b.start()

        @pl.when(core == 1)
        def _():
            keep_b.start()
            give_a.start()

        ending.append((keep_a, give_b))
        finished[part] = ending[-1]

    finished = {}

    def restage(part, earlier):
        keep, give = finished[earlier]
        keep.wait()
        for copy in (give, *second_hop[earlier]):
            mail.finish(copy)
        staged[part] = stage(part)

    count = width // small.shape[1]
    gain_one = row_of(small, 8, count)
    gain_two = row_of(small, 8 + count, count)

    gain_part[...] = jnp.zeros_like(gain_part)

    def into_resid(sub, spot, summed):
        normed, inverse = forward_norm(x1[spot, :])
        gain_part[1:2, :] += jnp.sum(summed * normed, axis=0, keepdims=True)
        grad = cot_chunk[spot, :].astype(F32) + backward_norm(summed * gain_two, normed, inverse)
        grad_resid[spot, :] = grad
        return grad.astype(BF16)

    def into_mixed(sub, spot, summed):
        return (x1[spot, :] + summed).astype(BF16)

    def into_tokens(sub, spot, summed):
        normed, inverse = forward_norm(token_chunk[spot, :].astype(F32))
        gain_part[0:1, :] += jnp.sum(summed * normed, axis=0, keepdims=True)
        grad = grad_resid[spot, :] + backward_norm(summed * gain_one, normed, inverse)
        return grad.astype(BF16)

    line = Line(here, partial, grad_resid_b, land, total, (line_send, line_recv), into_resid, subs=BACK_SUBS)
    ffn_line = Line(
        here, partial_ffn, mixed_out, land_ffn, total, (ffn_send, ffn_recv), into_mixed, own_ffn, subs=BACK_SUBS
    )
    tok_line = Line(
        here, partial, tokens_out, land, total, (line_send, line_recv), into_tokens, own_tokens, subs=BACK_SUBS
    )

    for i in (0, 1):
        for axis in (0, 1):
            ship(1, i, blocks[1][0], axis)
    for copy in (get_partial, get_x1, get_cot, get_tokens):
        copy.wait()

    def join(target, came, first=0, count=rows):
        @pl.loop(0, count // step)
        def _(index):
            at = pl.ds(pl.multiple_of(first + index * step, step), step)
            target[at, :] = (target[at, :].astype(F32) + came[at, :].astype(F32)).astype(BF16)

    def join_chunk(number):
        back_copies[number].wait_recv()
        join(partial, partial_ffn, chunks[number], rows // 4)

    join_chunk(0)

    quarter, n_heads = 32, n_query // HD
    block = 4 * quarter
    number_rows(segments, y, keys)
    grad_kv[...] = jnp.zeros_like(grad_kv)

    def stacked(value):
        return jnp.concatenate([value[:, i * HD : (i + 1) * HD] for i in range(n_heads)], axis=0)

    def back_through(query_b, grad_o, allowed):
        probs, bent = soft_probs(query_b, kv, allowed)
        grad_probs = against(kv[:, HD:], grad_o)
        row_dot = jnp.sum(probs * grad_probs, axis=0, keepdims=True)
        grad_raw = probs * (grad_probs - row_dot) * (1.0 - bent * bent) * HD ** (-0.5)
        grad_raw = grad_raw.astype(BF16)
        grad_kv[:, :HD] += natural(grad_raw, query_b)
        grad_kv[:, HD:] += natural(probs.astype(BF16), grad_o)
        return inner_rows(grad_raw, kv[:, :HD]).astype(BF16)

    def attend_back(sub):
        firsts = [j * (rows // 4) + sub * quarter for j in range(4)]
        spots = [slice(at, at + quarter) for at in firsts]

        def take(ref):
            return jnp.concatenate([ref[spot, :] for spot in spots], axis=0)

        index = lax.broadcasted_iota(jnp.int32, (1, block), 1)
        chunk = sum((index >= j * quarter).astype(jnp.int32) for j in (1, 2, 3))
        position = y * rows + index + chunk * (rows // 4 - quarter) + sub * quarter
        numbers = jnp.transpose(take(keys))[0:1, :]
        allowed = visible(keys, beside(numbers, n_heads), beside(position, n_heads), y)
        grad_o = natural(take(grad_resid_b), ea[:, n_in:]).astype(BF16)
        if sub == 0:
            edge_send[...] = grad_o[:EXTRA]
            edge_copies.append(mail.send(edge_send, edge_land, here.to_y))
            theirs = (lax.broadcasted_iota(jnp.int32, (block, 1), 0) == 0) & (y == 1)
            grad_o = jnp.where(theirs, jnp.zeros_like(grad_o), grad_o)
        grad_q = back_through(stacked(take(query)), stacked(grad_o), allowed)
        for i in range(n_heads):
            for j, spot in enumerate(spots):
                at = i * block + j * quarter
                grad_in[spot, i * HD : (i + 1) * HD] = grad_q[at : at + quarter]

    edge_copies = []

    def edge_back():
        edge_copies[0].wait_recv()
        ours = (lax.broadcasted_iota(jnp.int32, (EXTRA, 1), 0) == 0) & (y == 0)
        grad_o = jnp.where(ours, edge_land[...], jnp.zeros_like(edge_land))
        allowed = extra_visible(keys, y, n_heads)
        grad_q = back_through(stacked(query[rows:, :]), stacked(grad_o), allowed)
        for i in range(n_heads):
            row_send[:, i * HD : (i + 1) * HD] = grad_q[i * EXTRA : (i + 1) * EXTRA]
        row_send[:, n_query:] = grad_kv[rows:, :].astype(BF16)

    ffn_ticks = ffn_line.ticks()
    plan, count = list(OUTPUT_PLAN), itertools.count(2)

    def output_wave(place):
        while plan and plan[0] <= place:
            plan.pop(0)
            next(ffn_ticks, None)

    later = []
    for tick in line.ticks():
        if tick == 0:
            join_chunk(1)
        if tick == 1:
            join_chunk(2)
            join_chunk(3)
            get_ffn = fetch(ffn_in.at[pl.ds(0, rows)], partial_ffn)
            strips(1, 0, n_strips // 2)
        if tick == 2:
            strips(1, n_strips // 2, n_strips)
            for i in (0, 1):
                for axis in (0, 1):
                    ship(1, i, blocks[1][1], axis)
        if tick in (3, 4, 5):
            strips(2, 3 * tick - 9, 3 * tick - 6)
        if tick == 5:
            ship_all(2, 0)
            ship_all(2, 1)
        if tick in (6, 7):
            strips(0, 5 * tick - 30, min(5 * tick - 25, n_strips))
        if tick == 5:
            get_ffn.wait()
            ffn_copy.wait_recv()
            join(partial_ffn, h1)
            get_h1 = fetch(h1_in, h1)
        if tick == 7:
            later = [
                fetch(e_attn, ea),
                fetch(query_in, query),
                fetch(kv_in, kv),
                fetch(heads_in, heads),
            ]
        output_wave(tick)
        if tick == 9:
            get_slopes(1)
            relay(1)
        if tick == 11:
            ship_all(0, 0, (0,))
        if tick == 8:
            for copy in later:
                copy.wait()
        if tick in (8, 10, 12, 13):
            attend_back((8, 10, 12, 13).index(tick))
    output_wave(14)
    line.close()
    edge_back()
    row_copy = mail.send(row_send, row_land, here.to_y)
    ship_all(0, 0, (1,))
    ship_all(0, 1)
    output_wave(15)
    row_copy.wait_recv()
    at = pl.ds(edge(y, rows), EXTRA)
    grad_in[at, :n_query] = (grad_in[at, :n_query].astype(F32) + row_land[:, :n_query].astype(F32)).astype(BF16)
    grad_kv[at, :] += row_land[:, n_query:].astype(F32)
    grad_in[:, n_query:] = grad_kv[:rows, :].astype(BF16)

    @pl.loop(0, width // tile)
    def _(index):
        cols = pl.ds(mul(index, tile), tile)
        partial[:, cols] = against(grad_in[...], ea[cols, :n_in]).astype(BF16)

    tok_ticks = tok_line.ticks()
    next(tok_ticks, None)
    output_wave(17)

    @pl.loop(0, width // tile)
    def _(index):
        cols = pl.ds(mul(index, tile), tile)
        ea[cols, n_in:] = inner_rows(grad_resid_b[:, cols], heads[...]).astype(BF16)

    next(tok_ticks, None)
    output_wave(18)
    relay(2)
    settle(1)
    get_slopes(2)
    restage(0, 1)
    get_h1.wait()

    @pl.loop(0, width // tile)
    def _(index):
        cols = pl.ds(mul(index, tile), tile)
        ea[cols, :n_in] = inner_rows(h1[:, cols], grad_in[...]).astype(BF16)

    def pair_rows(sx, score):
        return pl.ds(pl.multiple_of(here.slot(sx, score, 0) * share, 2 * share), 2 * share)

    core_copies = [
        mail.send(ea.at[pair_rows(i, 1 - core)], core_land.at[i], here.to_core) for i in (0, 1)
    ]
    for _ in range(2):
        next(tok_ticks, None)
        output_wave(17 + next(count))
    for copy in core_copies:
        copy.wait_recv()

    @pl.loop(0, 2 * share // step)
    def _(index):
        for i in (0, 1):
            at = pl.ds(
                pl.multiple_of(here.slot(i, core, 0) * share + index * step, step), step
            )
            flat = pl.ds(mul(index, step), step)
            ea[at, :] = (ea[at, :].astype(F32) + core_land[i, flat, :].astype(F32)).astype(BF16)

    slope_attn = core_land.at[0, pl.ds(0, share)]
    get_slope_attn = fetch(slope_attn_in, slope_attn)
    cut = attn_a.shape[1]
    left, right = pl.ds(0, cut), pl.ds(cut, n_attn - cut)

    def one_rows(sx, sy):
        return pl.ds(pl.multiple_of(here.slot(sx, core, sy) * share, share), share)

    attn_first = [mail.send(ea.at[pair_rows(1 - x, core), left], attn_a, here.to_x)]
    for i in (0, 1):
        attn_first.append(mail.send(ea.at[one_rows(i, 1 - y), right], attn_b.at[i], here.to_y))
    for _ in range(2):
        next(tok_ticks, None)
        output_wave(17 + next(count))
    relay(0)
    settle(2)
    get_slopes(0)
    for _ in range(3):
        next(tok_ticks, None)
        output_wave(17 + next(count))

    def gain_steps():
        rounds = ([near_target], [far_target], plane)
        mine, at = gain_part, 0
        for number, targets in enumerate(rounds):
            places = gain_land.at[pl.ds(at, len(targets))]
            send_at, recv_at, came = mail.group(places, places, here.to_core)
            for i, target in enumerate(targets):
                mail.send(mine, gain_land.at[at + i], target, send_at, recv_at)
            yield
            came.wait_recv()
            added = mine[...]
            for i in range(len(targets)):
                added = added + gain_land[at + i]
            gain_sum[number] = added
            mine, at = gain_sum.at[number], at + len(targets)

    gain_waves = gain_steps()
    for copy in attn_first:
        copy.wait_recv()

    @pl.loop(0, share // step)
    def _(index):
        flat = pl.ds(mul(index, step), step)
        at = pl.ds(pl.multiple_of(here.slot(x, core, 1 - y) * share + index * step, step), step)
        came = pl.ds(pl.multiple_of((1 - y) * share + index * step, step), step)
        ea[at, left] = (ea[at, left].astype(F32) + attn_a[came, :].astype(F32)).astype(BF16)
        at = pl.ds(pl.multiple_of(here.slot(1 - x, core, y) * share + index * step, step), step)
        ea[at, right] = (
            ea[at, right].astype(F32) + attn_b[1 - x, flat, :].astype(F32)
        ).astype(BF16)

    attn_second = [
        mail.send(ea.at[one_rows(x, 1 - y), left], attn_last_a, here.to_y),
        mail.send(ea.at[one_rows(1 - x, y), right], attn_last_b, here.to_x),
    ]
    def settle_attn():
        get_slope_attn.wait()
        for copy in attn_second:
            copy.wait_recv()

        @pl.loop(0, share // step)
        def _(index):
            flat = pl.ds(mul(index, step), step)
            at = pl.ds(pl.multiple_of(here.slot(x, core, y) * share + index * step, step), step)
            came = pl.ds(pl.multiple_of(y * share + index * step, step), step)
            mine = ea[at, left].astype(F32) + attn_a[came, :].astype(F32)
            mine = mine + attn_last_a[flat, :].astype(F32)
            ea[at, left] = (mine * slope_attn[flat, left].astype(F32)).astype(BF16)
            mine = ea[at, right].astype(F32) + attn_b[x, flat, :].astype(F32)
            mine = mine + attn_last_b[flat, :].astype(F32)
            ea[at, right] = (mine * slope_attn[flat, right].astype(F32)).astype(BF16)

        ends.append(fetch(ea.at[one_rows(x, y)], out_attn))

    ends = []
    for tick in tok_ticks:
        output_wave(17 + next(count))
        if tick > 9:
            next(gain_waves, None)
        if tick == 10:
            ends.append(fetch(own_ffn, mixed_out.at[chunk_rows]))
            ends.append(fetch(own_tokens, tokens_out.at[chunk_rows]))
        if tick == 11:
            settle(0)
        if tick == 12:
            settle_attn()
    for tick in ffn_ticks:
        pass
    for _ in gain_waves:
        pass
    ends.append(fetch(gain_sum.at[2], gains_out))
    ffn_line.close()
    tok_line.close()
    for keep, give in ending:
        give.wait_recv()
    for keep, give in ending[1:]:
        keep.wait()
    mail.close()
    for copy in ends:
        copy.wait()


def back(given, x1, small, attn, tokens, cotangent, segments, slope_ffn, slope_attn):
    rows, width = tokens.shape
    half = given[2].shape[1]
    share = width // 8
    e_attn, query, kv = attn[0], attn[1], attn[2]
    n_attn, n_query, n_kv = e_attn.shape[1], query.shape[1], kv.shape[1]
    cut = 3 * n_attn // 4
    chunk = rows // 4
    shapes = [
        *[((share, 2 * half), BF16)] * 3,
        ((share, n_attn), BF16),
        ((rows, width), BF16),
        ((rows, width), BF16),
        ((2, width), F32),
        *[((width, half), BF16)] * 3,
    ]
    in_vmem = pl.BlockSpec(memory_space=pltpu.VMEM)
    anywhere = pl.BlockSpec(memory_space=pl.ANY)
    scratch = [
        pltpu.VMEM((2, 2 * share, half), BF16),
        pltpu.VMEM((2, 2, share, half), BF16),
        pltpu.VMEM((3, 2 * share, half), BF16),
        pltpu.VMEM((3, 2, share, half), BF16),
        pltpu.VMEM((3, share, half), BF16),
        pltpu.VMEM((3, share, half), BF16),
        pltpu.VMEM((2, share, half), BF16),
        pltpu.VMEM((rows, width), BF16),
        pltpu.VMEM((rows, width), BF16),
        pltpu.VMEM((rows, width), BF16),
        pltpu.VMEM((chunk, width), BF16),
        pltpu.VMEM((chunk, width), BF16),
        pltpu.VMEM((2, 3, chunk, width), BF16),
        pltpu.VMEM((2, 3, chunk, width), BF16),
        pltpu.VMEM((chunk // BACK_SUBS, width), F32),
        pltpu.VMEM((width, n_attn), BF16),
        pltpu.VMEM((2, 2 * share, n_attn), BF16),
        pltpu.VMEM((2 * share, cut), BF16),
        pltpu.VMEM((2, share, n_attn - cut), BF16),
        pltpu.VMEM((share, cut), BF16),
        pltpu.VMEM((share, n_attn - cut), BF16),
        pltpu.VMEM((rows + EXTRA, n_query), BF16),
        pltpu.VMEM((rows + EXTRA, n_kv), BF16),
        pltpu.VMEM((rows, n_query), BF16),
        pltpu.VMEM((rows, width), BF16),
        pltpu.VMEM((rows + EXTRA, 128), F32),
        pltpu.VMEM((rows, n_query + n_kv), BF16),
        pltpu.VMEM((rows + EXTRA, n_kv), F32),
        pltpu.VMEM((EXTRA, n_query), BF16),
        pltpu.VMEM((EXTRA, n_query), BF16),
        pltpu.VMEM((EXTRA, n_query + n_kv), BF16),
        pltpu.VMEM((EXTRA, n_query + n_kv), BF16),
        pltpu.VMEM((chunk, width), F32),
        pltpu.VMEM((chunk, width), F32),
        pltpu.VMEM((chunk, width), BF16),
        pltpu.VMEM((chunk, width), BF16),
        pltpu.VMEM((2, width), F32),
        pltpu.VMEM((3, 2, width), F32),
        pltpu.VMEM((9, 2, width), F32),
        *line_sems(BACK_SUBS),
        *line_sems(BACK_SUBS),
        pltpu.SemaphoreType.DMA((3, 2)),
        pltpu.SemaphoreType.DMA((36,)),
        pltpu.SemaphoreType.DMA((31,)),
        pltpu.SemaphoreType.DMA((31,)),
    ]
    places = [anywhere] * 9 + [in_vmem] + [anywhere] * 7 + [in_vmem] + [anywhere] * 2
    return pl.pallas_call(
        back_kernel,
        out_shape=[jax.ShapeDtypeStruct(s, d) for s, d in shapes],
        in_specs=places,
        out_specs=[anywhere] * len(shapes),
        scratch_shapes=scratch,
        compiler_params=pltpu.CompilerParams(
            collective_id=1, has_side_effects=True, vmem_limit_bytes=VMEM_BYTES
        ),
        cost_estimate=pl.CostEstimate(
            flops=26 * 10**9, bytes_accessed=120 * 10**6, transcendentals=4 * 10**6
        ),
        name="back",
    )(*given, x1, small, *attn, tokens, cotangent, segments, slope_ffn, slope_attn)


def end_kernel(
    mixed_in,
    tokens_in,
    gate_in,
    up_in,
    attn_in,
    down_in,
    small_in,
    peaks_in,
    gains_in,
    mixed,
    tokens,
    query,
    key,
    value,
    out,
    gate,
    up,
    down,
    attn_out,
    kv_out,
    ffn_out,
    one_out,
    two_out,
    small,
    peaks,
    gain_sum,
    attn_scales,
    kv_scales,
    ffn_scales,
    gain_one,
    gain_two,
    tall_in,
    tall_out,
    wide_in,
    wide_out,
    attn_b,
    attn_f,
    down_b,
    down_f,
    turned,
    in_sem,
    out_sem,
):
    n_query, n_key = query.shape[1], key.shape[1]
    n_in = n_query + 2 * n_key
    step = 32
    reads = [
        (mixed_in, tall_in.at[0]),
        (tokens_in, tall_in.at[1]),
        (down_in, down_b),
        (gate_in, wide_in.at[0]),
        (up_in, wide_in.at[1]),
        (attn_in, attn_b),
        (small_in, small),
        (peaks_in, peaks),
        (gains_in, gain_sum),
    ]
    reads = [pltpu.make_async_copy(a, b, in_sem.at[i]) for i, (a, b) in enumerate(reads)]
    for copy in reads:
        copy.start()
    writes = []

    def write(src, dst):
        copy = pltpu.make_async_copy(src, dst, out_sem.at[len(writes)])
        copy.start()
        writes.append(copy)

    def widen(src, dst):
        @pl.loop(0, src.shape[0] // step)
        def _(index):
            at = pl.ds(mul(index, step), step)
            dst[at, :] = src[at, :].astype(F32)

    for i, target in enumerate((mixed, tokens)):
        reads[i].wait()
        widen(tall_in.at[i], tall_out.at[i])
        write(tall_out.at[i], target)
    for copy in reads[6:]:
        copy.wait()
    piece = small.shape[1]
    for row, first in enumerate((0, n_in)):
        for i in range(n_query // piece):
            at = first // piece + i
            attn_scales[row : row + 1, i * piece : (i + 1) * piece] = small[at : at + 1, :]
    for row in (0, 1):
        for i in range(n_key // piece):
            at = (n_query + row * n_key) // piece + i
            kv_scales[row : row + 1, i * piece : (i + 1) * piece] = small[at : at + 1, :]
    ffn_scales[...] = peaks[0:3, :]
    share, width = gain_one.shape[0], gain_sum.shape[1]
    slot = lax.axis_index("dp") * 2 + lax.axis_index("seq")
    turned[...] = jnp.zeros_like(turned)
    turned[0:2, :] = gain_sum[...]
    turned[...] = pltpu.roll(turned[...], lax.rem(width - slot * share, width), 1)
    gain_one[...] = turned[0, :share]
    gain_two[...] = turned[1, :share]
    for src, dst in (
        (attn_scales, attn_out),
        (kv_scales, kv_out),
        (ffn_scales, ffn_out),
        (gain_one, one_out),
        (gain_two, two_out),
    ):
        write(src, dst)
    reads[2].wait()
    widen(down_b, down_f)
    write(down_f, down)
    for i, target in enumerate((gate, up)):
        reads[3 + i].wait()
        widen(wide_in.at[i], wide_out.at[i])
        write(wide_out.at[i], target)
    reads[5].wait()
    widen(attn_b, attn_f)
    write(attn_f.at[:, pl.ds(0, n_query)], query)
    write(attn_f.at[:, pl.ds(n_query, n_key)], key)
    write(attn_f.at[:, pl.ds(n_query + n_key, n_key)], value)
    write(attn_f.at[:, pl.ds(n_in, n_query)], out)
    for copy in writes:
        copy.wait()


def end(mixed_b, tokens_b, sum_gate, sum_up, sum_attn, sum_down, small, peaks, gain_sum, n_query):
    rows, width = mixed_b.shape
    share, hidden = sum_gate.shape
    n_attn = sum_attn.shape[1]
    n_key = (n_attn - 2 * n_query) // 2
    shapes = [
        (rows, width),
        (rows, width),
        (share, n_query),
        (share, n_key),
        (share, n_key),
        (share, n_query),
        (share, hidden),
        (share, hidden),
        (share, hidden),
        (2, n_query),
        (2, n_key),
        (3, hidden),
        (share,),
        (share,),
    ]
    anywhere = pl.BlockSpec(memory_space=pl.ANY)
    return pl.pallas_call(
        end_kernel,
        out_shape=[jax.ShapeDtypeStruct(s, F32) for s in shapes],
        in_specs=[anywhere] * 9,
        out_specs=[anywhere] * 14,
        scratch_shapes=[
            *(pltpu.VMEM(a.shape, F32) for a in (small, peaks, gain_sum)),
            *(pltpu.VMEM(shape, F32) for shape in shapes[9:]),
            pltpu.VMEM((2, rows, width), BF16),
            pltpu.VMEM((2, rows, width), F32),
            pltpu.VMEM((2, share, hidden), BF16),
            pltpu.VMEM((2, share, hidden), F32),
            pltpu.VMEM((share, n_attn), BF16),
            pltpu.VMEM((share, n_attn), F32),
            pltpu.VMEM((share, hidden), BF16),
            pltpu.VMEM((share, hidden), F32),
            pltpu.VMEM((8, width), F32),
            pltpu.SemaphoreType.DMA((9,)),
            pltpu.SemaphoreType.DMA((14,)),
        ],
        compiler_params=pltpu.CompilerParams(vmem_limit_bytes=VMEM_BYTES),
        cost_estimate=pl.CostEstimate(flops=0, bytes_accessed=29 * 10**6, transcendentals=0),
        name="end",
    )(mixed_b, tokens_b, sum_gate, sum_up, sum_attn, sum_down, small, peaks, gain_sum)


def paired_block(
    tokens,
    gain_attn,
    w_query,
    w_key,
    w_value,
    w_out,
    gain_ffn,
    w_gate,
    w_up,
    w_down,
    width_pick,
    segments,
    cotangent,
):
    n_query = w_query.shape[1]
    weights = (w_query, w_key, w_value, w_out.T, w_down.T, w_gate, w_up)
    (
        e_attn,
        hidden_two,
        resid,
        query_b,
        kv,
        heads_b,
        hidden_one,
        cot_other,
        mixed_in,
        grad_gate_b,
        grad_up_b,
        back_part,
        ffn_part,
        slope_ffn,
        slope_attn,
        small,
        peaks,
        early,
    ) = front(width_pick, weights, gain_attn, gain_ffn, tokens, cotangent, segments)
    sum_down, sum_gate, sum_up, sum_attn, mixed_b, tokens_b, gain_sum, _, _, _ = back(
        (back_part, ffn_part, mixed_in, grad_gate_b, grad_up_b, hidden_two, cot_other, early),
        resid,
        small,
        (e_attn, query_b, kv, heads_b, hidden_one),
        tokens,
        cotangent,
        segments,
        slope_ffn,
        slope_attn,
    )
    mixed, grad_tokens, g_query, g_key, g_value, g_out, g_gate, g_up, g_down, *scales, gain_one, gain_two = end(
        mixed_b, tokens_b, sum_gate, sum_up, sum_attn, sum_down, small, peaks, gain_sum, n_query
    )
    return (
        mixed,
        grad_tokens,
        g_query,
        g_key,
        g_value,
        g_out.T,
        g_gate,
        g_up,
        g_down.T,
        gain_one,
        gain_two,
        *scales,
    )


def solution(mesh):
    in_specs = (
        P(("dp", "seq"), None),
        P(("dp", "seq")),
        P(("dp", "seq"), "mp"),
        P(("dp", "seq"), "mp"),
        P(("dp", "seq"), "mp"),
        P("mp", ("dp", "seq")),
        P(("dp", "seq")),
        P(("dp", "seq"), "mp"),
        P(("dp", "seq"), "mp"),
        P("mp", ("dp", "seq")),
        P(),
        P("dp", None),
        P(("dp", "seq"), None),
    )
    out_specs = (
        P(("dp", "seq"), None),
        P(("dp", "seq"), None),
        P(("dp", "seq"), "mp"),
        P(("dp", "seq"), "mp"),
        P(("dp", "seq"), "mp"),
        P("mp", ("dp", "seq")),
        P(("dp", "seq"), "mp"),
        P(("dp", "seq"), "mp"),
        P("mp", ("dp", "seq")),
        P(("dp", "seq")),
        P(("dp", "seq")),
        P(None, "mp"),
        P(None, "mp"),
        P(None, "mp"),
    )
    shape = dict(mesh.shape)
    paired = shape["dp"] == 4 and shape["seq"] == 2 and shape["mp"] == 4
    block = paired_block if paired else on_device
    return jax.shard_map(
        block, mesh=mesh, in_specs=in_specs, out_specs=out_specs, check_vma=False
    )
```
